32 devices in a mesh: ctx: 8 (over z, core), wsh: 4 (over y, x).
Axes of the slice: x: 2, y: 2, z: 4, core: 2. Of those that a mesh axis runs over, the one named last changes fastest.
Arguments:
- tokens: bfloat16 [16, 2048, 1536], P('wsh', 'ctx'), may hold values from -6 to 6
- cotangent: bfloat16 [16, 2048, 1536], P('wsh', 'ctx'), may hold values from -6 to 6
- group_slot: int32 [12], replicated, may hold values from 0 to 15, as said below
- group_adapter: int32 [12], replicated, may hold values from 0 to 7
- attn_gain: bfloat16 [1536], replicated, may hold values from 0.5 to 1.5
- mlp_gain: bfloat16 [1536], replicated, may hold values from 0.5 to 1.5
- w_query: bfloat16 [1536, 1536], P('wsh', 'ctx'), may hold values from -0.15625 to 0.15625
- w_key: bfloat16 [1536, 256], P('wsh', 'ctx'), may hold values from -0.15625 to 0.15625
- w_value: bfloat16 [1536, 256], P('wsh', 'ctx'), may hold values from -0.15625 to 0.15625
- w_output: bfloat16 [1536, 1536], P('wsh', 'ctx'), may hold values from -1.25 to 1.25
- w_gate: bfloat16 [1536, 8960], P('wsh', 'ctx'), may hold values from -0.15625 to 0.15625
- w_up: bfloat16 [1536, 8960], P('wsh', 'ctx'), may hold values from -0.15625 to 0.15625
- w_down: bfloat16 [8960, 1536], P('wsh', 'ctx'), may hold values from -0.0625 to 0.0625
- query_bias: bfloat16 [1536], replicated, may hold values from -3 to 3
- key_bias: bfloat16 [256], replicated, may hold values from -3 to 3
- value_bias: bfloat16 [256], replicated, may hold values from -3 to 3
- adapt_query_in: bfloat16 [8, 16, 1536], replicated, may hold values from -0.15625 to 0.15625
- adapt_query_out: bfloat16 [8, 16, 1536], replicated, may hold values from -1.5 to 1.5
- adapt_key_in: bfloat16 [8, 16, 1536], replicated, may hold values from -0.15625 to 0.15625
- adapt_key_out: bfloat16 [8, 16, 256], replicated, may hold values from -1.5 to 1.5
- adapt_value_in: bfloat16 [8, 16, 1536], replicated, may hold values from -0.15625 to 0.15625
- adapt_value_out: bfloat16 [8, 16, 256], replicated, may hold values from -1.5 to 1.5
- adapt_output_in: bfloat16 [8, 16, 1536], replicated, may hold values from -1.25 to 1.25
- adapt_output_out: bfloat16 [8, 16, 1536], replicated, may hold values from -1.5 to 1.5
- adapt_gate_in: bfloat16 [8, 16, 1536], replicated, may hold values from -0.15625 to 0.15625
- adapt_gate_out: bfloat16 [8, 16, 8960], replicated, may hold values from -1.5 to 1.5
- adapt_up_in: bfloat16 [8, 16, 1536], replicated, may hold values from -0.15625 to 0.15625
- adapt_up_out: bfloat16 [8, 16, 8960], replicated, may hold values from -1.5 to 1.5
- adapt_down_in: bfloat16 [8, 16, 8960], replicated, may hold values from -0.0625 to 0.0625
- adapt_down_out: bfloat16 [8, 16, 1536], replicated, may hold values from -1.5 to 1.5
Outputs:
- layer_out: bfloat16 [16, 2048, 1536], P('wsh', 'ctx')
- input_grad: bfloat16 [16, 2048, 1536], P('wsh', 'ctx')
- grad_query_in: float32 [8, 16, 1536], replicated
- grad_query_out: float32 [8, 16, 1536], replicated
- grad_key_in: float32 [8, 16, 1536], replicated
- grad_key_out: float32 [8, 16, 256], replicated
- grad_value_in: float32 [8, 16, 1536], replicated
- grad_value_out: float32 [8, 16, 256], replicated
- grad_output_in: float32 [8, 16, 1536], replicated
- grad_output_out: float32 [8, 16, 1536], replicated
- grad_gate_in: float32 [8, 16, 1536], replicated
- grad_gate_out: float32 [8, 16, 8960], replicated
- grad_up_in: float32 [8, 16, 1536], replicated
- grad_up_out: float32 [8, 16, 8960], replicated
- grad_down_in: float32 [8, 16, 8960], replicated
- grad_down_out: float32 [8, 16, 1536], replicated
The draws below stay inside these ranges and needn't reach their ends.
Inputs may be any that keep to these rules, and one draw needn't show every extreme that they name: 12 distinct slot numbers; group g fills slot group_slot[g], which weight shard group_slot[g] // 4 holds; slots that no group names are empty.
All inputs are finite; a program needn't handle non-finite values.
Results may differ from the reference program's by a relative error of at most 0.023.
Values may be sent and summed in bfloat16 or wider, within the bound.
No kernel may reach another device: no remote copies, remote signals or barrier semaphores. Data moves between devices by JAX's collectives and lax.ppermute only.
A program may use at most 512 MiB of HBM per device.

```python
import math
import jax
import jax.numpy as jnp
from jax import lax

D = 1536
HEADS = 12
HEAD_DIM = 128
FF = 8960
RANK = 16
ADAPTERS = 8
PROMPT = 1024
CONTS = 4
CONT = 256
KVD = 256
GROUP_LEN = 2048
SLOT_TOTAL = 16
GROUPS = 12


def draw_group_slot(key, part):
    key = jax.random.fold_in(key, 11)
    order = jax.random.permutation(key, SLOT_TOTAL)
    return order[:GROUPS].astype(jnp.int32)


def with_ends(values, stream_key, smallest, high):
    spot = [jax.random.randint(jax.random.fold_in(stream_key, axis), (), 0, length) for axis, length in enumerate(values.shape)]
    main_axis = values.shape.index(max(values.shape))
    neighbour = spot[:main_axis] + [(spot[main_axis] + 1) % values.shape[main_axis]] + spot[main_axis + 1:]
    return values.at[tuple(spot)].set(smallest).at[tuple(neighbour)].set(high)


def level_of(own_key, shape, cuts, least, largest):
    gain, own = 1.0, jax.random.fold_in(own_key, 6)
    for dim, shards_of in cuts:
        draws = jnp.exp(jax.random.uniform(jax.random.fold_in(own, dim), (shards_of,), jnp.float32, least / len(cuts), largest / len(cuts)))
        gain = gain * jnp.repeat(draws, shape[dim] // shards_of).reshape([-1 if axis == dim else 1 for axis in range(len(shape))])
    return gain


def bell_draw(stream_key, shape, width, limit, cuts=(), kind=jnp.bfloat16):
    result = width * jax.random.normal(stream_key, shape, jnp.float32)
    if cuts:
        result = result * level_of(stream_key, shape, cuts, -0.22, 0.18)
    return jnp.clip(result, -limit, limit).astype(kind)


def setup_inputs(seed: int = 0) -> dict:
    seeds = jax.random.split(jax.random.key(seed), 31)
    return {
        "tokens": bell_draw(seeds[0], (SLOT_TOTAL, GROUP_LEN, D), 1.0, 6.0, ((0, 4), (1, 8))),
        "cotangent": bell_draw(seeds[1], (SLOT_TOTAL, GROUP_LEN, D), 1.0, 6.0, ((0, 4), (1, 8))),
        "group_slot": draw_group_slot(jax.random.fold_in(seeds[30], 71), 0),
        "group_adapter": with_ends(jax.random.randint(seeds[3], (GROUPS,), 0, ADAPTERS), jax.random.fold_in(seeds[3], 1), 0, ADAPTERS - 1).astype(jnp.int32),
        "attn_gain": jnp.clip(1.0 + 0.1 * jax.random.normal(seeds[4], (D,), jnp.float32), 0.5, 1.5).astype(jnp.bfloat16),
        "mlp_gain": jnp.clip(1.0 + 0.1 * jax.random.normal(seeds[5], (D,), jnp.float32), 0.5, 1.5).astype(jnp.bfloat16),
        "w_query": bell_draw(seeds[6], (D, D), D ** -0.5, 0.15625, ((0, 4), (1, 8))),
        "w_key": bell_draw(seeds[7], (D, KVD), D ** -0.5, 0.15625, ((0, 4), (1, 8))),
        "w_value": bell_draw(seeds[8], (D, KVD), D ** -0.5, 0.15625, ((0, 4), (1, 8))),
        "w_output": bell_draw(seeds[9], (D, D), (D // 64) ** -0.5, 1.25, ((0, 4), (1, 8))),
        "w_gate": bell_draw(seeds[10], (D, FF), D ** -0.5, 0.15625, ((0, 4), (1, 8))),
        "w_up": bell_draw(seeds[11], (D, FF), D ** -0.5, 0.15625, ((0, 4), (1, 8))),
        "w_down": bell_draw(seeds[12], (FF, D), FF ** -0.5, 0.0625, ((0, 4), (1, 8))),
        "query_bias": bell_draw(seeds[13], (D,), 0.5, 3.0),
        "key_bias": bell_draw(seeds[14], (KVD,), 0.5, 3.0),
        "value_bias": bell_draw(seeds[15], (KVD,), 0.5, 3.0),
        "adapt_query_in": bell_draw(seeds[16], (ADAPTERS, RANK, D), D ** -0.5, 0.15625),
        "adapt_query_out": bell_draw(seeds[17], (ADAPTERS, RANK, D), RANK ** -0.5, 1.5),
        "adapt_key_in": bell_draw(seeds[18], (ADAPTERS, RANK, D), D ** -0.5, 0.15625),
        "adapt_key_out": bell_draw(seeds[19], (ADAPTERS, RANK, KVD), RANK ** -0.5, 1.5),
        "adapt_value_in": bell_draw(seeds[20], (ADAPTERS, RANK, D), D ** -0.5, 0.15625),
        "adapt_value_out": bell_draw(seeds[21], (ADAPTERS, RANK, KVD), RANK ** -0.5, 1.5),
        "adapt_output_in": bell_draw(seeds[22], (ADAPTERS, RANK, D), (D // 64) ** -0.5, 1.25),
        "adapt_output_out": bell_draw(seeds[23], (ADAPTERS, RANK, D), RANK ** -0.5, 1.5),
        "adapt_gate_in": bell_draw(seeds[24], (ADAPTERS, RANK, D), D ** -0.5, 0.15625),
        "adapt_gate_out": bell_draw(seeds[25], (ADAPTERS, RANK, FF), RANK ** -0.5, 1.5),
        "adapt_up_in": bell_draw(seeds[26], (ADAPTERS, RANK, D), D ** -0.5, 0.15625),
        "adapt_up_out": bell_draw(seeds[27], (ADAPTERS, RANK, FF), RANK ** -0.5, 1.5),
        "adapt_down_in": bell_draw(seeds[28], (ADAPTERS, RANK, FF), FF ** -0.5, 0.0625),
        "adapt_down_out": bell_draw(seeds[29], (ADAPTERS, RANK, D), RANK ** -0.5, 1.5),
    }


@jax.custom_vjp
def low(v):
    return lax.optimization_barrier(v.astype(jnp.bfloat16)).astype(jnp.float32)

@jax.custom_vjp
def low_back(v):
    return v

def low_keep(v):
    return (low(v), None)

def low_pass(kept, grad):
    return (grad,)

def back_keep(v):
    return (v, None)

def back_low(kept, grad):
    return (low(grad),)
low.defvjp(low_keep, low_pass)
low_back.defvjp(back_keep, back_low)
norm_eps = 1e-06
adapter_scale = 0.5
rope_base = 1000000.0
masked_score = -1e+30

def matmul(left, right):
    return jnp.dot(left, right, precision=lax.Precision.HIGHEST, preferred_element_type=jnp.float32)

def rms_scale(hidden, gain_vec):
    return hidden * lax.rsqrt(lax.optimization_barrier(jnp.mean(hidden * hidden, axis=-1, keepdims=True)) + norm_eps) * gain_vec

def token_layout(token_index):
    cont_tokens = CONTS * CONT
    in_prompt = token_index >= cont_tokens
    segment = jnp.where(in_prompt, 0, 1 + token_index // CONT).astype(jnp.int32)
    position = jnp.where(in_prompt, token_index - cont_tokens, PROMPT + token_index % CONT).astype(jnp.int32)
    return (segment, position)

def rotate(values, position):
    half_dim = values.shape[-1] // 2
    frequency = rope_base ** (-(jnp.arange(half_dim, dtype=jnp.float32) * 2.0) / values.shape[-1])
    angles = position.astype(jnp.float32)[:, None] * frequency[None, :]
    cosine_table = jnp.concatenate([jnp.cos(angles), jnp.cos(angles)], axis=-1)
    sine_table = jnp.concatenate([jnp.sin(angles), jnp.sin(angles)], axis=-1)
    turned = jnp.concatenate([-values[..., half_dim:], values[..., :half_dim]], axis=-1)
    layout = (position.shape[0],) + (1,) * (values.ndim - 2) + (values.shape[-1],)
    return values * cosine_table.reshape(layout) + turned * sine_table.reshape(layout)

def attention(queries, keys, values, segment):
    count = queries.shape[0]
    block_rows = math.gcd(count, 512)
    score_scale = HEAD_DIM ** (-0.5)
    key_index = jnp.arange(count, dtype=jnp.int32)
    blocks = queries.reshape((count // block_rows, block_rows) + queries.shape[1:])
    starts = jnp.arange(count // block_rows, dtype=jnp.int32) * block_rows

    def one_block(element):
        block_q, start = element
        query_index = start + jnp.arange(block_rows, dtype=jnp.int32)
        query_segment = lax.dynamic_slice_in_dim(segment, start, block_rows)
        same_part = (key_index[None, :] <= query_index[:, None]) & (segment[None, :] == query_segment[:, None])
        allowed = same_part | (segment[None, :] == 0) & (query_segment[:, None] != 0)
        scores = low_back(jnp.einsum('bkgd,tkd->kgbt', block_q, keys, precision=lax.Precision.HIGHEST) * score_scale)
        scores = jnp.where(allowed, scores, masked_score)
        shifted = jnp.exp(scores - lax.optimization_barrier(jnp.max(scores, axis=-1, keepdims=True)))
        probs = shifted / lax.optimization_barrier(jnp.sum(shifted, axis=-1, keepdims=True))
        return jnp.einsum('kgbt,tkd->bkgd', low(probs), values, precision=lax.Precision.HIGHEST)
    mixed = lax.map(jax.checkpoint(one_block), (blocks, starts))
    return mixed.reshape(count, -1)

def slot_forward(hidden, pick, fixed, adapters):
    w_query, w_key, w_value, w_output, w_gate, w_up, w_down, query_bias, key_bias, value_bias, attn_gain, mlp_gain = fixed

    def adapt(input_rows, number):
        selected_down_weight = jnp.tensordot(pick, adapters[2 * number], axes=1, precision=lax.Precision.HIGHEST)
        selected_up_weight = jnp.tensordot(pick, adapters[2 * number + 1], axes=1, precision=lax.Precision.HIGHEST)
        projected_rank_rows = low(low_back(matmul(input_rows, selected_down_weight.T)))
        return adapter_scale * matmul(projected_rank_rows, selected_up_weight)
    count = hidden.shape[0]
    kv_heads = w_key.shape[1] // HEAD_DIM
    group_size = HEADS // kv_heads
    segment, position = token_layout(jnp.arange(count, dtype=jnp.int32))
    normed = low(rms_scale(hidden, attn_gain))
    query_lin = matmul(normed, w_query) + query_bias + adapt(normed, 0)
    key_lin = matmul(normed, w_key) + key_bias + adapt(normed, 1)
    value_lin = matmul(normed, w_value) + value_bias + adapt(normed, 2)
    queries = low(rotate(low_back(query_lin).reshape(count, kv_heads, group_size, HEAD_DIM), position))
    keys = low(rotate(low_back(key_lin).reshape(count, kv_heads, HEAD_DIM), position))
    values = low(low_back(value_lin)).reshape(count, kv_heads, HEAD_DIM)
    context = low(low_back(attention(queries, keys, values, segment)))
    branch = low_back(matmul(context, w_output) + adapt(context, 3))
    middle = hidden + branch
    normed2 = low(rms_scale(middle, mlp_gain))
    gate_lin = low_back(matmul(normed2, w_gate) + adapt(normed2, 4))
    up_lin = low_back(matmul(normed2, w_up) + adapt(normed2, 5))
    act_rows = low(gate_lin * jax.nn.sigmoid(gate_lin) * up_lin)
    return middle + matmul(act_rows, w_down) + adapt(act_rows, 6)

def reference(tokens, cotangent, group_slot, group_adapter, attn_gain, mlp_gain, w_query, w_key, w_value, w_output, w_gate, w_up, w_down, query_bias, key_bias, value_bias, adapt_query_in, adapt_query_out, adapt_key_in, adapt_key_out, adapt_value_in, adapt_value_out, adapt_output_in, adapt_output_out, adapt_gate_in, adapt_gate_out, adapt_up_in, adapt_up_out, adapt_down_in, adapt_down_out):
    slot_ids = jnp.arange(SLOT_TOTAL, dtype=jnp.int32)
    matches = group_slot[None, :] == slot_ids[:, None]
    live_slot = jnp.any(matches, axis=1).astype(jnp.float32)
    named = (group_adapter[:, None] == jnp.arange(ADAPTERS, dtype=jnp.int32)[None, :]).astype(jnp.float32)
    choose = matmul(matches.astype(jnp.float32), named)
    fixed = tuple((w.astype(jnp.float32) for w in (w_query, w_key, w_value, w_output, w_gate, w_up, w_down, query_bias, key_bias, value_bias, attn_gain, mlp_gain)))
    adapters = tuple((w.astype(jnp.float32) for w in (adapt_query_in, adapt_query_out, adapt_key_in, adapt_key_out, adapt_value_in, adapt_value_out, adapt_output_in, adapt_output_out, adapt_gate_in, adapt_gate_out, adapt_up_in, adapt_up_out, adapt_down_in, adapt_down_out)))

    def forward(input_rows, adapter_set):

        def one_slot(element):
            return jax.checkpoint(slot_forward)(element[0], element[1], fixed, adapter_set)
        return lax.map(one_slot, (input_rows, choose))
    outputs, pullback = jax.vjp(forward, tokens.astype(jnp.float32), adapters)
    live_rows = live_slot[:, None, None]
    grad_input, grad_set = pullback(cotangent.astype(jnp.float32) * live_rows)
    g_query_in, g_query_out, g_key_in, g_key_out, g_value_in, g_value_out, g_output_in, g_output_out, g_gate_in, g_gate_out, g_up_in, g_up_out, g_down_in, g_down_out = grad_set
    return ((outputs * live_rows).astype(jnp.bfloat16), (grad_input * live_rows).astype(jnp.bfloat16), g_query_in, g_query_out, g_key_in, g_key_out, g_value_in, g_value_out, g_output_in, g_output_out, g_gate_in, g_gate_out, g_up_in, g_up_out, g_down_in, g_down_out)
```

```python
import functools
import math

import jax
import jax.numpy as jnp
from jax import lax
from jax.experimental import pallas as pl
from jax.experimental.pallas import tpu as pltpu
from jax.sharding import PartitionSpec as P

HEAD_DIM = 128
PROMPT = 1024
CONTS = 4
CONT = 256
RANK = 16

norm_eps = 1e-06
adapter_scale = 0.5
rope_base = 1000000.0
masked_score = -1e30
score_scale = HEAD_DIM ** (-0.5)
score_to_log2 = score_scale * math.log2(math.e)

f32 = jnp.float32
bf16 = jnp.bfloat16
VMEM_LIMIT = 60 * 2**20
PIECE = 256


def nt(left, right):
    return lax.dot_general(left, right, (((1,), (1,)), ((), ())), preferred_element_type=f32)


def nn(left, right):
    return lax.dot_general(left, right, (((1,), (0,)), ((), ())), preferred_element_type=f32)


def tn(left, right):
    return lax.dot_general(left, right, (((0,), (0,)), ((), ())), preferred_element_type=f32)


def along_line(array, pairs):
    return lax.ppermute(array, "ctx", [(2 * a + c, 2 * b + c) for a, b in pairs for c in (0, 1)])


def swap_cores(array):
    size = lax.axis_size("ctx")
    return lax.ppermute(array, "ctx", [(i, i ^ 1) for i in range(size)])


def hold_kernel(*refs):
    pass


def hold(arrays, *after):
    anywhere = pl.BlockSpec(memory_space=pl.ANY)
    count = len(arrays)
    return pl.pallas_call(
        hold_kernel,
        in_specs=[anywhere] * (count + len(after)),
        out_specs=[anywhere] * count,
        out_shape=[jax.ShapeDtypeStruct(a.shape, a.dtype) for a in arrays],
        input_output_aliases={i: i for i in range(count)},
        name="hold",
    )(*arrays, *after)


def line_gather(piece, place, line, after=()):
    came = [
        along_line(piece, [(i, (i + by) % line) for i in range(line)]) for by in range(1, line)
    ]
    if after:
        came = hold(came, *after)
    out = jnp.zeros((line,) + piece.shape, piece.dtype)
    out = lax.dynamic_update_index_in_dim(out, piece, place, 0)
    for by in range(1, line):
        out = lax.dynamic_update_index_in_dim(out, came[by - 1], (place - by) % line, 0)
    return out


def shard_gather(lined):
    return lax.all_gather(lined, "wsh", axis=0, tiled=False)


def add_up(arrays):
    return functools.reduce(jnp.add, [a.astype(f32) for a in arrays]).astype(bf16)


def reduce_ctx(parts, place, core, line):
    pairs = parts.reshape((line, 2) + parts.shape[1:])
    keep = lax.dynamic_index_in_dim(pairs, core, 1, False)
    give = lax.dynamic_index_in_dim(pairs, 1 - core, 1, False)
    mine = add_up([keep, swap_cores(give)])
    terms = [lax.dynamic_index_in_dim(mine, place, 0, False)]
    for by in range(1, line):
        out = lax.dynamic_index_in_dim(mine, (place + by) % line, 0, False)
        terms.append(along_line(out, [(i, (i + by) % line) for i in range(line)]))
    return add_up(terms)


def across(array, by):
    size = lax.axis_size("wsh")
    return lax.ppermute(array, "wsh", [(i, i ^ by) for i in range(size)])


def reduce_wsh(parts, shard):
    terms = [lax.dynamic_index_in_dim(parts, shard, 0, False)]
    for by in range(1, parts.shape[0]):
        terms.append(across(lax.dynamic_index_in_dim(parts, shard ^ by, 0, False), by))
    return add_up(terms)


def gather_all(piece, place, core, shard, line):
    own = line_gather(piece, place, line)
    shards = lax.axis_size("wsh")
    all_own = jnp.zeros((shards,) + own.shape, own.dtype)
    all_own = lax.dynamic_update_index_in_dim(all_own, own, shard, 0)
    for by in range(1, shards):
        all_own = lax.dynamic_update_index_in_dim(all_own, across(own, by), shard ^ by, 0)
    other = swap_cores(all_own)
    pair = jnp.stack([jnp.where(core == 0, all_own, other), jnp.where(core == 0, other, all_own)])
    return jnp.moveaxis(pair, 2, 0)


def params(**more):
    return pltpu.CompilerParams(
        dimension_semantics=("arbitrary",), vmem_limit_bytes=VMEM_LIMIT, **more
    )


def whole(array):
    return pl.BlockSpec(array.shape, lambda s, *pre: (0,) * array.ndim)


def by_slot(array):
    return pl.BlockSpec((1,) + array.shape[1:], lambda s, *pre: (s,) + (0,) * (array.ndim - 1))


def second_by_slot(array):
    return pl.BlockSpec(
        (array.shape[0], 1) + array.shape[2:], lambda s, *pre: (0, s) + (0,) * (array.ndim - 2)
    )


def cost(flops, bytes_accessed, exps=0):
    return pl.CostEstimate(flops=int(flops), bytes_accessed=int(bytes_accessed), transcendentals=int(exps))


def slot_lanes(adapter, block, ranks):
    lane = lax.broadcasted_iota(jnp.int32, (block, ranks), 1)
    return lane // RANK == adapter[pl.program_id(0)]


def picked(mask, values):
    return jnp.where(mask, values, 0.0).astype(bf16)


def struct(shape, dtype):
    return jax.ShapeDtypeStruct(shape, dtype)


def turn(u, cos, sin):
    return u * cos + pltpu.roll(u, HEAD_DIM // 2, 1) * sin


def turn_back(u, cos, sin):
    return u * cos - pltpu.roll(u, HEAD_DIM // 2, 1) * sin


def key_value_kernel(
    adapter, tok, gain, weight, bias, in_k, in_v, out_k, out_v, cosine, sine,
    normed_ref, rank_k_ref, rank_v_ref, kv_ref,
):
    hidden = tok[0].astype(f32)
    inverse = lax.rsqrt(jnp.mean(hidden * hidden, axis=-1, keepdims=True) + norm_eps)
    normed = (hidden * inverse * gain[...]).astype(bf16)
    normed_ref[0] = normed
    mask = slot_lanes(adapter, normed.shape[0], in_k.shape[0])
    kv_width = kv_ref.shape[-1] // 2
    lin = nt(normed, weight[...]) + bias[...]
    rank_k = picked(mask, nt(normed, in_k[...]))
    rank_v = picked(mask, nt(normed, in_v[...]))
    rank_k_ref[0], rank_v_ref[0] = rank_k, rank_v
    key = lin[:, :kv_width] + adapter_scale * nn(rank_k, out_k[...])
    value = lin[:, kv_width:] + adapter_scale * nn(rank_v, out_v[...])
    cos, sin = cosine[...], sine[...]
    for h in range(kv_width // HEAD_DIM):
        part = slice(h * HEAD_DIM, (h + 1) * HEAD_DIM)
        kv_ref[0, :, part] = turn(key[:, part], cos, sin).astype(bf16)
    kv_ref[0, :, kv_width:] = value.astype(bf16)


def key_value_side(adapter_of, tokens, gain, weight, bias, adapters, cosine, sine):
    slots, block, width = tokens.shape
    shared = (gain, weight, bias, *adapters, cosine, sine)
    ranks = struct((slots, block, adapters[0].shape[0]), bf16)
    outs = (struct(tokens.shape, bf16), ranks, ranks, struct((slots, block, weight.shape[0]), bf16))
    return pl.pallas_call(
        key_value_kernel,
        grid_spec=pltpu.PrefetchScalarGridSpec(
            num_scalar_prefetch=1,
            grid=(slots,),
            in_specs=[by_slot(tokens)] + [whole(a) for a in shared],
            out_specs=[by_slot(o) for o in outs],
        ),
        out_shape=outs,
        compiler_params=params(),
        cost_estimate=cost(3 * slots * block * width * weight.shape[0], 12e6),
        name="key_value_side",
    )(adapter_of, tokens, *shared)


def query_kernel(adapter, normed, weight, bias, in_q, out_q, cosine, sine, rank_ref, query_ref):
    x = normed[0]
    mask = slot_lanes(adapter, x.shape[0], in_q.shape[0])
    rank = picked(mask, nt(x, in_q[...]))
    rank_ref[0] = rank
    query = nt(x, weight[...]) + bias[...] + adapter_scale * nn(rank, out_q[...])
    cos, sin = cosine[...], sine[...]
    for h in range(query.shape[1] // HEAD_DIM):
        part = slice(h * HEAD_DIM, (h + 1) * HEAD_DIM)
        query_ref[0, :, part] = turn(query[:, part], cos, sin).astype(bf16)


def query_side(adapter_of, normed, weight, bias, adapters, cosine, sine):
    slots, block, width = normed.shape
    shared = (weight, bias, *adapters, cosine, sine)
    outs = (struct((slots, block, adapters[0].shape[0]), bf16), struct(normed.shape, bf16))
    return pl.pallas_call(
        query_kernel,
        grid_spec=pltpu.PrefetchScalarGridSpec(
            num_scalar_prefetch=1,
            grid=(slots,),
            in_specs=[by_slot(normed)] + [whole(a) for a in shared],
            out_specs=[by_slot(o) for o in outs],
        ),
        out_shape=outs,
        compiler_params=params(),
        cost_estimate=cost(2.5 * slots * block * width * width, 12e6),
        name="query_side",
    )(adapter_of, normed, *shared)


def attend_kernel(kv_heads, group, mates, flags, *refs):
    query, own, even, odd = refs[:4]
    mate = refs[4] if mates else None
    context_ref, mixed_ref, log_ref = refs[4 + mates :]
    block = query.shape[1]
    half = even.shape[0]
    kv_width = kv_heads * HEAD_DIM
    rows = lax.broadcasted_iota(jnp.int32, (block, block), 0)
    cols = lax.broadcasted_iota(jnp.int32, (block, block), 1)
    causal = rows <= cols
    bias = [jnp.where(flags[i] != 0, 0.0, masked_score) for i in range(2 * half + mates)]
    for kv in range(kv_heads):
        k_part = slice(kv * HEAD_DIM, (kv + 1) * HEAD_DIM)
        v_part = slice(kv_width + kv * HEAD_DIM, kv_width + (kv + 1) * HEAD_DIM)
        sources = [own[0]] + [even[i, 0] for i in range(half)] + [odd[i, 0] for i in range(half)]
        sources += [mate[0]] if mates else []
        keys = [s[:, k_part] for s in sources]
        values_t = [s[:, v_part].T for s in sources]
        for g in range(group):
            h = kv * group + g
            part = slice(h * HEAD_DIM, (h + 1) * HEAD_DIM)
            q = query[0, :, part]
            scores = [nt(k, q) for k in keys]
            scores[0] = jnp.where(causal, scores[0], masked_score)
            scores = scores[:1] + [s + b for s, b in zip(scores[1:], bias)]
            top = functools.reduce(jnp.maximum, [jnp.max(s, axis=0, keepdims=True) for s in scores])
            shift = top * score_to_log2
            total, mixed = 0.0, 0.0
            for s, v in zip(scores, values_t):
                p = jnp.exp2(s * score_to_log2 - shift)
                total = total + jnp.sum(p, axis=0, keepdims=True)
                mixed = mixed + nn(v, p.astype(bf16))
            mixed = mixed / total
            mixed_ref[0, h] = mixed
            log_ref[0, h : h + 1, :] = shift + jnp.log2(total)
            context_ref[0, :, part] = mixed.T.astype(bf16)


def attend(flags, query, own, even, odd, mate, kv_heads):
    slots, block, width = query.shape
    heads = width // HEAD_DIM
    mates = len(mate)
    operands = (query, own, even, odd, *mate)
    specs = [by_slot(query), by_slot(own), second_by_slot(even), second_by_slot(odd)]
    specs += [by_slot(m) for m in mate]
    outs = (
        struct((slots, block, width), bf16),
        struct((slots, heads, HEAD_DIM, block), f32),
        struct((slots, heads, block), f32),
    )
    return pl.pallas_call(
        functools.partial(attend_kernel, kv_heads, heads // kv_heads, mates),
        grid_spec=pltpu.PrefetchScalarGridSpec(
            num_scalar_prefetch=1, grid=(slots,), in_specs=specs, out_specs=[by_slot(o) for o in outs]
        ),
        out_shape=outs,
        compiler_params=params(),
        cost_estimate=cost(20e9, 20e6, slots * heads * block * (own.shape[1] * 5)),
        name="attend",
    )(flags, *operands)


def attend_back_kernel(kv_heads, group, mates, flags, *refs):
    query, own, even, odd = refs[:4]
    mate = refs[4] if mates else None
    grad, mixed_ref, log_ref, cosine, sine = refs[4 + mates : 9 + mates]
    d_query, d_own, d_even, d_odd = refs[9 + mates : 13 + mates]
    d_mate = refs[13 + mates] if mates else None
    acc = refs[13 + 2 * mates]
    block = query.shape[1]
    half = even.shape[0]
    kv_width = kv_heads * HEAD_DIM
    rows = lax.broadcasted_iota(jnp.int32, (block, block), 0)
    cols = lax.broadcasted_iota(jnp.int32, (block, block), 1)
    causal = rows <= cols
    bias = [jnp.where(flags[i] != 0, 0.0, masked_score) for i in range(2 * half + mates)]
    cos, sin = cosine[...], sine[...]
    for kv in range(kv_heads):
        k_part = slice(kv * HEAD_DIM, (kv + 1) * HEAD_DIM)
        v_part = slice(kv_width + kv * HEAD_DIM, kv_width + (kv + 1) * HEAD_DIM)
        sources = [own[0]] + [even[i, 0] for i in range(half)] + [odd[i, 0] for i in range(half)]
        sources += [mate[0]] if mates else []
        keys = [s[:, k_part] for s in sources]
        keys_t = [k.T for k in keys]
        values = [s[:, v_part] for s in sources]
        for g in range(group):
            h = kv * group + g
            part = slice(h * HEAD_DIM, (h + 1) * HEAD_DIM)
            q = query[0, :, part]
            d_o = grad[0, :, part]
            delta = jnp.sum(d_o.astype(f32).T * mixed_ref[0, h], axis=0, keepdims=True)
            shift = log_ref[0, h : h + 1, :]
            d_q = 0.0
            for i in range(len(sources)):
                s = nt(keys[i], q)
                s = jnp.where(causal, s, masked_score) if i == 0 else s + bias[i - 1]
                p = jnp.exp2(s * score_to_log2 - shift)
                d_p = nt(values[i], d_o)
                d_s = (p * (d_p - delta)).astype(bf16)
                d_value = nn(p.astype(bf16), d_o)
                d_key = nn(d_s, q)
                if g == 0:
                    acc[i, :, v_part] = d_value
                    acc[i, :, k_part] = d_key
                else:
                    acc[i, :, v_part] += d_value
                    acc[i, :, k_part] += d_key
                d_q = d_q + nn(keys_t[i], d_s)
            u = d_q.T * score_scale
            d_query[0, :, part] = (u * cos - pltpu.roll(u, HEAD_DIM // 2, 1) * sin).astype(bf16)
    targets = [(d_own, 0)] + [(d_even, i) for i in range(half)] + [(d_odd, i) for i in range(half)]
    targets += [(d_mate, 0)] if mates else []
    for i, (target, j) in enumerate(targets):
        if target is d_own or target is d_mate:
            target[0, :, :kv_width] = (acc[i, :, :kv_width] * score_scale).astype(target.dtype)
            target[0, :, kv_width:] = acc[i, :, kv_width:].astype(target.dtype)
        else:
            target[j, 0, :, :kv_width] = (acc[i, :, :kv_width] * score_scale).astype(target.dtype)
            target[j, 0, :, kv_width:] = acc[i, :, kv_width:].astype(target.dtype)


def attend_back(flags, query, own, even, odd, mate, grad, mixed, logs, cosine, sine, kv_heads):
    slots, block, width = query.shape
    heads = width // HEAD_DIM
    mates = len(mate)
    operands = (query, own, even, odd, *mate, grad, mixed, logs, cosine, sine)
    specs = [by_slot(query), by_slot(own), second_by_slot(even), second_by_slot(odd)]
    specs += [by_slot(m) for m in mate]
    specs += [by_slot(grad), by_slot(mixed), by_slot(logs), whole(cosine), whole(sine)]
    outs = (
        struct(query.shape, bf16),
        struct(own.shape, f32),
        struct(even.shape, bf16),
        struct(odd.shape, bf16),
        *(struct(m.shape, bf16) for m in mate),
    )
    out_specs = [by_slot(outs[0]), by_slot(outs[1]), second_by_slot(even), second_by_slot(odd)]
    out_specs += [by_slot(m) for m in mate]
    count = 1 + 2 * even.shape[0] + mates
    return pl.pallas_call(
        functools.partial(attend_back_kernel, kv_heads, heads // kv_heads, mates),
        grid_spec=pltpu.PrefetchScalarGridSpec(
            num_scalar_prefetch=1,
            grid=(slots,),
            in_specs=specs,
            out_specs=out_specs,
            scratch_shapes=[pltpu.VMEM((count,) + own.shape[1:], f32)],
        ),
        out_shape=outs,
        compiler_params=params(),
        cost_estimate=cost(50e9, 40e6, slots * heads * block * (own.shape[1] * 5)),
        name="attend_back",
    )(flags, *operands)


def middle_kernel(
    adapter, live, context, tok, cot, weight, in_o, out_o, gain, in_g, in_u, out_d,
    mid_ref, normed_ref, grad_ref, rank_o_ref, rank_g_ref, rank_u_ref, grad_rank_ref,
):
    s = pl.program_id(0)
    ctx = context[0]
    mask = slot_lanes(adapter, ctx.shape[0], in_o.shape[0])
    rank = picked(mask, nt(ctx, in_o[...]))
    rank_o_ref[0] = rank
    mid = tok[0].astype(f32) + nt(ctx, weight[...]) + adapter_scale * nn(rank, out_o[...])
    mid_ref[0] = mid
    inverse = lax.rsqrt(jnp.mean(mid * mid, axis=-1, keepdims=True) + norm_eps)
    normed = (mid * inverse * gain[...]).astype(bf16)
    normed_ref[0] = normed
    rank_g_ref[0] = picked(mask, nt(normed, in_g[...]))
    rank_u_ref[0] = picked(mask, nt(normed, in_u[...]))
    on = jnp.where(live[s] != 0, 1.0, 0.0)
    grad = (cot[0].astype(f32) * on).astype(bf16)
    grad_ref[0] = grad
    grad_rank_ref[0] = picked(mask, adapter_scale * nt(grad, out_d[...]))


def middle_side(adapter_of, live, context, tokens, cotangent, weight, in_o, out_o, gain, in_g, in_u, out_d):
    slots, block, width = tokens.shape
    shared = (weight, in_o, out_o, gain, in_g, in_u, out_d)
    rank = struct((slots, block, in_o.shape[0]), bf16)
    wide = struct(tokens.shape, bf16)
    outs = (struct(tokens.shape, f32), wide, wide, rank, rank, rank, rank)
    return pl.pallas_call(
        middle_kernel,
        grid_spec=pltpu.PrefetchScalarGridSpec(
            num_scalar_prefetch=2,
            grid=(slots,),
            in_specs=[by_slot(a) for a in (context, tokens, cotangent)] + [whole(a) for a in shared],
            out_specs=[by_slot(o) for o in outs],
        ),
        out_shape=outs,
        compiler_params=params(),
        cost_estimate=cost(3 * slots * block * width * width, 28e6),
        name="middle_side",
    )(adapter_of, live, context, tokens, cotangent, *shared)


def weight_copies(core, own, other, gate, up, down, sems):
    copies = []

    def add(source, target):
        copies.append(pltpu.make_async_copy(source, target, sems.at[len(copies)]))

    shards, line, rows, cols = own.shape
    rows //= 3
    for side, half in ((core, own), (1 - core, other)):
        for w in range(shards):
            span = pl.ds(w * cols, cols)
            add(half.at[w, :, pl.ds(0, rows), :], gate.at[side, :, :, span])
            add(half.at[w, :, pl.ds(rows, rows), :], up.at[side, :, :, span])
            for z in range(line):
                add(
                    half.at[w, z, pl.ds(2 * rows, rows), :],
                    down.at[side, w, :, pl.ds(z * cols, cols)],
                )
    return copies


def wide_copies(core, own, other, gate, up, down, sems):
    copies = []
    for side, half in ((core, own), (1 - core, other)):
        for i, target in enumerate((gate, up, down)):
            copies.append(pltpu.make_async_copy(half.at[i], target.at[side], sems.at[len(copies)]))
    return copies


def feed_kernel(first, plan, span, core, own, other, normed, grad, rank_d, rank_g, rank_u,
                in_d, out_g, out_u, *refs):
    if first:
        sums_in = None
    else:
        sums_in, refs = refs[:5], refs[5:]
    y_ref, dx_ref, rd_ref, rg_ref, ru_ref, terms_ref = refs[:6]
    gate_w, up_w, down_w, acc, sems = refs[6:]
    copies = plan(core[0], own, other, gate_w, up_w, down_w, sems)
    s = pl.program_id(0)

    @pl.when(s == 0)
    def _():
        for c in copies:
            c.start()
        acc[...] = jnp.zeros_like(acc)
        for c in copies:
            c.wait()

    _, line, rows, width = gate_w.shape
    hidden = 2 * line * rows
    gate_m = gate_w[...].reshape(hidden, width)
    up_m = up_w[...].reshape(hidden, width)
    down_m = down_w[...].reshape(hidden, width)
    x, g = normed[0], grad[0]
    r_d, r_g, r_u = rank_d[0], rank_g[0], rank_u[0]
    sums = [0.0] * 5 if first else [r[0] for r in sums_in]
    for at in range(0, hidden, span):
        part = slice(at, min(at + span, hidden))
        o_g, o_u, i_d = out_g[part], out_u[part], in_d[part]
        w_g, w_u, w_d = gate_m[part], up_m[part], down_m[part]
        gate = nt(x, w_g) + adapter_scale * nt(r_g, o_g)
        up = nt(x, w_u) + adapter_scale * nt(r_u, o_u)
        d_act = nt(g, w_d) + nt(r_d, i_d)
        sig = 1.0 / (1.0 + jnp.exp(-gate))
        lit = gate * sig
        act = (lit * up).astype(bf16)
        d_gate = (d_act * up * sig * (1.0 + gate * (1.0 - sig))).astype(bf16)
        d_up = (d_act * lit).astype(bf16)
        sums[0] = sums[0] + nn(act, w_d)
        sums[1] = sums[1] + nn(d_gate, w_g) + nn(d_up, w_u)
        sums[2] = sums[2] + nn(act, i_d)
        sums[3] = sums[3] + nn(d_gate, o_g)
        sums[4] = sums[4] + nn(d_up, o_u)
        acc[0, :, part] += tn(r_g, d_gate)
        acc[1, :, part] += tn(r_u, d_up)
        acc[2, :, part] += tn(r_d, act)
    for ref, value in zip((y_ref, dx_ref, rd_ref, rg_ref, ru_ref), sums):
        ref[0] = value

    @pl.when(s == pl.num_programs(0) - 1)
    def _():
        for i, scale in enumerate((adapter_scale, adapter_scale, 1.0)):
            turned = (acc[i] * scale).T.astype(bf16)
            for side in range(2):
                for z in range(line):
                    at = (side * line + z) * rows
                    terms_ref[2 * z + side, i * rows : (i + 1) * rows, :] = turned[at : at + rows]


def feed_part(core, own, other, normed, grad, ranks, adapters, sums):
    slots, block, width = normed.shape
    hidden, rank_width = adapters[0].shape
    first = sums is None
    if own.shape[-1] == width:
        plan, count, line, rows = wide_copies, 6, own.shape[1], own.shape[2]
    else:
        shards, line = own.shape[:2]
        plan, count, rows = weight_copies, 2 * shards * (2 + line), own.shape[2] // 3
    anywhere = pl.BlockSpec(memory_space=pl.ANY)
    operands = (own, other, normed, grad, *ranks, *adapters)
    specs = [anywhere, anywhere, by_slot(normed), by_slot(grad)]
    specs += [by_slot(r) for r in ranks] + [whole(a) for a in adapters]
    aliases = {}
    if not first:
        aliases = {1 + len(operands) + i: i for i in range(len(sums))}
        operands += tuple(sums)
        specs += [by_slot(a) for a in sums]
    rank_sum = struct((slots, block, rank_width), f32)
    wide_sum = struct((slots, block, width), f32)
    terms = struct((2 * line, 3 * rows, rank_width), bf16)
    outs = (wide_sum, wide_sum, rank_sum, rank_sum, rank_sum, terms)
    buffer = pltpu.VMEM((2, line, rows, width), bf16)
    return pl.pallas_call(
        functools.partial(feed_kernel, first, plan, 512),
        grid_spec=pltpu.PrefetchScalarGridSpec(
            num_scalar_prefetch=1,
            grid=(slots,),
            in_specs=specs,
            out_specs=[by_slot(o) for o in outs[:5]] + [whole(terms)],
            scratch_shapes=[
                buffer,
                buffer,
                buffer,
                pltpu.VMEM((3, rank_width, hidden), f32),
                pltpu.SemaphoreType.DMA((count,)),
            ],
        ),
        out_shape=outs,
        input_output_aliases=aliases,
        compiler_params=params(),
        cost_estimate=cost(15 * slots * block * hidden * width, 60e6, slots * block * hidden),
        name="feed_part",
    )(core, *operands)


def rms_back(hidden, gain, grad_normed):
    scaled = grad_normed * gain
    inverse = lax.rsqrt(jnp.mean(hidden * hidden, axis=-1, keepdims=True) + norm_eps)
    return inverse * scaled - hidden * (inverse * inverse * inverse) * jnp.mean(
        scaled * hidden, axis=-1, keepdims=True
    )


def keep_terms(acc, out, terms):
    s = pl.program_id(0)
    total = acc.shape[1]

    @pl.when(s == 0)
    def _():
        at = 0
        for t in terms:
            acc[:, at : at + t.shape[1]] = t
            at += t.shape[1]

    @pl.when(s != 0)
    def _():
        at = 0
        for t in terms:
            acc[:, at : at + t.shape[1]] += t
            at += t.shape[1]

    @pl.when(s == pl.num_programs(0) - 1)
    def _():
        for i in range(out.shape[0]):
            if i * PIECE < total:
                out[i] = acc[:, i * PIECE : (i + 1) * PIECE].astype(bf16)
            else:
                out[i] = jnp.zeros(out.shape[1:], bf16)


def return_kernel(
    adapter, live, y, dx, sum_d, sum_g, sum_u, mid_in, normed, grad, context, rank_o, rank_d, weight,
    in_o, out_o, gain, in_g, in_u, out_d, layer_ref, d_mid_ref, d_ctx_ref, terms_ref, acc,
):
    s = pl.program_id(0)
    on = jnp.where(live[s] != 0, 1.0, 0.0)
    mid = mid_in[0]
    g = grad[0]
    mask = slot_lanes(adapter, g.shape[0], in_o.shape[0])
    rank_down = picked(mask, sum_d[0])
    result = mid + y[0] + adapter_scale * nn(rank_down, out_d[...])
    layer_ref[0] = (result * on).astype(bf16)
    back_g = picked(mask, adapter_scale * sum_g[0])
    back_u = picked(mask, adapter_scale * sum_u[0])
    d_normed = dx[0] + nn(back_g, in_g[...]) + nn(back_u, in_u[...])
    d_mid = g.astype(f32) + rms_back(mid, gain[...], d_normed)
    d_mid_ref[0] = d_mid
    branch = d_mid.astype(bf16)
    back_o = picked(mask, adapter_scale * nt(branch, out_o[...]))
    d_ctx_ref[0] = (nn(branch, weight[...]) + nn(back_o, in_o[...])).astype(bf16)
    x = normed[0]
    keep_terms(
        acc,
        terms_ref,
        (
            tn(back_o, context[0]),
            adapter_scale * tn(rank_o[0], branch),
            tn(back_g, x),
            tn(back_u, x),
            adapter_scale * tn(rank_down, g),
        ),
    )


def piece_count(columns):
    devices = lax.axis_size("ctx") * lax.axis_size("wsh")
    pieces = -(-columns // PIECE)
    return pieces + -pieces % devices


def return_side(adapter_of, live, sums, mid, normed, grad, context, rank_o, rank_d, weight, in_o, out_o,
                gain, in_g, in_u, out_d):
    slots, block, width = mid.shape
    rows = (*sums, mid, normed, grad, context, rank_o, rank_d)
    shared = (weight, in_o, out_o, gain, in_g, in_u, out_d)
    ranks = in_o.shape[0]
    outs = (
        struct(mid.shape, bf16),
        struct(mid.shape, f32),
        struct(mid.shape, bf16),
        struct((piece_count(5 * width), ranks, PIECE), bf16),
    )
    return pl.pallas_call(
        return_kernel,
        grid_spec=pltpu.PrefetchScalarGridSpec(
            num_scalar_prefetch=2,
            grid=(slots,),
            in_specs=[by_slot(r) for r in rows] + [whole(a) for a in shared],
            out_specs=[by_slot(o) for o in outs[:3]] + [whole(outs[3])],
            scratch_shapes=[pltpu.VMEM((ranks, 5 * width), f32)],
        ),
        out_shape=outs,
        compiler_params=params(),
        cost_estimate=cost(4 * slots * block * width * width, 50e6),
        name="return_side",
    )(adapter_of, live, *rows, *shared)


def query_back_kernel(
    adapter, d_query, normed, rank_q, weight, in_q, out_q, d_normed_ref, terms_ref, acc
):
    g, x = d_query[0], normed[0]
    mask = slot_lanes(adapter, g.shape[0], in_q.shape[0])
    rank_back = picked(mask, adapter_scale * nt(g, out_q[...]))
    d_normed_ref[0] = nn(g, weight[...]) + nn(rank_back, in_q[...])
    keep_terms(acc, terms_ref, (tn(rank_back, x), adapter_scale * tn(rank_q[0], g)))


def query_back_side(adapter_of, d_query, normed, rank_q, weight, in_q, out_q):
    slots, block, width = normed.shape
    ranks = in_q.shape[0]
    rows = (d_query, normed, rank_q)
    shared = (weight, in_q, out_q)
    outs = (
        struct(normed.shape, f32),
        struct((piece_count(2 * width), ranks, PIECE), bf16),
    )
    return pl.pallas_call(
        query_back_kernel,
        grid_spec=pltpu.PrefetchScalarGridSpec(
            num_scalar_prefetch=1,
            grid=(slots,),
            in_specs=[by_slot(r) for r in rows] + [whole(a) for a in shared],
            out_specs=[by_slot(outs[0]), whole(outs[1])],
            scratch_shapes=[pltpu.VMEM((ranks, 2 * width), f32)],
        ),
        out_shape=outs,
        compiler_params=params(),
        cost_estimate=cost(3 * slots * block * width * width, 22e6),
        name="query_back_side",
    )(adapter_of, *rows, *shared)


def output_kernel(
    adapter, live, d_kv, d_normed_q, d_mid, normed, rank_k, rank_v, tok, weight, gain, cosine, sine,
    in_k, in_v, out_k, out_v, grad_ref, terms_ref, acc,
):
    s = pl.program_id(0)
    on = jnp.where(live[s] != 0, 1.0, 0.0)
    kv_width = d_kv.shape[-1] // 2
    cos, sin = cosine[...], sine[...]
    back = d_kv[0]
    x = normed[0]
    mask = slot_lanes(adapter, x.shape[0], in_k.shape[0])
    keys = []
    for h in range(kv_width // HEAD_DIM):
        keys.append(turn_back(back[:, h * HEAD_DIM : (h + 1) * HEAD_DIM], cos, sin).astype(bf16))
    g_k, g_v = jnp.concatenate(keys, axis=1), back[:, kv_width:].astype(bf16)
    back_k = picked(mask, adapter_scale * nt(g_k, out_k[...]))
    back_v = picked(mask, adapter_scale * nt(g_v, out_v[...]))
    d_normed = d_normed_q[0] + nn(g_k, weight[:kv_width]) + nn(g_v, weight[kv_width:])
    d_normed = d_normed + nn(back_k, in_k[...]) + nn(back_v, in_v[...])
    hidden = tok[0].astype(f32)
    d_hidden = d_mid[0] + rms_back(hidden, gain[...], d_normed)
    grad_ref[0] = (d_hidden * on).astype(bf16)
    keep_terms(
        acc,
        terms_ref,
        (
            tn(back_k, x),
            tn(back_v, x),
            adapter_scale * tn(rank_k[0], g_k),
            adapter_scale * tn(rank_v[0], g_v),
        ),
    )


def output_side(adapter_of, live, d_kv, d_normed_q, d_mid, normed, rank_k, rank_v, tokens, weight, gain,
                cosine, sine, adapters):
    slots, block, width = tokens.shape
    ranks = adapters[0].shape[0]
    columns = 2 * width + weight.shape[0]
    rows = (d_kv, d_normed_q, d_mid, normed, rank_k, rank_v, tokens)
    shared = (weight, gain, cosine, sine, *adapters)
    outs = (
        struct(tokens.shape, bf16),
        struct((piece_count(columns), ranks, PIECE), bf16),
    )
    return pl.pallas_call(
        output_kernel,
        grid_spec=pltpu.PrefetchScalarGridSpec(
            num_scalar_prefetch=2,
            grid=(slots,),
            in_specs=[by_slot(r) for r in rows] + [whole(a) for a in shared],
            out_specs=[by_slot(outs[0]), whole(outs[1])],
            scratch_shapes=[pltpu.VMEM((ranks, columns), f32)],
        ),
        out_shape=outs,
        compiler_params=params(),
        cost_estimate=cost(3 * slots * block * width * weight.shape[0], 30e6),
        name="output_side",
    )(adapter_of, live, *rows, *shared)


def prompt_blocks(mine, place, line):
    half = line // 2
    from_above = [mine]
    for _ in range(line - 1):
        t = len(from_above)
        pairs = [(z, z - 1) for z in range(1, line) if half <= z + t - 1 < line]
        from_above.append(along_line(from_above[-1], pairs))
    from_below = [mine]
    for _ in range(half - 1):
        t = len(from_below)
        pairs = [(z, z + 1) for z in range(line - 1) if half <= z - t + 1]
        from_below.append(along_line(from_below[-1], pairs))
    blocks = []
    for b in range(half, line):
        out = mine
        for z in range(line):
            if z < b:
                out = jnp.where(place == z, from_above[b - z], out)
            elif z > b:
                out = jnp.where(place == z, from_below[z - b], out)
        blocks.append(out)
    return jnp.stack(blocks)


def return_blocks(parts, place, line):
    half = line // 2

    def chain(parts, sends):
        total = parts
        for pairs, block_of in sends:
            at = jnp.clip(block_of - half, 0, half - 1)
            out = lax.dynamic_index_in_dim(total, at, 0, False)
            came, at_in = along_line(out, pairs[0]), jnp.clip(pairs[1] - half, 0, half - 1)
            old = lax.dynamic_index_in_dim(total, at_in, 0, False)
            total = lax.dynamic_update_index_in_dim(
                total, (old.astype(f32) + came.astype(f32)).astype(total.dtype), at_in, 0
            )
        return total

    up = []
    for t in range(1, line):
        pairs = [(z, z + 1) for z in range(line - 1) if half <= line - t + z < line]
        up.append(((pairs, line - t + place - 1), line - t + place))
    down = []
    for t in range(1, half):
        shift = half - 1 + t - (line - 1)
        pairs = [(z, z - 1) for z in range(1, line) if half <= shift + z < z]
        down.append(((pairs, shift + place + 1), shift + place))
    owned = jnp.clip(place - half, 0, half - 1)
    own = lax.dynamic_index_in_dim(parts, owned, 0, False).astype(f32)
    through_up = lax.dynamic_index_in_dim(chain(parts, up), owned, 0, False).astype(f32)
    if not down:
        return jnp.where(place >= half, through_up, 0.0)
    through_down = lax.dynamic_index_in_dim(chain(parts, down), owned, 0, False).astype(f32)
    return jnp.where(place >= half, through_up + through_down - own, 0.0)


def sum_pieces(pieces, place, core, shard, line):
    shards = lax.axis_size("wsh")
    each = pieces.shape[0] // (2 * line * shards)
    cut = pieces.reshape((2 * line, shards, each) + pieces.shape[1:])
    mine = reduce_wsh(reduce_ctx(cut, place, core, line), shard)
    return gather_all(mine, place, core, shard, line).reshape(pieces.shape)


def lay_out_kernel(widths, *refs):
    pieces, outs = refs[0], refs[1:]
    at = 0
    for out, width in zip(outs, widths):
        for i in range(width // PIECE):
            block = pieces[at].astype(f32)
            out[:, :, i * PIECE : (i + 1) * PIECE] = block.reshape(out.shape[:2] + (PIECE,))
            at += 1


def lay_out(pieces, widths):
    adapters = pieces.shape[1] // RANK
    return pl.pallas_call(
        functools.partial(lay_out_kernel, widths),
        out_shape=tuple(struct((adapters, RANK, w), f32) for w in widths),
        compiler_params=pltpu.CompilerParams(vmem_limit_bytes=VMEM_LIMIT),
        name="lay_out",
    )(pieces)


def turn_kernel(sums, *outs):
    for i, out in enumerate(outs):
        out[...] = sums[i].astype(f32).T.reshape(out.shape)


def turn_over(sums):
    count, hidden, ranks = sums.shape
    step = 1280
    out = struct((ranks // RANK, RANK, hidden), f32)
    return pl.pallas_call(
        turn_kernel,
        grid=(hidden // step,),
        in_specs=[pl.BlockSpec((count, step, ranks), lambda i: (0, i, 0))],
        out_specs=[pl.BlockSpec(out.shape[:2] + (step,), lambda i: (0, 0, i))] * count,
        out_shape=(out,) * count,
        compiler_params=params(),
        name="turn_over",
    )(sums)


def local(
    tokens,
    cotangent,
    group_slot,
    group_adapter,
    attn_gain,
    mlp_gain,
    w_query,
    w_key,
    w_value,
    w_output,
    w_gate,
    w_up,
    w_down,
    query_bias,
    key_bias,
    value_bias,
    adapt_query_in,
    adapt_query_out,
    adapt_key_in,
    adapt_key_out,
    adapt_value_in,
    adapt_value_out,
    adapt_output_in,
    adapt_output_out,
    adapt_gate_in,
    adapt_gate_out,
    adapt_up_in,
    adapt_up_out,
    adapt_down_in,
    adapt_down_out,
):
    slots, block, width = tokens.shape
    ctx_size, shards = lax.axis_size("ctx"), lax.axis_size("wsh")
    line = ctx_size // 2
    ctx_place, shard_place = lax.axis_index("ctx"), lax.axis_index("wsh")
    place, core = ctx_place // 2, ctx_place % 2
    kv_width = key_bias.shape[0]
    kv_heads = kv_width // HEAD_DIM
    hidden = adapt_gate_out.shape[-1]
    if line != shards or (CONTS * CONT) != line * block or CONT // block > 2:
        raise ValueError("unsupported mesh")
    mates = CONT // block - 1

    slot_ids = shard_place * slots + jnp.arange(slots, dtype=jnp.int32)
    matches = group_slot[None, :] == slot_ids[:, None]
    live = jnp.any(matches, axis=1).astype(jnp.int32)
    adapter_of = jnp.sum(jnp.where(matches, group_adapter[None, :], 0), axis=1).astype(jnp.int32)
    index = ctx_place * block + jnp.arange(block, dtype=jnp.int32)
    position = jnp.where(index >= CONTS * CONT, index - CONTS * CONT, PROMPT + index % CONT)
    frequency = rope_base ** (-(jnp.arange(HEAD_DIM // 2, dtype=f32) * 2.0) / HEAD_DIM)
    angles = position.astype(f32)[:, None] * frequency[None, :]
    cosine = jnp.concatenate([jnp.cos(angles), jnp.cos(angles)], axis=-1)
    sine = jnp.concatenate([-jnp.sin(angles), jnp.sin(angles)], axis=-1)

    is_cont = ctx_place < line
    of_side = [2 * (line // 2 + i) + core for i in range(line // 2)]
    of_other = [2 * (line // 2 + i) + 1 - core for i in range(line // 2)]
    flags = [(is_cont | (b < ctx_place)) for b in of_side + of_other]
    flags += [is_cont & (core == 1)] if mates else []
    flags = jnp.stack(flags).astype(jnp.int32)

    def natural(own, other, at, count):
        pair = jnp.stack([own[:, :, at : at + count], other[:, :, at : at + count]])
        pair = jnp.where(core == 0, pair, pair[::-1])
        return jnp.transpose(pair, (2, 0, 3, 1, 4)).reshape(line * 2 * count, width)

    q_rows, kv_rows = w_query.shape[1], w_key.shape[1]
    lined_qkv = line_gather(jnp.concatenate([w_query.T, w_key.T, w_value.T], axis=0), place, line)
    own = shard_gather(lined_qkv)
    other = swap_cores(own)
    (o_piece,) = hold([w_output.T], lined_qkv)
    lined_o = line_gather(o_piece, place, line)
    q_weight = natural(own, other, 0, q_rows)
    kv_weight = jnp.concatenate(
        [natural(own, other, q_rows, kv_rows), natural(own, other, q_rows + kv_rows, kv_rows)], axis=0
    )
    own = shard_gather(lined_o)
    other = swap_cores(own)
    o_weight = natural(own, other, 0, w_output.shape[1])

    shard_hidden = w_gate.shape[1]
    shard_cols = w_gate.shape[0]
    parts = 5
    rows = shard_hidden // parts
    halves = w_down.reshape(2, shard_hidden, w_down.shape[1])
    kept = lax.dynamic_index_in_dim(halves, core, 0, False)
    given = swap_cores(lax.dynamic_index_in_dim(halves, 1 - core, 0, False))
    down_piece = jnp.where(
        core == 0,
        jnp.concatenate([kept, given], axis=1),
        jnp.concatenate([given, kept], axis=1),
    )
    turned = [w_gate.T, w_up.T, down_piece]
    pieces = [
        jnp.concatenate([m[i * rows : (i + 1) * rows] for m in turned], axis=0) for i in range(parts)
    ]
    (pieces[0],) = hold([pieces[0]], lined_o)
    lined = [line_gather(pieces[0], place, line)]
    halves = [shard_gather(lined[0])]

    def widen(half):
        cut = half.reshape(shards, line, 3, rows, shard_cols)
        out_in = jnp.transpose(cut[:, :, :2], (2, 1, 3, 0, 4)).reshape(2, line, rows, width)
        in_out = jnp.transpose(cut[:, :, 2], (0, 2, 1, 3)).reshape(1, shards, rows, width)
        return jnp.concatenate([out_in, in_out], axis=0)

    def flat(adapters):
        return adapters.reshape(-1, adapters.shape[-1])

    def by_part(adapters):
        cut = flat(adapters).T.reshape(line, 2, parts, rows, -1)
        return jnp.transpose(cut, (2, 1, 0, 3, 4)).reshape(parts, hidden // parts, -1)

    query_in, key_in, value_in, output_in, gate_in, up_in = (
        flat(a)
        for a in (adapt_query_in, adapt_key_in, adapt_value_in, adapt_output_in, adapt_gate_in, adapt_up_in)
    )
    query_out, key_out, value_out, output_out, down_out = (
        flat(a)
        for a in (adapt_query_out, adapt_key_out, adapt_value_out, adapt_output_out, adapt_down_out)
    )

    gain_one = attn_gain.astype(f32)[None, :]
    gain_two = mlp_gain.astype(f32)[None, :]
    q_bias = query_bias.astype(f32)[None, :]
    kv_bias = jnp.concatenate([key_bias, value_bias]).astype(f32)[None, :]

    kv_adapters = (key_in, value_in, key_out, value_out)
    normed, rank_k, rank_v, key_value = key_value_side(
        adapter_of, tokens, gain_one, kv_weight, kv_bias, kv_adapters, cosine, sine
    )
    (pieces[1],) = hold([pieces[1]], key_value)
    side = prompt_blocks(key_value, place, line)
    other_side = swap_cores(side)
    mate = (swap_cores(key_value),) if mates else ()
    rank_q, queries = query_side(
        adapter_of, normed, q_weight, q_bias, (query_in, query_out), cosine, sine
    )
    context, mixed, logs = attend(flags, queries, key_value, side, other_side, mate, kv_heads)
    lined.append(line_gather(pieces[1], place, line, (context,)))
    halves.append(shard_gather(lined[1]))
    halves[0], pieces[2] = hold([halves[0], pieces[2]], context, lined[1])
    others = [swap_cores(halves[0])]
    mid, normed2, grad_out, rank_o, rank_g, rank_u, rank_d = middle_side(
        adapter_of, live, context, tokens, cotangent, o_weight, output_in, output_out, gain_two,
        gate_in, up_in, down_out,
    )

    down_in, gate_out, up_out = by_part(adapt_down_in), by_part(adapt_gate_out), by_part(adapt_up_out)
    core_place = core.astype(jnp.int32)[None]
    lined.append(line_gather(pieces[2], place, line, (normed2,)))
    halves.append(shard_gather(lined[2]))
    (normed2, pieces[3]) = hold([normed2, pieces[3]], lined[2])
    sums, hidden_terms = None, []
    for i in range(parts):
        if i:
            ready = list(sums[2:3])
            if i + 2 < parts:
                ready.append(lined[i + 2])
            if i >= 2:
                ready.append(hidden_terms[i - 2])
            (halves[i],) = hold([halves[i]], *ready)
            others.append(swap_cores(halves[i]))
        own, other = halves[i], others[i]
        if shard_cols % 128:
            own, other = widen(own), widen(other)
        *sums, terms = feed_part(
            core_place, own, other, normed2, grad_out, (rank_d, rank_g, rank_u),
            (down_in[i], gate_out[i], up_out[i]), sums,
        )
        if i + 3 < parts:
            lined.append(line_gather(pieces[i + 3], place, line, (terms,)))
            halves.append(shard_gather(lined[i + 3]))
            if i + 4 < parts:
                (pieces[i + 4],) = hold([pieces[i + 4]], terms)
        hidden_terms.append(reduce_ctx(terms, place, core, line))
    (sums[2],) = hold([sums[2]], hidden_terms[parts - 2])
    hidden_terms = [t.reshape(3, rows, -1) for t in hidden_terms]
    layer_out, d_mid, d_context, terms = return_side(
        adapter_of, live, sums, mid, normed2, grad_out, context, rank_o, rank_d, o_weight,
        output_in, output_out, gain_two, gate_in, up_in, down_out,
    )

    hidden_terms = jnp.concatenate(hidden_terms, axis=1)
    hidden_terms = reduce_wsh(
        hidden_terms.reshape(shards, 3 * shard_hidden // shards, -1), shard_place
    )
    hidden_sums = gather_all(hidden_terms, place, core, shard_place, line)
    hidden_sums = hidden_sums.reshape(2 * line, 3, shard_hidden, -1)
    hidden_sums = jnp.transpose(hidden_sums, (1, 0, 2, 3)).reshape(3, hidden, -1)
    g_gate_out, g_up_out, g_down_in = turn_over(hidden_sums)
    g_output_in, g_output_out, g_gate_in, g_up_in, g_down_out = lay_out(
        sum_pieces(terms, place, core, shard_place, line), (width,) * 5
    )

    back = attend_back(
        flags, queries, key_value, side, other_side, mate, d_context, mixed, logs, cosine, sine, kv_heads
    )
    d_query, d_own, d_side, d_other = back[:4]
    d_side = (d_side.astype(f32) + swap_cores(d_other).astype(f32)).astype(bf16)
    d_kv = d_own + return_blocks(d_side, place, line)
    if mates:
        d_kv = d_kv + swap_cores(back[4]).astype(f32)
    d_normed_q, terms = query_back_side(
        adapter_of, d_query, normed, rank_q, q_weight, query_in, query_out
    )
    g_query_in, g_query_out = lay_out(
        sum_pieces(terms, place, core, shard_place, line), (width, width)
    )
    input_grad, terms = output_side(
        adapter_of, live, d_kv, d_normed_q, d_mid, normed, rank_k, rank_v, tokens, kv_weight, gain_one,
        cosine, sine, kv_adapters,
    )
    g_key_in, g_value_in, g_key_out, g_value_out = lay_out(
        sum_pieces(terms, place, core, shard_place, line), (width, width, kv_width, kv_width)
    )
    return (
        layer_out,
        input_grad,
        g_query_in,
        g_query_out,
        g_key_in,
        g_key_out,
        g_value_in,
        g_value_out,
        g_output_in,
        g_output_out,
        g_gate_in,
        g_gate_out,
        g_up_in,
        g_up_out,
        g_down_in,
        g_down_out,
    )


def solution(mesh):
    weight = P("wsh", "ctx")
    rows = P("wsh", "ctx", None)
    return jax.shard_map(
        local,
        mesh=mesh,
        in_specs=(rows, rows) + (P(),) * 4 + (weight,) * 7 + (P(),) * 17,
        out_specs=(rows, rows) + (P(),) * 14,
        check_vma=False,
    )
```

```python
import functools
import math

import jax
import jax.numpy as jnp
from jax import lax
from jax.experimental import pallas as pl
from jax.experimental.pallas import tpu as pltpu
from jax.sharding import PartitionSpec as P

HEAD_DIM = 128
PROMPT = 1024
CONTS = 4
CONT = 256
RANK = 16

norm_eps = 1e-06
adapter_scale = 0.5
rope_base = 1000000.0
masked_score = -1e30
score_scale = HEAD_DIM ** (-0.5)
score_to_log2 = score_scale * math.log2(math.e)

f32 = jnp.float32
bf16 = jnp.bfloat16
VMEM_LIMIT = 60 * 2**20


def nt(left, right):
    return lax.dot_general(left, right, (((1,), (1,)), ((), ())), preferred_element_type=f32)


def nn(left, right):
    return lax.dot_general(left, right, (((1,), (0,)), ((), ())), preferred_element_type=f32)


def tn(left, right):
    return lax.dot_general(left, right, (((0,), (0,)), ((), ())), preferred_element_type=f32)


def along_line(array, pairs):
    return lax.ppermute(array, "ctx", [(2 * a + c, 2 * b + c) for a, b in pairs for c in (0, 1)])


def swap_cores(array):
    size = lax.axis_size("ctx")
    return lax.ppermute(array, "ctx", [(i, i ^ 1) for i in range(size)])


def hold_kernel(*refs):
    pass


def hold(arrays, *after):
    anywhere = pl.BlockSpec(memory_space=pl.ANY)
    count = len(arrays)
    held = pl.pallas_call(
        hold_kernel,
        in_specs=[anywhere] * (count + len(after)),
        out_specs=[anywhere] * count,
        out_shape=[jax.ShapeDtypeStruct(a.shape, a.dtype) for a in arrays],
        input_output_aliases={i: i for i in range(count)},
        name="hold",
    )(*arrays, *after)
    return list(held)


def line_moves(piece, line):
    return [
        along_line(piece, [(i, (i + by) % line) for i in range(line)]) for by in range(1, line)
    ]


def in_order(piece, came, place, line):
    out = jnp.zeros((line,) + piece.shape, piece.dtype)
    out = lax.dynamic_update_index_in_dim(out, piece, place, 0)
    for by in range(1, line):
        out = lax.dynamic_update_index_in_dim(out, came[by - 1], (place - by) % line, 0)
    return out


def shard_gather(lined):
    return lax.all_gather(lined, "wsh", axis=0, tiled=False)


def add_up(arrays):
    return functools.reduce(jnp.add, [a.astype(f32) for a in arrays]).astype(bf16)


def line_outs(mine, place, line):
    return [
        lax.dynamic_index_in_dim(mine, (place + by) % line, 0, False) for by in range(1, line)
    ]


def line_send(outs, line):
    return [
        along_line(out, [(i, (i + by + 1) % line) for i in range(line)]) for by, out in enumerate(outs)
    ]


def line_sum(mine, place, came):
    return add_up([lax.dynamic_index_in_dim(mine, place, 0, False)] + came)


def across(array, by):
    size = lax.axis_size("wsh")
    return lax.ppermute(array, "wsh", [(i, i ^ by) for i in range(size)])


def wsh_outs(parts, shard):
    return [
        lax.dynamic_index_in_dim(parts, shard ^ by, 1, False) for by in range(1, parts.shape[1])
    ]


def wsh_send(outs):
    return [across(out, by + 1) for by, out in enumerate(outs)]


def wsh_sum(parts, shard, came):
    return add_up([lax.dynamic_index_in_dim(parts, shard, 1, False)] + came)


def tip(array):
    ends = (1,) * (array.ndim - 2) + (min(16, array.shape[-2]), min(128, array.shape[-1]))
    return lax.slice(array, (0,) * array.ndim, ends)


def gather_wsh(piece, shard, after=()):
    shards = lax.axis_size("wsh")
    came = [across(piece, by) for by in range(1, shards)]
    came = hold(came, *after) if after else came
    out = jnp.zeros((shards,) + piece.shape, piece.dtype)
    out = lax.dynamic_update_index_in_dim(out, piece, shard, 0)
    for by in range(1, shards):
        out = lax.dynamic_update_index_in_dim(out, came[by - 1], shard ^ by, 0)
    return out


def both_cores(half, other, core):
    return jnp.stack([jnp.where(core == 0, half, other), jnp.where(core == 0, other, half)])


def params(**more):
    return pltpu.CompilerParams(
        dimension_semantics=("arbitrary",), vmem_limit_bytes=VMEM_LIMIT, **more
    )


def whole(array):
    return pl.BlockSpec(array.shape, lambda s, *pre: (0,) * array.ndim)


def by_slot(array):
    return pl.BlockSpec((1,) + array.shape[1:], lambda s, *pre: (s,) + (0,) * (array.ndim - 1))


def second_by_slot(array):
    return pl.BlockSpec(
        (array.shape[0], 1) + array.shape[2:], lambda s, *pre: (0, s) + (0,) * (array.ndim - 2)
    )


def half_copies(core, own, other, parts, sems):
    copies = []
    shards, _, _, cols = own.shape
    for side, half in ((core, own), (1 - core, other)):
        for w in range(shards):
            for at, count, buffer in parts:
                copies.append(
                    pltpu.make_async_copy(
                        half.at[w, :, pl.ds(at, count), :],
                        buffer.at[:, side, :, pl.ds(w * cols, cols)],
                        sems.at[len(copies)],
                    )
                )
    return copies


def fetch_once(copies):
    @pl.when(pl.program_id(0) == 0)
    def _():
        for c in copies:
            c.start()
        for c in copies:
            c.wait()


def buffers(own, rows, width):
    line, shards = own.shape[1], own.shape[0]
    held = [pltpu.VMEM((line, 2, n, width), bf16) for n in rows]
    return held + [pltpu.SemaphoreType.DMA((2 * shards * len(rows),))]


def as_matrix(buffer):
    return buffer[...].reshape(-1, buffer.shape[-1])


anywhere = pl.BlockSpec(memory_space=pl.ANY)


def cost(flops, bytes_accessed, exps=0):
    return pl.CostEstimate(flops=int(flops), bytes_accessed=int(bytes_accessed), transcendentals=int(exps))


def slot_lanes(adapter, block, ranks):
    lane = lax.broadcasted_iota(jnp.int32, (block, ranks), 1)
    return lane // RANK == adapter[pl.program_id(0)]


def picked(mask, values):
    return jnp.where(mask, values, 0.0).astype(bf16)


def struct(shape, dtype):
    return jax.ShapeDtypeStruct(shape, dtype)


def turn(u, cos, sin):
    return u * cos + pltpu.roll(u, HEAD_DIM // 2, 1) * sin


def turn_back(u, cos, sin):
    return u * cos - pltpu.roll(u, HEAD_DIM // 2, 1) * sin


def key_value_kernel(
    first, adapter, core, own, other, tok, gain, bias, in_k, in_v, out_k, out_v, cosine, sine,
    normed_ref, rank_k_ref, rank_v_ref, kv_ref, key_w, value_w, sems,
):
    rows = key_w.shape[2]
    parts = ((first, rows, key_w), (first + rows, rows, value_w))
    fetch_once(half_copies(core[0], own, other, parts, sems))
    hidden = tok[0].astype(f32)
    inverse = lax.rsqrt(jnp.mean(hidden * hidden, axis=-1, keepdims=True) + norm_eps)
    normed = (hidden * inverse * gain[...]).astype(bf16)
    normed_ref[0] = normed
    mask = slot_lanes(adapter, normed.shape[0], in_k.shape[0])
    kv_width = kv_ref.shape[-1] // 2
    rank_k = picked(mask, nt(normed, in_k[...]))
    rank_v = picked(mask, nt(normed, in_v[...]))
    rank_k_ref[0], rank_v_ref[0] = rank_k, rank_v
    lin_k = nt(normed, as_matrix(key_w)) + bias[:, :kv_width]
    lin_v = nt(normed, as_matrix(value_w)) + bias[:, kv_width:]
    key = lin_k + adapter_scale * nn(rank_k, out_k[...])
    value = lin_v + adapter_scale * nn(rank_v, out_v[...])
    cos, sin = cosine[...], sine[...]
    for h in range(kv_width // HEAD_DIM):
        part = slice(h * HEAD_DIM, (h + 1) * HEAD_DIM)
        kv_ref[0, :, part] = turn(key[:, part], cos, sin).astype(bf16)
    kv_ref[0, :, kv_width:] = value.astype(bf16)


def key_value_side(adapter_of, core, own, other, first, tokens, gain, bias, adapters, cosine, sine):
    slots, block, width = tokens.shape
    kv_rows = bias.shape[1] // 4 // own.shape[1]
    shared = (gain, bias, *adapters, cosine, sine)
    ranks = struct((slots, block, adapters[0].shape[0]), bf16)
    outs = (struct(tokens.shape, bf16), ranks, ranks, struct((slots, block, bias.shape[1]), bf16))
    return pl.pallas_call(
        functools.partial(key_value_kernel, first),
        grid_spec=pltpu.PrefetchScalarGridSpec(
            num_scalar_prefetch=2,
            grid=(slots,),
            in_specs=[anywhere, anywhere, by_slot(tokens)] + [whole(a) for a in shared],
            out_specs=[by_slot(o) for o in outs],
            scratch_shapes=buffers(own, (kv_rows, kv_rows), width),
        ),
        out_shape=outs,
        compiler_params=params(),
        cost_estimate=cost(3 * slots * block * width * bias.shape[1], 12e6),
        name="key_value_side",
    )(adapter_of, core, own, other, tokens, *shared)


def query_kernel(
    adapter, core, own, other, normed, bias, in_q, out_q, cosine, sine, rank_ref, query_ref, weight, sems
):
    fetch_once(half_copies(core[0], own, other, ((0, weight.shape[2], weight),), sems))
    x = normed[0]
    mask = slot_lanes(adapter, x.shape[0], in_q.shape[0])
    rank = picked(mask, nt(x, in_q[...]))
    rank_ref[0] = rank
    query = nt(x, as_matrix(weight)) + bias[...] + adapter_scale * nn(rank, out_q[...])
    cos, sin = cosine[...], sine[...]
    for h in range(query.shape[1] // HEAD_DIM):
        part = slice(h * HEAD_DIM, (h + 1) * HEAD_DIM)
        query_ref[0, :, part] = turn(query[:, part], cos, sin).astype(bf16)


def query_side(adapter_of, core, own, other, normed, bias, adapters, cosine, sine):
    slots, block, width = normed.shape
    shared = (bias, *adapters, cosine, sine)
    outs = (struct((slots, block, adapters[0].shape[0]), bf16), struct(normed.shape, bf16))
    return pl.pallas_call(
        query_kernel,
        grid_spec=pltpu.PrefetchScalarGridSpec(
            num_scalar_prefetch=2,
            grid=(slots,),
            in_specs=[anywhere, anywhere, by_slot(normed)] + [whole(a) for a in shared],
            out_specs=[by_slot(o) for o in outs],
            scratch_shapes=buffers(own, (width // 2 // own.shape[1],), width),
        ),
        out_shape=outs,
        compiler_params=params(),
        cost_estimate=cost(2.5 * slots * block * width * width, 12e6),
        name="query_side",
    )(adapter_of, core, own, other, normed, *shared)


def attend_kernel(kv_heads, group, mates, flags, *refs):
    query, own, even, odd = refs[:4]
    mate = refs[4] if mates else None
    context_ref, mixed_ref, log_ref = refs[4 + mates :]
    block = query.shape[1]
    half = even.shape[0]
    kv_width = kv_heads * HEAD_DIM
    rows = lax.broadcasted_iota(jnp.int32, (block, block), 0)
    cols = lax.broadcasted_iota(jnp.int32, (block, block), 1)
    causal = rows <= cols
    bias = [jnp.where(flags[i] != 0, 0.0, masked_score) for i in range(2 * half + mates)]
    for kv in range(kv_heads):
        k_part = slice(kv * HEAD_DIM, (kv + 1) * HEAD_DIM)
        v_part = slice(kv_width + kv * HEAD_DIM, kv_width + (kv + 1) * HEAD_DIM)
        sources = [own[0]] + [even[i, 0] for i in range(half)] + [odd[i, 0] for i in range(half)]
        sources += [mate[0]] if mates else []
        keys = [s[:, k_part] for s in sources]
        values_t = [s[:, v_part].T for s in sources]
        for g in range(group):
            h = kv * group + g
            part = slice(h * HEAD_DIM, (h + 1) * HEAD_DIM)
            q = query[0, :, part]
            scores = [nt(k, q) for k in keys]
            scores[0] = jnp.where(causal, scores[0], masked_score)
            scores = scores[:1] + [s + b for s, b in zip(scores[1:], bias)]
            top = functools.reduce(jnp.maximum, [jnp.max(s, axis=0, keepdims=True) for s in scores])
            shift = top * score_to_log2
            total, mixed = 0.0, 0.0
            for s, v in zip(scores, values_t):
                p = jnp.exp2(s * score_to_log2 - shift)
                total = total + jnp.sum(p, axis=0, keepdims=True)
                mixed = mixed + nn(v, p.astype(bf16))
            mixed = mixed / total
            mixed_ref[0, h] = mixed
            log_ref[0, h : h + 1, :] = shift + jnp.log2(total)
            context_ref[0, :, part] = mixed.T.astype(bf16)


def attend(flags, query, own, even, odd, mate, kv_heads):
    slots, block, width = query.shape
    heads = width // HEAD_DIM
    mates = len(mate)
    operands = (query, own, even, odd, *mate)
    specs = [by_slot(query), by_slot(own), second_by_slot(even), second_by_slot(odd)]
    specs += [by_slot(m) for m in mate]
    outs = (
        struct((slots, block, width), bf16),
        struct((slots, heads, HEAD_DIM, block), f32),
        struct((slots, heads, block), f32),
    )
    return pl.pallas_call(
        functools.partial(attend_kernel, kv_heads, heads // kv_heads, mates),
        grid_spec=pltpu.PrefetchScalarGridSpec(
            num_scalar_prefetch=1, grid=(slots,), in_specs=specs, out_specs=[by_slot(o) for o in outs]
        ),
        out_shape=outs,
        compiler_params=params(),
        cost_estimate=cost(20e9, 20e6, slots * heads * block * (own.shape[1] * 5)),
        name="attend",
    )(flags, *operands)


def attend_back_kernel(kv_heads, group, mates, more, flags, *refs):
    refs = refs[more:]
    query, own, even, odd = refs[:4]
    mate = refs[4] if mates else None
    grad, mixed_ref, log_ref, cosine, sine = refs[4 + mates : 9 + mates]
    d_query, d_own, d_even, d_odd = refs[9 + mates : 13 + mates]
    d_mate = refs[13 + mates] if mates else None
    acc = refs[13 + 2 * mates]
    block = query.shape[1]
    half = even.shape[0]
    kv_width = kv_heads * HEAD_DIM
    rows = lax.broadcasted_iota(jnp.int32, (block, block), 0)
    cols = lax.broadcasted_iota(jnp.int32, (block, block), 1)
    causal = rows <= cols
    bias = [jnp.where(flags[i] != 0, 0.0, masked_score) for i in range(2 * half + mates)]
    cos, sin = cosine[...], sine[...]
    for kv in range(kv_heads):
        k_part = slice(kv * HEAD_DIM, (kv + 1) * HEAD_DIM)
        v_part = slice(kv_width + kv * HEAD_DIM, kv_width + (kv + 1) * HEAD_DIM)
        sources = [own[0]] + [even[i, 0] for i in range(half)] + [odd[i, 0] for i in range(half)]
        sources += [mate[0]] if mates else []
        keys = [s[:, k_part] for s in sources]
        keys_t = [k.T for k in keys]
        values = [s[:, v_part] for s in sources]
        for g in range(group):
            h = kv * group + g
            part = slice(h * HEAD_DIM, (h + 1) * HEAD_DIM)
            q = query[0, :, part]
            d_o = grad[0, :, part]
            delta = jnp.sum(d_o.astype(f32).T * mixed_ref[0, h], axis=0, keepdims=True)
            shift = log_ref[0, h : h + 1, :]
            d_q = 0.0
            for i in range(len(sources)):
                s = nt(keys[i], q)
                s = jnp.where(causal, s, masked_score) if i == 0 else s + bias[i - 1]
                p = jnp.exp2(s * score_to_log2 - shift)
                d_p = nt(values[i], d_o)
                d_s = (p * (d_p - delta)).astype(bf16)
                d_value = nn(p.astype(bf16), d_o)
                d_key = nn(d_s, q)
                if g == 0:
                    acc[i, :, v_part] = d_value
                    acc[i, :, k_part] = d_key
                else:
                    acc[i, :, v_part] += d_value
                    acc[i, :, k_part] += d_key
                d_q = d_q + nn(keys_t[i], d_s)
            u = d_q.T * score_scale
            d_query[0, :, part] = (u * cos - pltpu.roll(u, HEAD_DIM // 2, 1) * sin).astype(bf16)
    targets = [(d_own, 0)] + [(d_even, i) for i in range(half)] + [(d_odd, i) for i in range(half)]
    targets += [(d_mate, 0)] if mates else []
    for i, (target, j) in enumerate(targets):
        if target is d_own or target is d_mate:
            target[0, :, :kv_width] = (acc[i, :, :kv_width] * score_scale).astype(target.dtype)
            target[0, :, kv_width:] = acc[i, :, kv_width:].astype(target.dtype)
        else:
            target[j, 0, :, :kv_width] = (acc[i, :, :kv_width] * score_scale).astype(target.dtype)
            target[j, 0, :, kv_width:] = acc[i, :, kv_width:].astype(target.dtype)


def attend_back(flags, query, own, even, odd, mate, grad, mixed, logs, cosine, sine, kv_heads, start, slots, d_query=None):
    _, block, width = query.shape

    def by_slot(array):
        lead = array.ndim - 1
        return pl.BlockSpec((1,) + array.shape[1:], lambda s, *pre: (s + start,) + (0,) * lead)

    def second_by_slot(array):
        lead = array.ndim - 2
        shape = (array.shape[0], 1) + array.shape[2:]
        return pl.BlockSpec(shape, lambda s, *pre: (0, s + start) + (0,) * lead)

    def out_by_slot(array):
        return pl.BlockSpec((1,) + array.shape[1:], lambda s, *pre: (s,) + (0,) * (array.ndim - 1))

    def out_second(array):
        shape = (array.shape[0], 1) + array.shape[2:]
        return pl.BlockSpec(shape, lambda s, *pre: (0, s) + (0,) * (array.ndim - 2))

    heads = width // HEAD_DIM
    mates = len(mate)
    earlier = () if d_query is None else (d_query,)
    operands = (*earlier, query, own, even, odd, *mate, grad, mixed, logs, cosine, sine)
    specs = [anywhere] * len(earlier) + [by_slot(query), by_slot(own), second_by_slot(even), second_by_slot(odd)]
    specs += [by_slot(m) for m in mate]
    specs += [by_slot(grad), by_slot(mixed), by_slot(logs), whole(cosine), whole(sine)]
    outs = (
        struct(query.shape, bf16),
        struct((slots,) + own.shape[1:], f32),
        struct((even.shape[0], slots) + even.shape[2:], bf16),
        struct((odd.shape[0], slots) + odd.shape[2:], bf16),
        *(struct((slots,) + m.shape[1:], bf16) for m in mate),
    )
    out_specs = [by_slot(outs[0]), out_by_slot(outs[1]), out_second(even), out_second(odd)]
    out_specs += [out_by_slot(m) for m in mate]
    count = 1 + 2 * even.shape[0] + mates
    return pl.pallas_call(
        functools.partial(attend_back_kernel, kv_heads, heads // kv_heads, mates, len(earlier)),
        grid_spec=pltpu.PrefetchScalarGridSpec(
            num_scalar_prefetch=1,
            grid=(slots,),
            in_specs=specs,
            out_specs=out_specs,
            scratch_shapes=[pltpu.VMEM((count,) + own.shape[1:], f32)],
        ),
        out_shape=outs,
        input_output_aliases={1: 0} if earlier else {},
        compiler_params=params(),
        cost_estimate=cost(25e9, 20e6, slots * heads * block * (own.shape[1] * 5)),
        name="attend_back",
    )(flags, *operands)


def middle_kernel(
    first, adapter, live, core, own, other, context, tok, cot, in_o, out_o, gain, in_g, in_u, out_d,
    mid_ref, normed_ref, grad_ref, rank_o_ref, rank_g_ref, rank_u_ref, grad_rank_ref, weight, sems,
):
    fetch_once(half_copies(core[0], own, other, ((first, weight.shape[2], weight),), sems))
    s = pl.program_id(0)
    ctx = context[0]
    mask = slot_lanes(adapter, ctx.shape[0], in_o.shape[0])
    rank = picked(mask, nt(ctx, in_o[...]))
    rank_o_ref[0] = rank
    mid = tok[0].astype(f32) + nt(ctx, as_matrix(weight)) + adapter_scale * nn(rank, out_o[...])
    mid_ref[0] = mid
    inverse = lax.rsqrt(jnp.mean(mid * mid, axis=-1, keepdims=True) + norm_eps)
    normed = (mid * inverse * gain[...]).astype(bf16)
    normed_ref[0] = normed
    rank_g_ref[0] = picked(mask, nt(normed, in_g[...]))
    rank_u_ref[0] = picked(mask, nt(normed, in_u[...]))
    on = jnp.where(live[s] != 0, 1.0, 0.0)
    grad = (cot[0].astype(f32) * on).astype(bf16)
    grad_ref[0] = grad
    grad_rank_ref[0] = picked(mask, adapter_scale * nt(grad, out_d[...]))


def middle_side(adapter_of, live, core, own, other, first, context, tokens, cotangent, in_o, out_o, gain,
                in_g, in_u, out_d):
    slots, block, width = tokens.shape
    shared = (in_o, out_o, gain, in_g, in_u, out_d)
    rank = struct((slots, block, in_o.shape[0]), bf16)
    wide = struct(tokens.shape, bf16)
    outs = (struct(tokens.shape, f32), wide, wide, rank, rank, rank, rank)
    return pl.pallas_call(
        functools.partial(middle_kernel, first),
        grid_spec=pltpu.PrefetchScalarGridSpec(
            num_scalar_prefetch=3,
            grid=(slots,),
            in_specs=[anywhere, anywhere]
            + [by_slot(a) for a in (context, tokens, cotangent)]
            + [whole(a) for a in shared],
            out_specs=[by_slot(o) for o in outs],
            scratch_shapes=buffers(own, (width // 2 // own.shape[1],), width),
        ),
        out_shape=outs,
        compiler_params=params(),
        cost_estimate=cost(3 * slots * block * width * width, 28e6),
        name="middle_side",
    )(adapter_of, live, core, own, other, context, tokens, cotangent, *shared)


def feed_copies(half, gate, up, down, sems, base):
    copies = []

    def add(source, target):
        copies.append(pltpu.make_async_copy(source, target, sems.at[base + len(copies)]))

    shards, line, rows, cols = half.shape
    rows //= 3
    for w in range(shards):
        span = pl.ds(w * cols, cols)
        add(half.at[w, :, pl.ds(0, rows), :], gate.at[:, :, span])
        add(half.at[w, :, pl.ds(rows, rows), :], up.at[:, :, span])
    last = pl.ds(2 * rows, rows)
    if shards == 1:
        add(half.at[0, :, last, :], down)
    else:
        for w in range(shards):
            for z in range(line):
                add(half.at[w, z, last, :], down.at[w, :, pl.ds(z * cols, cols)])
    return copies


def feed_kernel(first, count, span, core, *refs):
    halves, refs = refs[:count], refs[count:]
    x_ref, g_ref, rank_d, rank_g, rank_u = refs[:5]
    adapters, refs = refs[5 : 5 + 3 * count], refs[5 + 3 * count :]
    if first:
        sums_in = None
    else:
        sums_in, refs = refs[:5], refs[5:]
    sums_out, terms, refs = refs[:5], refs[5 : 5 + count], refs[5 + count :]
    weights, accs, sems = refs[: 3 * count], refs[3 * count : 4 * count], refs[4 * count]
    s = pl.program_id(0)
    copies, base = [], 0
    for i in range(count):
        copies.append(feed_copies(halves[i], *weights[3 * i : 3 * i + 3], sems, base))
        base += len(copies[-1])

    @pl.when(s == 0)
    def _():
        for group in copies:
            for c in group:
                c.start()
        for acc in accs:
            acc[...] = jnp.zeros_like(acc)

    x, g = x_ref[0], g_ref[0]
    r_d, r_g, r_u = rank_d[0], rank_g[0], rank_u[0]
    sums = [0.0] * 5 if first else [r[0] for r in sums_in]
    for i in range(count):

        @pl.when(s == 0)
        def _(i=i):
            for c in copies[i]:
                c.wait()

        gate_m, up_m, down_m = (as_matrix(b) for b in weights[3 * i : 3 * i + 3])
        in_d, out_g, out_u = (a[0] for a in adapters[3 * i : 3 * i + 3])
        acc = accs[i]
        hidden = gate_m.shape[0]
        for at in range(0, hidden, span):
            part = slice(at, min(at + span, hidden))
            o_g, o_u, i_d = out_g[part], out_u[part], in_d[part]
            w_g, w_u, w_d = gate_m[part], up_m[part], down_m[part]
            gate = nt(x, w_g) + adapter_scale * nt(r_g, o_g)
            up = nt(x, w_u) + adapter_scale * nt(r_u, o_u)
            d_act = nt(g, w_d) + nt(r_d, i_d)
            sig = 1.0 / (1.0 + jnp.exp(-gate))
            lit = gate * sig
            act = (lit * up).astype(bf16)
            d_gate = (d_act * up * sig * (1.0 + gate * (1.0 - sig))).astype(bf16)
            d_up = (d_act * lit).astype(bf16)
            sums[0] = sums[0] + nn(act, w_d)
            sums[1] = sums[1] + nn(d_gate, w_g) + nn(d_up, w_u)
            sums[2] = sums[2] + nn(act, i_d)
            sums[3] = sums[3] + nn(d_gate, o_g)
            sums[4] = sums[4] + nn(d_up, o_u)
            acc[0, :, part] += tn(r_g, d_gate)
            acc[1, :, part] += tn(r_u, d_up)
            acc[2, :, part] += tn(r_d, act)
    for ref, value in zip(sums_out, sums):
        ref[0] = value

    @pl.when(s == pl.num_programs(0) - 1)
    def _():
        for i in range(count):
            line, rows, _ = weights[3 * i].shape
            for j, scale in enumerate((adapter_scale, adapter_scale, 1.0)):
                turned = (accs[i][j] * scale).T.astype(bf16)
                for z in range(line):
                    terms[i][z, j * rows : (j + 1) * rows, :] = turned[z * rows : (z + 1) * rows]


def feed_part(core, halves, normed, grad, ranks, sums):
    slots, block, width = normed.shape
    rank_width = ranks[0].shape[-1]
    count = len(halves)
    first = sums is None
    operands = [h[0] for h in halves] + [normed, grad, *ranks]
    specs = [anywhere] * count + [by_slot(a) for a in (normed, grad, *ranks)]
    for _, of_other, adapters in halves:
        for a in adapters:
            operands.append(a)
            side = (lambda s, c: (1 - c[0], 0, 0)) if of_other else (lambda s, c: (c[0], 0, 0))
            specs.append(pl.BlockSpec((1,) + a.shape[1:], side))
    aliases = {}
    if not first:
        aliases = {1 + len(operands) + i: i for i in range(len(sums))}
        operands += list(sums)
        specs += [by_slot(a) for a in sums]
    rank_sum = struct((slots, block, rank_width), f32)
    wide_sum = struct((slots, block, width), f32)
    outs = [wide_sum, wide_sum, rank_sum, rank_sum, rank_sum]
    out_specs = [by_slot(o) for o in outs]
    scratch, hidden, copies = [], 0, 0
    for half, _, _ in halves:
        shards, line, rows = half.shape[:3]
        terms = struct((line, rows, rank_width), bf16)
        outs.append(terms)
        out_specs.append(whole(terms))
        scratch += [pltpu.VMEM((line, rows // 3, width), bf16)] * 3
        hidden += line * rows // 3
        copies += 2 * shards + (1 if shards == 1 else shards * line)
    for half, _, _ in halves:
        scratch.append(pltpu.VMEM((3, rank_width, half.shape[1] * half.shape[2] // 3), f32))
    return pl.pallas_call(
        functools.partial(feed_kernel, first, count, 512),
        grid_spec=pltpu.PrefetchScalarGridSpec(
            num_scalar_prefetch=1,
            grid=(slots,),
            in_specs=specs,
            out_specs=out_specs,
            scratch_shapes=scratch + [pltpu.SemaphoreType.DMA((copies,))],
        ),
        out_shape=outs,
        input_output_aliases=aliases,
        compiler_params=params(),
        cost_estimate=cost(20 * slots * block * hidden * width, 60e6, slots * block * hidden),
        name="feed_part",
    )(core, *operands)


def rms_back(hidden, gain, grad_normed):
    scaled = grad_normed * gain
    inverse = lax.rsqrt(jnp.mean(hidden * hidden, axis=-1, keepdims=True) + norm_eps)
    return inverse * scaled - hidden * (inverse * inverse * inverse) * jnp.mean(
        scaled * hidden, axis=-1, keepdims=True
    )


def keep_terms(acc, out, core, terms):
    s = pl.program_id(0)

    @pl.when(s == 0)
    def _():
        at = 0
        for t in terms:
            acc[:, at : at + t.shape[1]] = t
            at += t.shape[1]

    @pl.when(s != 0)
    def _():
        at = 0
        for t in terms:
            acc[:, at : at + t.shape[1]] += t
            at += t.shape[1]

    @pl.when(s == pl.num_programs(0) - 1)
    def _():
        line = out.shape[1]
        at, row = 0, 0
        for t in terms:
            n = t.shape[1]
            cut = n // (2 * line)
            turned = acc[:, at : at + n].T.astype(bf16)
            for z in range(line):
                for side in (0, 1):
                    block = turned[(2 * z + side) * cut : (2 * z + side + 1) * cut]
                    out[jnp.where(core == side, 0, 1), z, row : row + cut, :] = block
            at += n
            row += cut


def turned_terms(line, columns, ranks):
    return struct((2, line, columns // (2 * line), ranks), bf16)


def return_kernel(
    first, adapter, live, core, own, other, y, dx, sum_d, sum_g, sum_u, mid_in, normed, grad, context,
    rank_o, in_o, out_o, gain, in_g, in_u, out_d, layer_ref, d_mid_ref, d_ctx_ref, terms_ref, acc,
    weight, sems,
):
    fetch_once(half_copies(core[0], own, other, ((first, weight.shape[2], weight),), sems))
    s = pl.program_id(0)
    on = jnp.where(live[s] != 0, 1.0, 0.0)
    mid = mid_in[0]
    g = grad[0]
    mask = slot_lanes(adapter, g.shape[0], in_o.shape[0])
    rank_down = picked(mask, sum_d[0])
    result = mid + y[0] + adapter_scale * nn(rank_down, out_d[...])
    layer_ref[0] = (result * on).astype(bf16)
    back_g = picked(mask, adapter_scale * sum_g[0])
    back_u = picked(mask, adapter_scale * sum_u[0])
    d_normed = dx[0] + nn(back_g, in_g[...]) + nn(back_u, in_u[...])
    d_mid = g.astype(f32) + rms_back(mid, gain[...], d_normed)
    d_mid_ref[0] = d_mid
    branch = d_mid.astype(bf16)
    back_o = picked(mask, adapter_scale * nt(branch, out_o[...]))
    d_ctx_ref[0] = (nn(branch, as_matrix(weight)) + nn(back_o, in_o[...])).astype(bf16)
    x = normed[0]
    keep_terms(
        acc,
        terms_ref,
        core[0],
        (
            tn(back_o, context[0]),
            adapter_scale * tn(rank_o[0], branch),
            tn(back_g, x),
            tn(back_u, x),
            adapter_scale * tn(rank_down, g),
        ),
    )


def return_side(adapter_of, live, core, own, other, first, sums, mid, normed, grad, context, rank_o, in_o,
                out_o, gain, in_g, in_u, out_d):
    slots, block, width = mid.shape
    rows = (*sums, mid, normed, grad, context, rank_o)
    shared = (in_o, out_o, gain, in_g, in_u, out_d)
    ranks = in_o.shape[0]
    outs = (
        struct(mid.shape, bf16),
        struct(mid.shape, f32),
        struct(mid.shape, bf16),
        turned_terms(own.shape[1], 5 * width, ranks),
    )
    return pl.pallas_call(
        functools.partial(return_kernel, first),
        grid_spec=pltpu.PrefetchScalarGridSpec(
            num_scalar_prefetch=3,
            grid=(slots,),
            in_specs=[anywhere, anywhere] + [by_slot(r) for r in rows] + [whole(a) for a in shared],
            out_specs=[by_slot(o) for o in outs[:3]] + [whole(outs[3])],
            scratch_shapes=[pltpu.VMEM((ranks, 5 * width), f32)]
            + buffers(own, (width // 2 // own.shape[1],), width),
        ),
        out_shape=outs,
        compiler_params=params(),
        cost_estimate=cost(4 * slots * block * width * width, 50e6),
        name="return_side",
    )(adapter_of, live, core, own, other, *rows, *shared)


def query_back_kernel(
    adapter, core, own, other, d_query, normed, rank_q, in_q, out_q, d_normed_ref, terms_ref, acc,
    weight, sems,
):
    fetch_once(half_copies(core[0], own, other, ((0, weight.shape[2], weight),), sems))
    g, x = d_query[0], normed[0]
    mask = slot_lanes(adapter, g.shape[0], in_q.shape[0])
    rank_back = picked(mask, adapter_scale * nt(g, out_q[...]))
    d_normed_ref[0] = nn(g, as_matrix(weight)) + nn(rank_back, in_q[...])
    keep_terms(acc, terms_ref, core[0], (tn(rank_back, x), adapter_scale * tn(rank_q[0], g)))


def query_back_side(adapter_of, core, own, other, d_query, normed, rank_q, in_q, out_q):
    slots, block, width = normed.shape
    ranks = in_q.shape[0]
    rows = (d_query, normed, rank_q)
    shared = (in_q, out_q)
    outs = (struct(normed.shape, f32), turned_terms(own.shape[1], 2 * width, ranks))
    return pl.pallas_call(
        query_back_kernel,
        grid_spec=pltpu.PrefetchScalarGridSpec(
            num_scalar_prefetch=2,
            grid=(slots,),
            in_specs=[anywhere, anywhere] + [by_slot(r) for r in rows] + [whole(a) for a in shared],
            out_specs=[by_slot(outs[0]), whole(outs[1])],
            scratch_shapes=[pltpu.VMEM((ranks, 2 * width), f32)]
            + buffers(own, (width // 2 // own.shape[1],), width),
        ),
        out_shape=outs,
        compiler_params=params(),
        cost_estimate=cost(3 * slots * block * width * width, 22e6),
        name="query_back_side",
    )(adapter_of, core, own, other, *rows, *shared)


def output_kernel(
    first, adapter, live, core, own, other, d_kv, d_normed_q, d_mid, normed, rank_k, rank_v, tok, gain,
    cosine, sine, in_k, in_v, out_k, out_v, grad_ref, terms_ref, acc, key_w, value_w, sems,
):
    count = key_w.shape[2]
    parts = ((first, count, key_w), (first + count, count, value_w))
    fetch_once(half_copies(core[0], own, other, parts, sems))
    s = pl.program_id(0)
    on = jnp.where(live[s] != 0, 1.0, 0.0)
    kv_width = d_kv.shape[-1] // 2
    cos, sin = cosine[...], sine[...]
    back = d_kv[0]
    x = normed[0]
    mask = slot_lanes(adapter, x.shape[0], in_k.shape[0])
    keys = []
    for h in range(kv_width // HEAD_DIM):
        keys.append(turn_back(back[:, h * HEAD_DIM : (h + 1) * HEAD_DIM], cos, sin).astype(bf16))
    g_k, g_v = jnp.concatenate(keys, axis=1), back[:, kv_width:].astype(bf16)
    back_k = picked(mask, adapter_scale * nt(g_k, out_k[...]))
    back_v = picked(mask, adapter_scale * nt(g_v, out_v[...]))
    d_normed = d_normed_q[0] + nn(g_k, as_matrix(key_w)) + nn(g_v, as_matrix(value_w))
    d_normed = d_normed + nn(back_k, in_k[...]) + nn(back_v, in_v[...])
    hidden = tok[0].astype(f32)
    d_hidden = d_mid[0] + rms_back(hidden, gain[...], d_normed)
    grad_ref[0] = (d_hidden * on).astype(bf16)
    keep_terms(
        acc,
        terms_ref,
        core[0],
        (
            tn(back_k, x),
            tn(back_v, x),
            adapter_scale * tn(rank_k[0], g_k),
            adapter_scale * tn(rank_v[0], g_v),
        ),
    )


def output_side(adapter_of, live, core, own, other, first, d_kv, d_normed_q, d_mid, normed, rank_k, rank_v,
                tokens, gain, cosine, sine, adapters):
    slots, block, width = tokens.shape
    ranks = adapters[0].shape[0]
    kv_columns = d_kv.shape[-1]
    columns = 2 * width + kv_columns
    kv_rows = kv_columns // 4 // own.shape[1]
    rows = (d_kv, d_normed_q, d_mid, normed, rank_k, rank_v, tokens)
    shared = (gain, cosine, sine, *adapters)
    outs = (struct(tokens.shape, bf16), turned_terms(own.shape[1], columns, ranks))
    return pl.pallas_call(
        functools.partial(output_kernel, first),
        grid_spec=pltpu.PrefetchScalarGridSpec(
            num_scalar_prefetch=3,
            grid=(slots,),
            in_specs=[anywhere, anywhere] + [by_slot(r) for r in rows] + [whole(a) for a in shared],
            out_specs=[by_slot(outs[0]), whole(outs[1])],
            scratch_shapes=[pltpu.VMEM((ranks, columns), f32)]
            + buffers(own, (kv_rows, kv_rows), width),
        ),
        out_shape=outs,
        compiler_params=params(),
        cost_estimate=cost(3 * slots * block * width * kv_columns, 30e6),
        name="output_side",
    )(adapter_of, live, core, own, other, *rows, *shared)


def hop_up(array, t, line):
    half = line // 2
    return along_line(array, [(z, z - 1) for z in range(1, line) if half <= z + t - 1 < line])


def hops_down(mine, line):
    half = line // 2
    moved = [mine]
    for t in range(1, half):
        pairs = [(z, z + 1) for z in range(line - 1) if half <= z - t + 1]
        moved.append(along_line(moved[-1], pairs))
    return moved


def prompt_blocks(from_above, from_below, place, line):
    half = line // 2
    mine = from_above[0]
    blocks = []
    for b in range(half, line):
        out = mine
        for z in range(line):
            if z < b:
                out = jnp.where(place == z, from_above[b - z], out)
            elif z > b:
                out = jnp.where(place == z, from_below[z - b], out)
        blocks.append(out)
    return jnp.stack(blocks)


def take(blocks, at):
    return lax.dynamic_index_in_dim(blocks, jnp.clip(at, 0, blocks.shape[0] - 1), 0, False)


def fold_blocks(parts, line):
    half = line // 2
    return [along_line(parts, [(z, half - 1)]) for z in range(half - 1)]


def return_blocks(parts, total, place, line):
    half = line // 2
    came = []
    for b in range(half, line):
        came.append(along_line(total[b - half], [(half - 1, b)]))
    for by in range(1, half):
        pairs = [(z, z - by) for z in range(half + by, line)]
        came.append(along_line(take(parts, place - by - half), pairs))
    return came


def owned_blocks(parts, came, place, line):
    half = line // 2
    total = functools.reduce(jnp.add, [c.astype(f32) for c in came])
    total = total + take(parts, place - half).astype(f32)
    return jnp.where(place >= half, total, 0.0)


def finish_kernel(places, segments, core, own, other, *refs):
    count = len(places)
    outs, buffers, sems = refs[:count], refs[count : 2 * count], refs[2 * count]
    shards, line, rows, _ = own.shape
    copies = []
    for side, half in ((core[0], own), (1 - core[0], other)):
        for at, n, to, offset in segments:
            while n:
                w, row = at // rows, at % rows
                take = min(n, rows - row)
                for z in range(line):
                    start = pl.multiple_of((2 * z + side) * places[to] + offset, 16)
                    copies.append(
                        pltpu.make_async_copy(
                            half.at[w, z, pl.ds(row, take), :],
                            buffers[to].at[pl.ds(start, take), :],
                            sems.at[len(copies)],
                        )
                    )
                at, n, offset = at + take, n - take, offset + take
    for c in copies:
        c.start()
    for c in copies:
        c.wait()
    for out, buffer in zip(outs, buffers):
        total = buffer.shape[0]
        step = next(d for d in (1280, 768, 256) if total % d == 0)
        for at in range(0, total, step):
            block = buffer[at : at + step, :].astype(f32).T
            out[:, :, at : at + step] = block.reshape(out.shape[:2] + (step,))


def finish(core, own, other, places, segments):
    shards, line, rows, ranks = own.shape
    outs = [struct((ranks // RANK, RANK, 2 * line * p), f32) for p in places]
    pieces = 0
    for at, n, _, _ in segments:
        pieces += (at + n - 1) // rows - at // rows + 1
    return pl.pallas_call(
        functools.partial(finish_kernel, places, segments),
        grid_spec=pltpu.PrefetchScalarGridSpec(
            num_scalar_prefetch=1,
            grid=(1,),
            in_specs=[anywhere, anywhere],
            out_specs=[whole(o) for o in outs],
            scratch_shapes=[pltpu.VMEM((2 * line * p, ranks), bf16) for p in places]
            + [pltpu.SemaphoreType.DMA((2 * line * pieces,))],
        ),
        out_shape=outs,
        compiler_params=params(),
        name="finish",
    )(core, own, other)


def split_rows(mine, shards):
    n = mine.shape[1]
    padded = jnp.pad(mine, ((0, 0), (0, -n % (16 * shards)), (0, 0)))
    return padded.reshape(mine.shape[0], shards, -1, mine.shape[2])


def late_segments(rows, pitch, shift, counts, first):
    segments, at = [], 0
    for i, n in enumerate(counts):
        done = 0
        while done < n:
            w, row = (at + done) // rows, (at + done) % rows
            take = min(n - done, rows - row)
            segments.append((w * pitch + shift + row, take, first + i, done))
            done += take
        at += n
    return segments


def pack_kernel(spans, core, gate, up, down, given, *outs):
    kept = down[core[0]]
    came = given[...]
    first = jnp.where(core[0] == 0, kept, came)
    second = jnp.where(core[0] == 0, came, kept)
    turned = (gate[...].T, up[...].T, jnp.concatenate([first, second], axis=1))
    for out, (at, n) in zip(outs, spans):
        for i, t in enumerate(turned):
            out[i * n : (i + 1) * n, :] = t[at : at + n]


def pack_weights(spans, core, gate, up, down, given):
    outs = [struct((3 * n, gate.shape[0]), bf16) for _, n in spans]
    return pl.pallas_call(
        functools.partial(pack_kernel, spans),
        grid_spec=pltpu.PrefetchScalarGridSpec(
            num_scalar_prefetch=1,
            grid=(1,),
            in_specs=[whole(a) for a in (gate, up, down, given)],
            out_specs=[whole(o) for o in outs],
        ),
        out_shape=outs,
        compiler_params=params(),
        cost_estimate=cost(0, 12e6),
        name="pack_weights",
    )(core, gate, up, down, given)


def order_kernel(spans, line, wide, *outs):
    scratch = outs[-1]
    hidden = wide.shape[1]
    step = next(d for d in (1280, 256) if hidden % d == 0)
    for at in range(0, hidden, step):
        scratch[at : at + step, :] = wide[:, at : at + step].T
    shard = hidden // (2 * line)
    for out, (at, n) in zip(outs, spans):
        for z in range(line):
            for side in (0, 1):
                start = (2 * z + side) * shard + at
                out[side, z * n : (z + 1) * n, :] = scratch[start : start + n, :]


def order_adapters(spans, line, wide):
    ranks, hidden = wide.shape
    outs = [struct((2, line * n, ranks), bf16) for _, n in spans]
    return pl.pallas_call(
        functools.partial(order_kernel, spans, line),
        out_shape=outs,
        scratch_shapes=[pltpu.VMEM((hidden, ranks), bf16)],
        compiler_params=pltpu.CompilerParams(vmem_limit_bytes=VMEM_LIMIT),
        cost_estimate=cost(0, 5e6),
        name="order_adapters",
    )(wide)


def local(
    tokens,
    cotangent,
    group_slot,
    group_adapter,
    attn_gain,
    mlp_gain,
    w_query,
    w_key,
    w_value,
    w_output,
    w_gate,
    w_up,
    w_down,
    query_bias,
    key_bias,
    value_bias,
    adapt_query_in,
    adapt_query_out,
    adapt_key_in,
    adapt_key_out,
    adapt_value_in,
    adapt_value_out,
    adapt_output_in,
    adapt_output_out,
    adapt_gate_in,
    adapt_gate_out,
    adapt_up_in,
    adapt_up_out,
    adapt_down_in,
    adapt_down_out,
):
    slots, block, width = tokens.shape
    ctx_size, shards = lax.axis_size("ctx"), lax.axis_size("wsh")
    line = ctx_size // 2
    ctx_place, shard_place = lax.axis_index("ctx"), lax.axis_index("wsh")
    place, core = ctx_place // 2, ctx_place % 2
    kv_width = key_bias.shape[0]
    kv_heads = kv_width // HEAD_DIM
    hidden = adapt_gate_out.shape[-1]
    if line != shards or (CONTS * CONT) != line * block or CONT // block > 2:
        raise ValueError("unsupported mesh")
    mates = CONT // block - 1

    slot_ids = shard_place * slots + jnp.arange(slots, dtype=jnp.int32)
    matches = group_slot[None, :] == slot_ids[:, None]
    live = jnp.any(matches, axis=1).astype(jnp.int32)
    adapter_of = jnp.sum(jnp.where(matches, group_adapter[None, :], 0), axis=1).astype(jnp.int32)
    index = ctx_place * block + jnp.arange(block, dtype=jnp.int32)
    position = jnp.where(index >= CONTS * CONT, index - CONTS * CONT, PROMPT + index % CONT)
    frequency = rope_base ** (-(jnp.arange(HEAD_DIM // 2, dtype=f32) * 2.0) / HEAD_DIM)
    angles = position.astype(f32)[:, None] * frequency[None, :]
    cosine = jnp.concatenate([jnp.cos(angles), jnp.cos(angles)], axis=-1)
    sine = jnp.concatenate([-jnp.sin(angles), jnp.sin(angles)], axis=-1)

    is_cont = ctx_place < line
    of_side = [2 * (line // 2 + i) + core for i in range(line // 2)]
    of_other = [2 * (line // 2 + i) + 1 - core for i in range(line // 2)]
    flags = [(is_cont | (b < ctx_place)) for b in of_side + of_other]
    flags += [is_cont & (core == 1)] if mates else []
    flags = jnp.stack(flags).astype(jnp.int32)

    def wide(half):
        if half.shape[-1] % 128 == 0:
            return half
        return jnp.transpose(half, (1, 2, 0, 3)).reshape(1, line, half.shape[2], width)

    def wide_feed(half):
        if half.shape[-1] % 128 == 0:
            return half
        split = half.shape[2] // 3 * 2
        out_in = jnp.transpose(half[:, :, :split], (1, 2, 0, 3)).reshape(1, line, split, width)
        in_out = jnp.transpose(half[:, :, split:], (0, 2, 1, 3)).reshape(1, line, split // 2, width)
        return jnp.concatenate([out_in, in_out], axis=2)

    q_rows = w_query.shape[1]
    o_at = q_rows
    kv_piece = jnp.concatenate([w_key.T, w_value.T], axis=0)
    qo_piece = jnp.concatenate([w_query.T, w_output.T], axis=0)
    kv_moves = line_moves(kv_piece, line)
    qo_moves = line_moves(qo_piece, line)

    shard_hidden = w_gate.shape[1]
    unit = shard_hidden // 35
    part_rows = [5 * unit, 8 * unit, 8 * unit, 8 * unit, 6 * unit]
    part_at = [sum(part_rows[:i]) for i in range(len(part_rows))]
    parts = len(part_rows)
    spans = list(zip(part_at, part_rows))
    core_place = core.astype(jnp.int32)[None]
    down_halves = w_down.reshape(2, shard_hidden, w_down.shape[1])
    given = swap_cores(lax.dynamic_index_in_dim(down_halves, 1 - core, 0, False))
    pieces = pack_weights(spans, core_place, w_gate, w_up, down_halves, given)
    pieces = list(pieces)

    lined_kv = in_order(kv_piece, hold(kv_moves, pieces[0]), place, line)
    down_in, gate_out, up_out = (
        order_adapters(spans, line, a.reshape(-1, a.shape[-1]))
        for a in (adapt_down_in, adapt_gate_out, adapt_up_out)
    )
    kv_half = gather_wsh(lined_kv, shard_place)
    kv_own, kv_other = wide(kv_half), wide(swap_cores(kv_half))
    lined_qo = in_order(qo_piece, qo_moves, place, line)
    qo_half = shard_gather(lined_qo)

    def flat(adapters):
        return adapters.reshape(-1, adapters.shape[-1])

    query_in, key_in, value_in, output_in, gate_in, up_in = (
        flat(a)
        for a in (adapt_query_in, adapt_key_in, adapt_value_in, adapt_output_in, adapt_gate_in, adapt_up_in)
    )
    query_out, key_out, value_out, output_out, down_out = (
        flat(a)
        for a in (adapt_query_out, adapt_key_out, adapt_value_out, adapt_output_out, adapt_down_out)
    )

    gain_one = attn_gain.astype(f32)[None, :]
    gain_two = mlp_gain.astype(f32)[None, :]
    q_bias = query_bias.astype(f32)[None, :]
    kv_bias = jnp.concatenate([key_bias, value_bias]).astype(f32)[None, :]

    lined, halves = [], []

    def take_in(moves, group, *after):
        moves, at = hold(moves, *after), 0
        for i in group:
            n = pieces[i].shape[0]
            came = [m[at : at + n] for m in moves]
            lined.append(in_order(pieces[i], came, place, line))
            halves.append(shard_gather(lined[-1]))
            at += n

    def set_out(group, *after):
        together = hold([pieces[i] for i in group], *after)
        piece = jnp.concatenate(together, axis=0) if len(group) > 1 else together[0]
        return piece, line_moves(piece, line)

    _, moves = set_out([0], lined_qo)
    attn_kv = (core_place, kv_own, kv_other)
    kv_adapters = (key_in, value_in, key_out, value_out)
    normed, rank_k, rank_v, key_value = key_value_side(
        adapter_of, *attn_kv, 0, tokens, gain_one, kv_bias, kv_adapters, cosine, sine
    )
    hops = [key_value, hop_up(key_value, 1, line)]
    below = hops_down(key_value, line)
    mate = (swap_cores(key_value),) if mates else ()
    hops.append(hop_up(hops[1], 2, line))
    for t in range(3, line):
        hops.append(hop_up(hops[-1], t, line))
    take_in(moves, [0], key_value, *down_in, *gate_out, *up_out)
    _, moves = set_out([1], lined[0])
    take_in(moves, [1], tip(hops[2]))
    _, moves = set_out([2], lined[1])
    (qo_half,) = hold([qo_half], tip(hops[2]))
    attn = (core_place, wide(qo_half), wide(swap_cores(qo_half)))
    rank_q, queries = query_side(
        adapter_of, *attn, normed, q_bias, (query_in, query_out), cosine, sine
    )
    side = prompt_blocks(hops, below, place, line)
    other_side = swap_cores(side)
    (queries,) = hold([queries], lined[1])
    context, mixed, logs = attend(flags, queries, key_value, side, other_side, mate, kv_heads)
    take_in(moves, [2], context)
    _, moves = set_out([3], lined[2])
    (context,) = hold([context], lined[2])
    mid, normed2, grad_out, rank_o, rank_g, rank_u, rank_d = middle_side(
        adapter_of, live, *attn, o_at, context, tokens, cotangent, output_in, output_out, gain_two,
        gate_in, up_in, down_out,
    )

    sums, own_terms, other_terms, others = None, [], [], []
    before = normed2
    for i in range(parts + 1):
        if 0 < i < 3:
            take_in(moves, [i + 2], before)
            if i + 3 < parts:
                _, moves = set_out([i + 3], lined[i + 2])
        if i < parts:
            (halves[i],) = hold([halves[i]], before, lined[-1])
            others.append(swap_cores(halves[i]))
        use = []
        if i < parts:
            use.append((wide_feed(halves[i]), False, (down_in[i], gate_out[i], up_out[i])))
        if i:
            j = i - 1
            use.append((wide_feed(others[j]), True, (down_in[j], gate_out[j], up_out[j])))
        done = feed_part(core_place, use, normed2, grad_out, (rank_d, rank_g, rank_u), sums)
        sums, terms = done[:5], done[5:]
        if i < parts:
            own_terms.append(terms[0])
        if i:
            other_terms.append(terms[-1])
        before = sums[2]
    early_keep = jnp.concatenate(own_terms, axis=1)
    early_came = swap_cores(jnp.concatenate(other_terms, axis=1))
    layer_out, d_mid, d_context, terms = return_side(
        adapter_of, live, *attn, o_at, sums, mid, normed2, grad_out, context, rank_o,
        output_in, output_out, gain_two, gate_in, up_in, down_out,
    )

    first_half = slots // 2

    def slots_back(start, count, d_context, d_query=None):
        return attend_back(
            flags, queries, key_value, side, other_side, mate, d_context, mixed, logs, cosine, sine,
            kv_heads, start, count, d_query,
        )

    (early_came,) = hold([early_came], d_context)
    early = split_rows(add_up([early_keep, early_came]), shards)
    early_outs = wsh_outs(early, shard_place)
    late_keep, late_give = terms[0], terms[1]
    (d_context, late_give) = hold([d_context, late_give], *early_outs)
    early_moves = wsh_send(early_outs)
    late_came = swap_cores(late_give)
    back = [slots_back(0, first_half, d_context)]
    sides = [add_up([back[0][2], swap_cores(back[0][3])])]
    late_came, *early_moves = hold([late_came, *early_moves], back[0][1])
    late = split_rows(add_up([late_keep, late_came]), shards)
    late_outs = wsh_outs(late, shard_place)
    early = wsh_sum(early, shard_place, early_moves)
    early_outs = line_outs(early, place, line)
    (d_context,) = hold([d_context], sides[0], *late_outs, *early_outs)
    folded = [fold_blocks(sides[0], line)]
    late_moves = wsh_send(late_outs)
    early_moves = line_send(early_outs, line)
    back.append(slots_back(first_half, slots - first_half, d_context, back[0][0]))
    swapped = swap_cores(back[1][3])
    *late_moves, late = hold([*late_moves, late], back[1][1])
    folded[0] = hold(folded[0], back[1][1]) if folded[0] else []
    sides.append(add_up([back[1][2], swapped]))
    total = add_up([sides[0]] + folded[0])
    late = wsh_sum(late, shard_place, late_moves)
    late_outs = line_outs(late, place, line)
    early_terms = line_sum(early, place, hold(early_moves, back[1][1]))
    (d_query,) = hold([back[1][0]], sides[1], total, *late_outs, early_terms)
    folded.append(fold_blocks(sides[1], line))
    came = [return_blocks(sides[0], total, place, line)]
    late_moves = line_send(late_outs, line)
    early_moves = line_moves(early_terms, line)
    d_normed_q, query_terms = query_back_side(
        adapter_of, *attn, d_query, normed, rank_q, query_in, query_out
    )
    folded[1] = hold(folded[1], query_terms) if folded[1] else []
    total = add_up([sides[1]] + folded[1])
    came.append(return_blocks(sides[1], total, place, line))
    early_lined = in_order(early_terms, hold(early_moves, query_terms, tip(total)), place, line)
    early_half = shard_gather(early_lined)
    came[0] = hold(came[0], query_terms)
    d_kv = jnp.concatenate(
        [b[1] + owned_blocks(p, c, place, line) for b, p, c in zip(back, sides, came)], axis=0
    )
    if mates:
        d_kv = d_kv + swap_cores(jnp.concatenate([b[4] for b in back], axis=0)).astype(f32)
    late_terms = line_sum(late, place, hold(late_moves, query_terms, tip(total)))
    (d_kv,) = hold([d_kv], early_lined)
    input_grad, kv_terms = output_side(
        adapter_of, live, *attn_kv, 0, d_kv, d_normed_q, d_mid, normed, rank_k, rank_v, tokens, gain_one,
        cosine, sine, kv_adapters,
    )

    width_rows = width // (2 * line)
    last_keep = jnp.concatenate([query_terms[0], kv_terms[0]], axis=1)
    last_came = swap_cores(jnp.concatenate([query_terms[1], kv_terms[1]], axis=1))
    last = split_rows(add_up([last_keep, last_came]), shards)
    moves = wsh_send(wsh_outs(last, shard_place))
    last = wsh_sum(last, shard_place, moves)
    moves = line_send(line_outs(last, place, line), line)
    (early_half,) = hold([early_half], tip(last))
    early_other = swap_cores(early_half)
    last_terms = line_sum(last, place, moves)
    last_terms = jnp.concatenate([late_terms, last_terms], axis=0)
    last_lined = in_order(last_terms, line_moves(last_terms, line), place, line)
    last_own = gather_wsh(last_lined, shard_place)
    last_other = swap_cores(last_own)
    segments = [
        (3 * at + i * n, n, i, at) for at, n in spans for i in range(3)
    ]
    g_gate_out, g_up_out, g_down_in = finish(
        core_place, early_half, early_other, (shard_hidden,) * 3, segments
    )
    kv_rows = kv_width // (2 * line)
    segments = late_segments(late_terms.shape[0], last_terms.shape[0], 0, (width_rows,) * 5, 0)
    segments += late_segments(
        last_terms.shape[0] - late_terms.shape[0], last_terms.shape[0], late_terms.shape[0],
        (width_rows,) * 4 + (kv_rows,) * 2, 5,
    )
    (
        g_output_in, g_output_out, g_gate_in, g_up_in, g_down_out,
        g_query_in, g_query_out, g_key_in, g_value_in, g_key_out, g_value_out,
    ) = finish(
        core_place, last_own, last_other, (width_rows,) * 9 + (kv_rows,) * 2, segments
    )
    return (
        layer_out,
        input_grad,
        g_query_in,
        g_query_out,
        g_key_in,
        g_key_out,
        g_value_in,
        g_value_out,
        g_output_in,
        g_output_out,
        g_gate_in,
        g_gate_out,
        g_up_in,
        g_up_out,
        g_down_in,
        g_down_out,
    )


def solution(mesh):
    weight = P("wsh", "ctx")
    rows = P("wsh", "ctx", None)
    return jax.shard_map(
        local,
        mesh=mesh,
        in_specs=(rows, rows) + (P(),) * 4 + (weight,) * 7 + (P(),) * 17,
        out_specs=(rows, rows) + (P(),) * 14,
        check_vma=False,
    )
```

```python
import functools
import math

import jax
import jax.numpy as jnp
from jax import lax
from jax.experimental import pallas as pl
from jax.experimental.pallas import tpu as pltpu
from jax.sharding import PartitionSpec as P

HEAD_DIM = 128
PROMPT = 1024
CONTS = 4
CONT = 256
RANK = 16

norm_eps = 1e-06
adapter_scale = 0.5
rope_base = 1000000.0
masked_score = -1e30
score_scale = HEAD_DIM ** (-0.5)
score_to_log2 = score_scale * math.log2(math.e)

f32 = jnp.float32
bf16 = jnp.bfloat16
VMEM_LIMIT = 60 * 2**20


def nt(left, right):
    return lax.dot_general(left, right, (((1,), (1,)), ((), ())), preferred_element_type=f32)


def nn(left, right):
    return lax.dot_general(left, right, (((1,), (0,)), ((), ())), preferred_element_type=f32)


def tn(left, right):
    return lax.dot_general(left, right, (((0,), (0,)), ((), ())), preferred_element_type=f32)


def along_line(array, pairs):
    return lax.ppermute(array, "ctx", [(2 * a + c, 2 * b + c) for a, b in pairs for c in (0, 1)])


def swap_cores(array):
    size = lax.axis_size("ctx")
    return lax.ppermute(array, "ctx", [(i, i ^ 1) for i in range(size)])


def hold_kernel(*refs):
    pass


def hold(arrays, *after):
    anywhere = pl.BlockSpec(memory_space=pl.ANY)
    count = len(arrays)
    held = pl.pallas_call(
        hold_kernel,
        in_specs=[anywhere] * (count + len(after)),
        out_specs=[anywhere] * count,
        out_shape=[jax.ShapeDtypeStruct(a.shape, a.dtype) for a in arrays],
        input_output_aliases={i: i for i in range(count)},
        name="hold",
    )(*arrays, *after)
    return list(held)


def line_moves(piece, line):
    return [
        along_line(piece, [(i, (i + by) % line) for i in range(line)]) for by in range(1, line)
    ]


def in_order(piece, came, place, line):
    out = jnp.zeros((line,) + piece.shape, piece.dtype)
    out = lax.dynamic_update_index_in_dim(out, piece, place, 0)
    for by in range(1, line):
        out = lax.dynamic_update_index_in_dim(out, came[by - 1], (place - by) % line, 0)
    return out


def shard_gather(lined):
    return lax.all_gather(lined, "wsh", axis=0, tiled=False)


def add_up(arrays):
    return functools.reduce(jnp.add, [a.astype(f32) for a in arrays]).astype(bf16)


def line_outs(mine, place, line):
    return [
        lax.dynamic_index_in_dim(mine, (place + by) % line, 0, False) for by in range(1, line)
    ]


def line_send(outs, line):
    return [
        along_line(out, [(i, (i + by + 1) % line) for i in range(line)]) for by, out in enumerate(outs)
    ]


def line_sum(mine, place, came):
    return add_up([lax.dynamic_index_in_dim(mine, place, 0, False)] + came)


def across(array, by):
    size = lax.axis_size("wsh")
    return lax.ppermute(array, "wsh", [(i, i ^ by) for i in range(size)])


def wsh_outs(parts, shard):
    return [
        lax.dynamic_index_in_dim(parts, shard ^ by, 1, False) for by in range(1, parts.shape[1])
    ]


def wsh_send(outs):
    return [across(out, by + 1) for by, out in enumerate(outs)]


def wsh_sum(parts, shard, came):
    return add_up([lax.dynamic_index_in_dim(parts, shard, 1, False)] + came)


def tip(array):
    ends = (1,) * (array.ndim - 2) + (min(16, array.shape[-2]), min(128, array.shape[-1]))
    return lax.slice(array, (0,) * array.ndim, ends)


def gather_wsh(piece, shard, after=()):
    shards = lax.axis_size("wsh")
    came = [across(piece, by) for by in range(1, shards)]
    came = hold(came, *after) if after else came
    out = jnp.zeros((shards,) + piece.shape, piece.dtype)
    out = lax.dynamic_update_index_in_dim(out, piece, shard, 0)
    for by in range(1, shards):
        out = lax.dynamic_update_index_in_dim(out, came[by - 1], shard ^ by, 0)
    return out


def both_cores(half, other, core):
    return jnp.stack([jnp.where(core == 0, half, other), jnp.where(core == 0, other, half)])


def params(**more):
    return pltpu.CompilerParams(
        dimension_semantics=("arbitrary",), vmem_limit_bytes=VMEM_LIMIT, **more
    )


def whole(array):
    return pl.BlockSpec(array.shape, lambda s, *pre: (0,) * array.ndim)


def by_slot(array):
    return pl.BlockSpec((1,) + array.shape[1:], lambda s, *pre: (s,) + (0,) * (array.ndim - 1))


def second_by_slot(array):
    return pl.BlockSpec(
        (array.shape[0], 1) + array.shape[2:], lambda s, *pre: (0, s) + (0,) * (array.ndim - 2)
    )


def half_copies(core, own, other, parts, sems):
    copies = []
    shards, _, _, cols = own.shape
    for side, half in ((core, own), (1 - core, other)):
        for w in range(shards):
            for at, count, buffer in parts:
                copies.append(
                    pltpu.make_async_copy(
                        half.at[w, :, pl.ds(at, count), :],
                        buffer.at[:, side, :, pl.ds(w * cols, cols)],
                        sems.at[len(copies)],
                    )
                )
    return copies


def fetch_once(copies):
    @pl.when(pl.program_id(0) == 0)
    def _():
        for c in copies:
            c.start()
        for c in copies:
            c.wait()


def buffers(own, rows, width):
    line, shards = own.shape[1], own.shape[0]
    held = [pltpu.VMEM((line, 2, n, width), bf16) for n in rows]
    return held + [pltpu.SemaphoreType.DMA((2 * shards * len(rows),))]


def as_matrix(buffer):
    return buffer[...].reshape(-1, buffer.shape[-1])


anywhere = pl.BlockSpec(memory_space=pl.ANY)


def cost(flops, bytes_accessed, exps=0):
    return pl.CostEstimate(flops=int(flops), bytes_accessed=int(bytes_accessed), transcendentals=int(exps))


def slot_lanes(adapter, block, ranks):
    lane = lax.broadcasted_iota(jnp.int32, (block, ranks), 1)
    return lane // RANK == adapter[pl.program_id(0)]


def picked(mask, values):
    return jnp.where(mask, values, 0.0).astype(bf16)


def struct(shape, dtype):
    return jax.ShapeDtypeStruct(shape, dtype)


def turn(u, cos, sin):
    return u * cos + pltpu.roll(u, HEAD_DIM // 2, 1) * sin


def turn_back(u, cos, sin):
    return u * cos - pltpu.roll(u, HEAD_DIM // 2, 1) * sin


def key_value_kernel(
    first, adapter, core, own, other, tok, gain, bias, in_k, in_v, out_k, out_v, cosine, sine,
    normed_ref, rank_k_ref, rank_v_ref, kv_ref, key_w, value_w, sems,
):
    rows = key_w.shape[2]
    parts = ((first, rows, key_w), (first + rows, rows, value_w))
    fetch_once(half_copies(core[0], own, other, parts, sems))
    hidden = tok[0].astype(f32)
    inverse = lax.rsqrt(jnp.mean(hidden * hidden, axis=-1, keepdims=True) + norm_eps)
    normed = (hidden * inverse * gain[...]).astype(bf16)
    normed_ref[0] = normed
    mask = slot_lanes(adapter, normed.shape[0], in_k.shape[0])
    kv_width = kv_ref.shape[-1] // 2
    rank_k = picked(mask, nt(normed, in_k[...]))
    rank_v = picked(mask, nt(normed, in_v[...]))
    rank_k_ref[0], rank_v_ref[0] = rank_k, rank_v
    lin_k = nt(normed, as_matrix(key_w)) + bias[:, :kv_width]
    lin_v = nt(normed, as_matrix(value_w)) + bias[:, kv_width:]
    key = lin_k + adapter_scale * nn(rank_k, out_k[...])
    value = lin_v + adapter_scale * nn(rank_v, out_v[...])
    cos, sin = cosine[...], sine[...]
    for h in range(kv_width // HEAD_DIM):
        part = slice(h * HEAD_DIM, (h + 1) * HEAD_DIM)
        kv_ref[0, :, part] = turn(key[:, part], cos, sin).astype(bf16)
    kv_ref[0, :, kv_width:] = value.astype(bf16)


def key_value_side(adapter_of, core, own, other, first, tokens, gain, bias, adapters, cosine, sine):
    slots, block, width = tokens.shape
    kv_rows = bias.shape[1] // 4 // own.shape[1]
    shared = (gain, bias, *adapters, cosine, sine)
    ranks = struct((slots, block, adapters[0].shape[0]), bf16)
    outs = (struct(tokens.shape, bf16), ranks, ranks, struct((slots, block, bias.shape[1]), bf16))
    return pl.pallas_call(
        functools.partial(key_value_kernel, first),
        grid_spec=pltpu.PrefetchScalarGridSpec(
            num_scalar_prefetch=2,
            grid=(slots,),
            in_specs=[anywhere, anywhere, by_slot(tokens)] + [whole(a) for a in shared],
            out_specs=[by_slot(o) for o in outs],
            scratch_shapes=buffers(own, (kv_rows, kv_rows), width),
        ),
        out_shape=outs,
        compiler_params=params(),
        cost_estimate=cost(3 * slots * block * width * bias.shape[1], 12e6),
        name="key_value_side",
    )(adapter_of, core, own, other, tokens, *shared)


def query_kernel(
    adapter, core, own, other, normed, bias, in_q, out_q, cosine, sine, rank_ref, query_ref, weight, sems
):
    fetch_once(half_copies(core[0], own, other, ((0, weight.shape[2], weight),), sems))
    x = normed[0]
    mask = slot_lanes(adapter, x.shape[0], in_q.shape[0])
    rank = picked(mask, nt(x, in_q[...]))
    rank_ref[0] = rank
    query = nt(x, as_matrix(weight)) + bias[...] + adapter_scale * nn(rank, out_q[...])
    cos, sin = cosine[...], sine[...]
    for h in range(query.shape[1] // HEAD_DIM):
        part = slice(h * HEAD_DIM, (h + 1) * HEAD_DIM)
        query_ref[0, :, part] = turn(query[:, part], cos, sin).astype(bf16)


def query_side(adapter_of, core, own, other, normed, bias, adapters, cosine, sine):
    slots, block, width = normed.shape
    shared = (bias, *adapters, cosine, sine)
    outs = (struct((slots, block, adapters[0].shape[0]), bf16), struct(normed.shape, bf16))
    return pl.pallas_call(
        query_kernel,
        grid_spec=pltpu.PrefetchScalarGridSpec(
            num_scalar_prefetch=2,
            grid=(slots,),
            in_specs=[anywhere, anywhere, by_slot(normed)] + [whole(a) for a in shared],
            out_specs=[by_slot(o) for o in outs],
            scratch_shapes=buffers(own, (width // 2 // own.shape[1],), width),
        ),
        out_shape=outs,
        compiler_params=params(),
        cost_estimate=cost(2.5 * slots * block * width * width, 12e6),
        name="query_side",
    )(adapter_of, core, own, other, normed, *shared)


def attend_kernel(kv_heads, group, mates, flags, *refs):
    query, own, even, odd = refs[:4]
    mate = refs[4] if mates else None
    context_ref, mixed_ref, log_ref = refs[4 + mates :]
    block = query.shape[1]
    half = even.shape[0]
    kv_width = kv_heads * HEAD_DIM
    rows = lax.broadcasted_iota(jnp.int32, (block, block), 0)
    cols = lax.broadcasted_iota(jnp.int32, (block, block), 1)
    causal = rows <= cols
    bias = [jnp.where(flags[i] != 0, 0.0, masked_score) for i in range(2 * half + mates)]
    for kv in range(kv_heads):
        k_part = slice(kv * HEAD_DIM, (kv + 1) * HEAD_DIM)
        v_part = slice(kv_width + kv * HEAD_DIM, kv_width + (kv + 1) * HEAD_DIM)
        sources = [own[0]] + [even[i, 0] for i in range(half)] + [odd[i, 0] for i in range(half)]
        sources += [mate[0]] if mates else []
        keys = [s[:, k_part] for s in sources]
        values_t = [s[:, v_part].T for s in sources]
        for g in range(group):
            h = kv * group + g
            part = slice(h * HEAD_DIM, (h + 1) * HEAD_DIM)
            q = query[0, :, part]
            scores = [nt(k, q) for k in keys]
            scores[0] = jnp.where(causal, scores[0], masked_score)
            scores = scores[:1] + [s + b for s, b in zip(scores[1:], bias)]
            top = functools.reduce(jnp.maximum, [jnp.max(s, axis=0, keepdims=True) for s in scores])
            shift = top * score_to_log2
            total, mixed = 0.0, 0.0
            for s, v in zip(scores, values_t):
                p = jnp.exp2(s * score_to_log2 - shift)
                total = total + jnp.sum(p, axis=0, keepdims=True)
                mixed = mixed + nn(v, p.astype(bf16))
            mixed = mixed / total
            mixed_ref[0, h] = mixed
            log_ref[0, h : h + 1, :] = shift + jnp.log2(total)
            context_ref[0, :, part] = mixed.T.astype(bf16)


def attend(flags, query, own, even, odd, mate, kv_heads):
    slots, block, width = query.shape
    heads = width // HEAD_DIM
    mates = len(mate)
    operands = (query, own, even, odd, *mate)
    specs = [by_slot(query), by_slot(own), second_by_slot(even), second_by_slot(odd)]
    specs += [by_slot(m) for m in mate]
    outs = (
        struct((slots, block, width), bf16),
        struct((slots, heads, HEAD_DIM, block), f32),
        struct((slots, heads, block), f32),
    )
    return pl.pallas_call(
        functools.partial(attend_kernel, kv_heads, heads // kv_heads, mates),
        grid_spec=pltpu.PrefetchScalarGridSpec(
            num_scalar_prefetch=1, grid=(slots,), in_specs=specs, out_specs=[by_slot(o) for o in outs]
        ),
        out_shape=outs,
        compiler_params=params(),
        cost_estimate=cost(20e9, 20e6, slots * heads * block * (own.shape[1] * 5)),
        name="attend",
    )(flags, *operands)


def attend_back_kernel(kv_heads, group, mates, more, flags, *refs):
    refs = refs[more:]
    query, own, even, odd = refs[:4]
    mate = refs[4] if mates else None
    grad, mixed_ref, log_ref, cosine, sine = refs[4 + mates : 9 + mates]
    d_query, d_own, d_even, d_odd = refs[9 + mates : 13 + mates]
    d_mate = refs[13 + mates] if mates else None
    acc = refs[13 + 2 * mates]
    block = query.shape[1]
    half = even.shape[0]
    kv_width = kv_heads * HEAD_DIM
    rows = lax.broadcasted_iota(jnp.int32, (block, block), 0)
    cols = lax.broadcasted_iota(jnp.int32, (block, block), 1)
    causal = rows <= cols
    bias = [jnp.where(flags[i] != 0, 0.0, masked_score) for i in range(2 * half + mates)]
    cos, sin = cosine[...], sine[...]
    for kv in range(kv_heads):
        k_part = slice(kv * HEAD_DIM, (kv + 1) * HEAD_DIM)
        v_part = slice(kv_width + kv * HEAD_DIM, kv_width + (kv + 1) * HEAD_DIM)
        sources = [own[0]] + [even[i, 0] for i in range(half)] + [odd[i, 0] for i in range(half)]
        sources += [mate[0]] if mates else []
        keys = [s[:, k_part] for s in sources]
        keys_t = [k.T for k in keys]
        values = [s[:, v_part] for s in sources]
        for g in range(group):
            h = kv * group + g
            part = slice(h * HEAD_DIM, (h + 1) * HEAD_DIM)
            q = query[0, :, part]
            d_o = grad[0, :, part]
            delta = jnp.sum(d_o.astype(f32).T * mixed_ref[0, h], axis=0, keepdims=True)
            shift = log_ref[0, h : h + 1, :]
            d_q = 0.0
            for i in range(len(sources)):
                s = nt(keys[i], q)
                s = jnp.where(causal, s, masked_score) if i == 0 else s + bias[i - 1]
                p = jnp.exp2(s * score_to_log2 - shift)
                d_p = nt(values[i], d_o)
                d_s = (p * (d_p - delta)).astype(bf16)
                d_value = nn(p.astype(bf16), d_o)
                d_key = nn(d_s, q)
                if g == 0:
                    acc[i, :, v_part] = d_value
                    acc[i, :, k_part] = d_key
                else:
                    acc[i, :, v_part] += d_value
                    acc[i, :, k_part] += d_key
                d_q = d_q + nn(keys_t[i], d_s)
            u = d_q.T * score_scale
            d_query[0, :, part] = (u * cos - pltpu.roll(u, HEAD_DIM // 2, 1) * sin).astype(bf16)
    targets = [(d_own, 0)] + [(d_even, i) for i in range(half)] + [(d_odd, i) for i in range(half)]
    targets += [(d_mate, 0)] if mates else []
    for i, (target, j) in enumerate(targets):
        if target is d_own or target is d_mate:
            target[0, :, :kv_width] = (acc[i, :, :kv_width] * score_scale).astype(target.dtype)
            target[0, :, kv_width:] = acc[i, :, kv_width:].astype(target.dtype)
        else:
            target[j, 0, :, :kv_width] = (acc[i, :, :kv_width] * score_scale).astype(target.dtype)
            target[j, 0, :, kv_width:] = acc[i, :, kv_width:].astype(target.dtype)


def attend_back(flags, query, own, even, odd, mate, grad, mixed, logs, cosine, sine, kv_heads, start, slots, d_query=None):
    _, block, width = query.shape

    def by_slot(array):
        lead = array.ndim - 1
        return pl.BlockSpec((1,) + array.shape[1:], lambda s, *pre: (s + start,) + (0,) * lead)

    def second_by_slot(array):
        lead = array.ndim - 2
        shape = (array.shape[0], 1) + array.shape[2:]
        return pl.BlockSpec(shape, lambda s, *pre: (0, s + start) + (0,) * lead)

    def out_by_slot(array):
        return pl.BlockSpec((1,) + array.shape[1:], lambda s, *pre: (s,) + (0,) * (array.ndim - 1))

    def out_second(array):
        shape = (array.shape[0], 1) + array.shape[2:]
        return pl.BlockSpec(shape, lambda s, *pre: (0, s) + (0,) * (array.ndim - 2))

    heads = width // HEAD_DIM
    mates = len(mate)
    earlier = () if d_query is None else (d_query,)
    operands = (*earlier, query, own, even, odd, *mate, grad, mixed, logs, cosine, sine)
    specs = [anywhere] * len(earlier) + [by_slot(query), by_slot(own), second_by_slot(even), second_by_slot(odd)]
    specs += [by_slot(m) for m in mate]
    specs += [by_slot(grad), by_slot(mixed), by_slot(logs), whole(cosine), whole(sine)]
    outs = (
        struct(query.shape, bf16),
        struct((slots,) + own.shape[1:], f32),
        struct((even.shape[0], slots) + even.shape[2:], bf16),
        struct((odd.shape[0], slots) + odd.shape[2:], bf16),
        *(struct((slots,) + m.shape[1:], bf16) for m in mate),
    )
    out_specs = [by_slot(outs[0]), out_by_slot(outs[1]), out_second(even), out_second(odd)]
    out_specs += [out_by_slot(m) for m in mate]
    count = 1 + 2 * even.shape[0] + mates
    return pl.pallas_call(
        functools.partial(attend_back_kernel, kv_heads, heads // kv_heads, mates, len(earlier)),
        grid_spec=pltpu.PrefetchScalarGridSpec(
            num_scalar_prefetch=1,
            grid=(slots,),
            in_specs=specs,
            out_specs=out_specs,
            scratch_shapes=[pltpu.VMEM((count,) + own.shape[1:], f32)],
        ),
        out_shape=outs,
        input_output_aliases={1: 0} if earlier else {},
        compiler_params=params(),
        cost_estimate=cost(25e9, 20e6, slots * heads * block * (own.shape[1] * 5)),
        name="attend_back",
    )(flags, *operands)


def middle_kernel(
    first, adapter, live, core, own, other, context, tok, cot, in_o, out_o, gain, in_g, in_u, out_d,
    mid_ref, normed_ref, grad_ref, rank_o_ref, rank_g_ref, rank_u_ref, grad_rank_ref, weight, sems,
):
    fetch_once(half_copies(core[0], own, other, ((first, weight.shape[2], weight),), sems))
    s = pl.program_id(0)
    ctx = context[0]
    mask = slot_lanes(adapter, ctx.shape[0], in_o.shape[0])
    rank = picked(mask, nt(ctx, in_o[...]))
    rank_o_ref[0] = rank
    mid = tok[0].astype(f32) + nt(ctx, as_matrix(weight)) + adapter_scale * nn(rank, out_o[...])
    mid_ref[0] = mid
    inverse = lax.rsqrt(jnp.mean(mid * mid, axis=-1, keepdims=True) + norm_eps)
    normed = (mid * inverse * gain[...]).astype(bf16)
    normed_ref[0] = normed
    rank_g_ref[0] = picked(mask, nt(normed, in_g[...]))
    rank_u_ref[0] = picked(mask, nt(normed, in_u[...]))
    on = jnp.where(live[s] != 0, 1.0, 0.0)
    grad = (cot[0].astype(f32) * on).astype(bf16)
    grad_ref[0] = grad
    grad_rank_ref[0] = picked(mask, adapter_scale * nt(grad, out_d[...]))


def middle_side(adapter_of, live, core, own, other, first, context, tokens, cotangent, in_o, out_o, gain,
                in_g, in_u, out_d):
    slots, block, width = tokens.shape
    shared = (in_o, out_o, gain, in_g, in_u, out_d)
    rank = struct((slots, block, in_o.shape[0]), bf16)
    wide = struct(tokens.shape, bf16)
    outs = (struct(tokens.shape, f32), wide, wide, rank, rank, rank, rank)
    return pl.pallas_call(
        functools.partial(middle_kernel, first),
        grid_spec=pltpu.PrefetchScalarGridSpec(
            num_scalar_prefetch=3,
            grid=(slots,),
            in_specs=[anywhere, anywhere]
            + [by_slot(a) for a in (context, tokens, cotangent)]
            + [whole(a) for a in shared],
            out_specs=[by_slot(o) for o in outs],
            scratch_shapes=buffers(own, (width // 2 // own.shape[1],), width),
        ),
        out_shape=outs,
        compiler_params=params(),
        cost_estimate=cost(3 * slots * block * width * width, 28e6),
        name="middle_side",
    )(adapter_of, live, core, own, other, context, tokens, cotangent, *shared)


def feed_copies(half, gate, up, down, sems, base):
    copies = []

    def add(source, target):
        copies.append(pltpu.make_async_copy(source, target, sems.at[base + len(copies)]))

    shards, line, rows, cols = half.shape
    rows //= 3
    for w in range(shards):
        span = pl.ds(w * cols, cols)
        add(half.at[w, :, pl.ds(0, rows), :], gate.at[:, :, span])
        add(half.at[w, :, pl.ds(rows, rows), :], up.at[:, :, span])
    last = pl.ds(2 * rows, rows)
    if shards == 1:
        add(half.at[0, :, last, :], down)
    else:
        for w in range(shards):
            for z in range(line):
                add(half.at[w, z, last, :], down.at[w, :, pl.ds(z * cols, cols)])
    return copies


def feed_kernel(first, count, span, core, *refs):
    halves, refs = refs[:count], refs[count:]
    x_ref, g_ref, rank_d, rank_g, rank_u = refs[:5]
    adapters, refs = refs[5 : 5 + 3 * count], refs[5 + 3 * count :]
    if first:
        sums_in = None
    else:
        sums_in, refs = refs[:5], refs[5:]
    sums_out, terms, refs = refs[:5], refs[5 : 5 + count], refs[5 + count :]
    weights, accs, sems = refs[: 3 * count], refs[3 * count : 4 * count], refs[4 * count]
    s = pl.program_id(0)
    copies, base = [], 0
    for i in range(count):
        copies.append(feed_copies(halves[i], *weights[3 * i : 3 * i + 3], sems, base))
        base += len(copies[-1])

    @pl.when(s == 0)
    def _():
        for group in copies:
            for c in group:
                c.start()
        for acc in accs:
            acc[...] = jnp.zeros_like(acc)

    x, g = x_ref[0], g_ref[0]
    r_d, r_g, r_u = rank_d[0], rank_g[0], rank_u[0]
    sums = [0.0] * 5 if first else [r[0] for r in sums_in]
    for i in range(count):

        @pl.when(s == 0)
        def _(i=i):
            for c in copies[i]:
                c.wait()

        gate_m, up_m, down_m = (as_matrix(b) for b in weights[3 * i : 3 * i + 3])
        in_d, out_g, out_u = (a[0] for a in adapters[3 * i : 3 * i + 3])
        acc = accs[i]
        hidden = gate_m.shape[0]
        for at in range(0, hidden, span):
            part = slice(at, min(at + span, hidden))
            o_g, o_u, i_d = out_g[part], out_u[part], in_d[part]
            w_g, w_u, w_d = gate_m[part], up_m[part], down_m[part]
            gate = nt(x, w_g) + adapter_scale * nt(r_g, o_g)
            up = nt(x, w_u) + adapter_scale * nt(r_u, o_u)
            d_act = nt(g, w_d) + nt(r_d, i_d)
            sig = 1.0 / (1.0 + jnp.exp(-gate))
            lit = gate * sig
            act = (lit * up).astype(bf16)
            d_gate = (d_act * up * sig * (1.0 + gate * (1.0 - sig))).astype(bf16)
            d_up = (d_act * lit).astype(bf16)
            sums[0] = sums[0] + nn(act, w_d)
            sums[1] = sums[1] + nn(d_gate, w_g) + nn(d_up, w_u)
            sums[2] = sums[2] + nn(act, i_d)
            sums[3] = sums[3] + nn(d_gate, o_g)
            sums[4] = sums[4] + nn(d_up, o_u)
            acc[0, :, part] += tn(r_g, d_gate)
            acc[1, :, part] += tn(r_u, d_up)
            acc[2, :, part] += tn(r_d, act)
    for ref, value in zip(sums_out, sums):
        ref[0] = value

    @pl.when(s == pl.num_programs(0) - 1)
    def _():
        for i in range(count):
            line, rows, _ = weights[3 * i].shape
            for j, scale in enumerate((adapter_scale, adapter_scale, 1.0)):
                turned = (accs[i][j] * scale).T.astype(bf16)
                for z in range(line):
                    terms[i][z, j * rows : (j + 1) * rows, :] = turned[z * rows : (z + 1) * rows]


def feed_part(core, halves, normed, grad, ranks, sums):
    slots, block, width = normed.shape
    rank_width = ranks[0].shape[-1]
    count = len(halves)
    first = sums is None
    operands = [h[0] for h in halves] + [normed, grad, *ranks]
    specs = [anywhere] * count + [by_slot(a) for a in (normed, grad, *ranks)]
    for _, of_other, adapters in halves:
        for a in adapters:
            operands.append(a)
            side = (lambda s, c: (1 - c[0], 0, 0)) if of_other else (lambda s, c: (c[0], 0, 0))
            specs.append(pl.BlockSpec((1,) + a.shape[1:], side))
    aliases = {}
    if not first:
        aliases = {1 + len(operands) + i: i for i in range(len(sums))}
        operands += list(sums)
        specs += [by_slot(a) for a in sums]
    rank_sum = struct((slots, block, rank_width), f32)
    wide_sum = struct((slots, block, width), f32)
    outs = [wide_sum, wide_sum, rank_sum, rank_sum, rank_sum]
    out_specs = [by_slot(o) for o in outs]
    scratch, hidden, copies = [], 0, 0
    for half, _, _ in halves:
        shards, line, rows = half.shape[:3]
        terms = struct((line, rows, rank_width), bf16)
        outs.append(terms)
        out_specs.append(whole(terms))
        scratch += [pltpu.VMEM((line, rows // 3, width), bf16)] * 3
        hidden += line * rows // 3
        copies += 2 * shards + (1 if shards == 1 else shards * line)
    for half, _, _ in halves:
        scratch.append(pltpu.VMEM((3, rank_width, half.shape[1] * half.shape[2] // 3), f32))
    return pl.pallas_call(
        functools.partial(feed_kernel, first, count, 512),
        grid_spec=pltpu.PrefetchScalarGridSpec(
            num_scalar_prefetch=1,
            grid=(slots,),
            in_specs=specs,
            out_specs=out_specs,
            scratch_shapes=scratch + [pltpu.SemaphoreType.DMA((copies,))],
        ),
        out_shape=outs,
        input_output_aliases=aliases,
        compiler_params=params(),
        cost_estimate=cost(20 * slots * block * hidden * width, 60e6, slots * block * hidden),
        name="feed_part",
    )(core, *operands)


def rms_back(hidden, gain, grad_normed):
    scaled = grad_normed * gain
    inverse = lax.rsqrt(jnp.mean(hidden * hidden, axis=-1, keepdims=True) + norm_eps)
    return inverse * scaled - hidden * (inverse * inverse * inverse) * jnp.mean(
        scaled * hidden, axis=-1, keepdims=True
    )


def keep_terms(acc, out, core, terms):
    s = pl.program_id(0)

    @pl.when(s == 0)
    def _():
        at = 0
        for t in terms:
            acc[:, at : at + t.shape[1]] = t
            at += t.shape[1]

    @pl.when(s != 0)
    def _():
        at = 0
        for t in terms:
            acc[:, at : at + t.shape[1]] += t
            at += t.shape[1]

    @pl.when(s == pl.num_programs(0) - 1)
    def _():
        line = out.shape[1]
        at, row = 0, 0
        for t in terms:
            n = t.shape[1]
            cut = n // (2 * line)
            turned = acc[:, at : at + n].T.astype(bf16)
            for z in range(line):
                for side in (0, 1):
                    block = turned[(2 * z + side) * cut : (2 * z + side + 1) * cut]
                    out[jnp.where(core == side, 0, 1), z, row : row + cut, :] = block
            at += n
            row += cut


def turned_terms(line, columns, ranks):
    return struct((2, line, columns // (2 * line), ranks), bf16)


def return_kernel(
    first, adapter, live, core, own, other, y, dx, sum_d, sum_g, sum_u, mid_in, normed, grad, context,
    rank_o, in_o, out_o, gain, in_g, in_u, out_d, layer_ref, d_mid_ref, d_ctx_ref, terms_ref, acc,
    weight, sems,
):
    fetch_once(half_copies(core[0], own, other, ((first, weight.shape[2], weight),), sems))
    s = pl.program_id(0)
    on = jnp.where(live[s] != 0, 1.0, 0.0)
    mid = mid_in[0]
    g = grad[0]
    mask = slot_lanes(adapter, g.shape[0], in_o.shape[0])
    rank_down = picked(mask, sum_d[0])
    result = mid + y[0] + adapter_scale * nn(rank_down, out_d[...])
    layer_ref[0] = (result * on).astype(bf16)
    back_g = picked(mask, adapter_scale * sum_g[0])
    back_u = picked(mask, adapter_scale * sum_u[0])
    d_normed = dx[0] + nn(back_g, in_g[...]) + nn(back_u, in_u[...])
    d_mid = g.astype(f32) + rms_back(mid, gain[...], d_normed)
    d_mid_ref[0] = d_mid
    branch = d_mid.astype(bf16)
    back_o = picked(mask, adapter_scale * nt(branch, out_o[...]))
    d_ctx_ref[0] = (nn(branch, as_matrix(weight)) + nn(back_o, in_o[...])).astype(bf16)
    x = normed[0]
    keep_terms(
        acc,
        terms_ref,
        core[0],
        (
            tn(back_o, context[0]),
            adapter_scale * tn(rank_o[0], branch),
            tn(back_g, x),
            tn(back_u, x),
            adapter_scale * tn(rank_down, g),
        ),
    )


def return_side(adapter_of, live, core, own, other, first, sums, mid, normed, grad, context, rank_o, in_o,
                out_o, gain, in_g, in_u, out_d):
    slots, block, width = mid.shape
    rows = (*sums, mid, normed, grad, context, rank_o)
    shared = (in_o, out_o, gain, in_g, in_u, out_d)
    ranks = in_o.shape[0]
    outs = (
        struct(mid.shape, bf16),
        struct(mid.shape, f32),
        struct(mid.shape, bf16),
        turned_terms(own.shape[1], 5 * width, ranks),
    )
    return pl.pallas_call(
        functools.partial(return_kernel, first),
        grid_spec=pltpu.PrefetchScalarGridSpec(
            num_scalar_prefetch=3,
            grid=(slots,),
            in_specs=[anywhere, anywhere] + [by_slot(r) for r in rows] + [whole(a) for a in shared],
            out_specs=[by_slot(o) for o in outs[:3]] + [whole(outs[3])],
            scratch_shapes=[pltpu.VMEM((ranks, 5 * width), f32)]
            + buffers(own, (width // 2 // own.shape[1],), width),
        ),
        out_shape=outs,
        compiler_params=params(),
        cost_estimate=cost(4 * slots * block * width * width, 50e6),
        name="return_side",
    )(adapter_of, live, core, own, other, *rows, *shared)


def query_back_kernel(
    adapter, core, own, other, d_query, normed, rank_q, in_q, out_q, d_normed_ref, terms_ref, acc,
    weight, sems,
):
    fetch_once(half_copies(core[0], own, other, ((0, weight.shape[2], weight),), sems))
    g, x = d_query[0], normed[0]
    mask = slot_lanes(adapter, g.shape[0], in_q.shape[0])
    rank_back = picked(mask, adapter_scale * nt(g, out_q[...]))
    d_normed_ref[0] = nn(g, as_matrix(weight)) + nn(rank_back, in_q[...])
    keep_terms(acc, terms_ref, core[0], (tn(rank_back, x), adapter_scale * tn(rank_q[0], g)))


def query_back_side(adapter_of, core, own, other, d_query, normed, rank_q, in_q, out_q):
    slots, block, width = normed.shape
    ranks = in_q.shape[0]
    rows = (d_query, normed, rank_q)
    shared = (in_q, out_q)
    outs = (struct(normed.shape, f32), turned_terms(own.shape[1], 2 * width, ranks))
    return pl.pallas_call(
        query_back_kernel,
        grid_spec=pltpu.PrefetchScalarGridSpec(
            num_scalar_prefetch=2,
            grid=(slots,),
            in_specs=[anywhere, anywhere] + [by_slot(r) for r in rows] + [whole(a) for a in shared],
            out_specs=[by_slot(outs[0]), whole(outs[1])],
            scratch_shapes=[pltpu.VMEM((ranks, 2 * width), f32)]
            + buffers(own, (width // 2 // own.shape[1],), width),
        ),
        out_shape=outs,
        compiler_params=params(),
        cost_estimate=cost(3 * slots * block * width * width, 22e6),
        name="query_back_side",
    )(adapter_of, core, own, other, *rows, *shared)


def output_kernel(
    first, adapter, live, core, own, other, d_kv, d_normed_q, d_mid, normed, rank_k, rank_v, tok, gain,
    cosine, sine, in_k, in_v, out_k, out_v, grad_ref, terms_ref, acc, key_w, value_w, sems,
):
    count = key_w.shape[2]
    parts = ((first, count, key_w), (first + count, count, value_w))
    fetch_once(half_copies(core[0], own, other, parts, sems))
    s = pl.program_id(0)
    on = jnp.where(live[s] != 0, 1.0, 0.0)
    kv_width = d_kv.shape[-1] // 2
    cos, sin = cosine[...], sine[...]
    back = d_kv[0]
    x = normed[0]
    mask = slot_lanes(adapter, x.shape[0], in_k.shape[0])
    keys = []
    for h in range(kv_width // HEAD_DIM):
        keys.append(turn_back(back[:, h * HEAD_DIM : (h + 1) * HEAD_DIM], cos, sin).astype(bf16))
    g_k, g_v = jnp.concatenate(keys, axis=1), back[:, kv_width:].astype(bf16)
    back_k = picked(mask, adapter_scale * nt(g_k, out_k[...]))
    back_v = picked(mask, adapter_scale * nt(g_v, out_v[...]))
    d_normed = d_normed_q[0] + nn(g_k, as_matrix(key_w)) + nn(g_v, as_matrix(value_w))
    d_normed = d_normed + nn(back_k, in_k[...]) + nn(back_v, in_v[...])
    hidden = tok[0].astype(f32)
    d_hidden = d_mid[0] + rms_back(hidden, gain[...], d_normed)
    grad_ref[0] = (d_hidden * on).astype(bf16)
    keep_terms(
        acc,
        terms_ref,
        core[0],
        (
            tn(back_k, x),
            tn(back_v, x),
            adapter_scale * tn(rank_k[0], g_k),
            adapter_scale * tn(rank_v[0], g_v),
        ),
    )


def output_side(adapter_of, live, core, own, other, first, d_kv, d_normed_q, d_mid, normed, rank_k, rank_v,
                tokens, gain, cosine, sine, adapters):
    slots, block, width = tokens.shape
    ranks = adapters[0].shape[0]
    kv_columns = d_kv.shape[-1]
    columns = 2 * width + kv_columns
    kv_rows = kv_columns // 4 // own.shape[1]
    rows = (d_kv, d_normed_q, d_mid, normed, rank_k, rank_v, tokens)
    shared = (gain, cosine, sine, *adapters)
    outs = (struct(tokens.shape, bf16), turned_terms(own.shape[1], columns, ranks))
    return pl.pallas_call(
        functools.partial(output_kernel, first),
        grid_spec=pltpu.PrefetchScalarGridSpec(
            num_scalar_prefetch=3,
            grid=(slots,),
            in_specs=[anywhere, anywhere] + [by_slot(r) for r in rows] + [whole(a) for a in shared],
            out_specs=[by_slot(outs[0]), whole(outs[1])],
            scratch_shapes=[pltpu.VMEM((ranks, columns), f32)]
            + buffers(own, (kv_rows, kv_rows), width),
        ),
        out_shape=outs,
        compiler_params=params(),
        cost_estimate=cost(3 * slots * block * width * kv_columns, 30e6),
        name="output_side",
    )(adapter_of, live, core, own, other, *rows, *shared)


def hop_up(array, t, line):
    half = line // 2
    return along_line(array, [(z, z - 1) for z in range(1, line) if half <= z + t - 1 < line])


def hops_down(mine, line):
    half = line // 2
    moved = [mine]
    for t in range(1, half):
        pairs = [(z, z + 1) for z in range(line - 1) if half <= z - t + 1]
        moved.append(along_line(moved[-1], pairs))
    return moved


def prompt_blocks(from_above, from_below, place, line):
    half = line // 2
    mine = from_above[0]
    blocks = []
    for b in range(half, line):
        out = mine
        for z in range(line):
            if z < b:
                out = jnp.where(place == z, from_above[b - z], out)
            elif z > b:
                out = jnp.where(place == z, from_below[z - b], out)
        blocks.append(out)
    return jnp.stack(blocks)


def take(blocks, at):
    return lax.dynamic_index_in_dim(blocks, jnp.clip(at, 0, blocks.shape[0] - 1), 0, False)


def fold_blocks(parts, line):
    half = line // 2
    return [along_line(parts, [(z, half - 1)]) for z in range(half - 1)]


def return_blocks(parts, total, place, line):
    half = line // 2
    came = []
    for b in range(half, line):
        came.append(along_line(total[b - half], [(half - 1, b)]))
    for by in range(1, half):
        pairs = [(z, z - by) for z in range(half + by, line)]
        came.append(along_line(take(parts, place - by - half), pairs))
    return came


def owned_blocks(parts, came, place, line):
    half = line // 2
    total = functools.reduce(jnp.add, [c.astype(f32) for c in came])
    total = total + take(parts, place - half).astype(f32)
    return jnp.where(place >= half, total, 0.0)


def finish_kernel(places, segments, core, own, other, *refs):
    count = len(places)
    outs, buffers, sems = refs[:count], refs[count : 2 * count], refs[2 * count]
    shards, line, rows, _ = own.shape
    copies = []
    for side, half in ((core[0], own), (1 - core[0], other)):
        for at, n, to, offset in segments:
            while n:
                w, row = at // rows, at % rows
                take = min(n, rows - row)
                for z in range(line):
                    start = pl.multiple_of((2 * z + side) * places[to] + offset, 16)
                    copies.append(
                        pltpu.make_async_copy(
                            half.at[w, z, pl.ds(row, take), :],
                            buffers[to].at[pl.ds(start, take), :],
                            sems.at[len(copies)],
                        )
                    )
                at, n, offset = at + take, n - take, offset + take
    for c in copies:
        c.start()
    for c in copies:
        c.wait()
    for out, buffer in zip(outs, buffers):
        total = buffer.shape[0]
        step = next(d for d in (1280, 768, 256) if total % d == 0)
        for at in range(0, total, step):
            block = buffer[at : at + step, :].astype(f32).T
            out[:, :, at : at + step] = block.reshape(out.shape[:2] + (step,))


def finish(core, own, other, places, segments):
    shards, line, rows, ranks = own.shape
    outs = [struct((ranks // RANK, RANK, 2 * line * p), f32) for p in places]
    pieces = 0
    for at, n, _, _ in segments:
        pieces += (at + n - 1) // rows - at // rows + 1
    return pl.pallas_call(
        functools.partial(finish_kernel, places, segments),
        grid_spec=pltpu.PrefetchScalarGridSpec(
            num_scalar_prefetch=1,
            grid=(1,),
            in_specs=[anywhere, anywhere],
            out_specs=[whole(o) for o in outs],
            scratch_shapes=[pltpu.VMEM((2 * line * p, ranks), bf16) for p in places]
            + [pltpu.SemaphoreType.DMA((2 * line * pieces,))],
        ),
        out_shape=outs,
        compiler_params=params(),
        name="finish",
    )(core, own, other)


def split_rows(mine, shards):
    n = mine.shape[1]
    padded = jnp.pad(mine, ((0, 0), (0, -n % (16 * shards)), (0, 0)))
    return padded.reshape(mine.shape[0], shards, -1, mine.shape[2])


def late_segments(rows, pitch, shift, counts, first):
    segments, at = [], 0
    for i, n in enumerate(counts):
        done = 0
        while done < n:
            w, row = (at + done) // rows, (at + done) % rows
            take = min(n - done, rows - row)
            segments.append((w * pitch + shift + row, take, first + i, done))
            done += take
        at += n
    return segments


def pack_kernel(spans, core, gate, up, down, given, *outs):
    kept = down[core[0]]
    came = given[...]
    first = jnp.where(core[0] == 0, kept, came)
    second = jnp.where(core[0] == 0, came, kept)
    turned = (gate[...].T, up[...].T, jnp.concatenate([first, second], axis=1))
    for out, (at, n) in zip(outs, spans):
        for i, t in enumerate(turned):
            out[i * n : (i + 1) * n, :] = t[at : at + n]


def pack_weights(spans, core, gate, up, down, given):
    outs = [struct((3 * n, gate.shape[0]), bf16) for _, n in spans]
    return pl.pallas_call(
        functools.partial(pack_kernel, spans),
        grid_spec=pltpu.PrefetchScalarGridSpec(
            num_scalar_prefetch=1,
            grid=(1,),
            in_specs=[whole(a) for a in (gate, up, down, given)],
            out_specs=[whole(o) for o in outs],
        ),
        out_shape=outs,
        compiler_params=params(),
        cost_estimate=cost(0, 12e6),
        name="pack_weights",
    )(core, gate, up, down, given)


def order_kernel(spans, line, wide, *outs):
    scratch = outs[-1]
    hidden = wide.shape[1]
    step = next(d for d in (1280, 256) if hidden % d == 0)
    for at in range(0, hidden, step):
        scratch[at : at + step, :] = wide[:, at : at + step].T
    shard = hidden // (2 * line)
    for out, (at, n) in zip(outs, spans):
        for z in range(line):
            for side in (0, 1):
                start = (2 * z + side) * shard + at
                out[side, z * n : (z + 1) * n, :] = scratch[start : start + n, :]


def order_adapters(spans, line, wide):
    ranks, hidden = wide.shape
    outs = [struct((2, line * n, ranks), bf16) for _, n in spans]
    return pl.pallas_call(
        functools.partial(order_kernel, spans, line),
        out_shape=outs,
        scratch_shapes=[pltpu.VMEM((hidden, ranks), bf16)],
        compiler_params=pltpu.CompilerParams(vmem_limit_bytes=VMEM_LIMIT),
        cost_estimate=cost(0, 5e6),
        name="order_adapters",
    )(wide)


def local(
    tokens,
    cotangent,
    group_slot,
    group_adapter,
    attn_gain,
    mlp_gain,
    w_query,
    w_key,
    w_value,
    w_output,
    w_gate,
    w_up,
    w_down,
    query_bias,
    key_bias,
    value_bias,
    adapt_query_in,
    adapt_query_out,
    adapt_key_in,
    adapt_key_out,
    adapt_value_in,
    adapt_value_out,
    adapt_output_in,
    adapt_output_out,
    adapt_gate_in,
    adapt_gate_out,
    adapt_up_in,
    adapt_up_out,
    adapt_down_in,
    adapt_down_out,
):
    slots, block, width = tokens.shape
    ctx_size, shards = lax.axis_size("ctx"), lax.axis_size("wsh")
    line = ctx_size // 2
    ctx_place, shard_place = lax.axis_index("ctx"), lax.axis_index("wsh")
    place, core = ctx_place // 2, ctx_place % 2
    kv_width = key_bias.shape[0]
    kv_heads = kv_width // HEAD_DIM
    hidden = adapt_gate_out.shape[-1]
    if line != shards or (CONTS * CONT) != line * block or CONT // block > 2:
        raise ValueError("unsupported mesh")
    mates = CONT // block - 1

    slot_ids = shard_place * slots + jnp.arange(slots, dtype=jnp.int32)
    matches = group_slot[None, :] == slot_ids[:, None]
    live = jnp.any(matches, axis=1).astype(jnp.int32)
    adapter_of = jnp.sum(jnp.where(matches, group_adapter[None, :], 0), axis=1).astype(jnp.int32)
    index = ctx_place * block + jnp.arange(block, dtype=jnp.int32)
    position = jnp.where(index >= CONTS * CONT, index - CONTS * CONT, PROMPT + index % CONT)
    frequency = rope_base ** (-(jnp.arange(HEAD_DIM // 2, dtype=f32) * 2.0) / HEAD_DIM)
    angles = position.astype(f32)[:, None] * frequency[None, :]
    cosine = jnp.concatenate([jnp.cos(angles), jnp.cos(angles)], axis=-1)
    sine = jnp.concatenate([-jnp.sin(angles), jnp.sin(angles)], axis=-1)

    is_cont = ctx_place < line
    of_side = [2 * (line // 2 + i) + core for i in range(line // 2)]
    of_other = [2 * (line // 2 + i) + 1 - core for i in range(line // 2)]
    flags = [(is_cont | (b < ctx_place)) for b in of_side + of_other]
    flags += [is_cont & (core == 1)] if mates else []
    flags = jnp.stack(flags).astype(jnp.int32)

    def wide(half):
        if half.shape[-1] % 128 == 0:
            return half
        return jnp.transpose(half, (1, 2, 0, 3)).reshape(1, line, half.shape[2], width)

    def wide_feed(half):
        if half.shape[-1] % 128 == 0:
            return half
        split = half.shape[2] // 3 * 2
        out_in = jnp.transpose(half[:, :, :split], (1, 2, 0, 3)).reshape(1, line, split, width)
        in_out = jnp.transpose(half[:, :, split:], (0, 2, 1, 3)).reshape(1, line, split // 2, width)
        return jnp.concatenate([out_in, in_out], axis=2)

    q_rows = w_query.shape[1]
    o_at = q_rows
    kv_piece = jnp.concatenate([w_key.T, w_value.T], axis=0)
    qo_piece = jnp.concatenate([w_query.T, w_output.T], axis=0)
    kv_moves = line_moves(kv_piece, line)
    qo_moves = line_moves(qo_piece, line)

    shard_hidden = w_gate.shape[1]
    unit = shard_hidden // 35
    part_rows = [8 * unit, 8 * unit, 8 * unit, 6 * unit, 5 * unit]
    part_at = [sum(part_rows[:i]) for i in range(len(part_rows))]
    parts = len(part_rows)
    spans = list(zip(part_at, part_rows))
    core_place = core.astype(jnp.int32)[None]
    down_halves = w_down.reshape(2, shard_hidden, w_down.shape[1])
    given = swap_cores(lax.dynamic_index_in_dim(down_halves, 1 - core, 0, False))
    pieces = pack_weights(spans, core_place, w_gate, w_up, down_halves, given)
    pieces = list(pieces)

    lined_kv = in_order(kv_piece, kv_moves, place, line)
    down_in, gate_out, up_out = (
        order_adapters(spans, line, a.reshape(-1, a.shape[-1]))
        for a in (adapt_down_in, adapt_gate_out, adapt_up_out)
    )
    kv_half = gather_wsh(lined_kv, shard_place)
    kv_own, kv_other = wide(kv_half), wide(swap_cores(kv_half))
    lined_qo = in_order(qo_piece, hold(qo_moves, pieces[0]), place, line)
    qo_half = shard_gather(lined_qo)

    def flat(adapters):
        return adapters.reshape(-1, adapters.shape[-1])

    query_in, key_in, value_in, output_in, gate_in, up_in = (
        flat(a)
        for a in (adapt_query_in, adapt_key_in, adapt_value_in, adapt_output_in, adapt_gate_in, adapt_up_in)
    )
    query_out, key_out, value_out, output_out, down_out = (
        flat(a)
        for a in (adapt_query_out, adapt_key_out, adapt_value_out, adapt_output_out, adapt_down_out)
    )

    gain_one = attn_gain.astype(f32)[None, :]
    gain_two = mlp_gain.astype(f32)[None, :]
    q_bias = query_bias.astype(f32)[None, :]
    kv_bias = jnp.concatenate([key_bias, value_bias]).astype(f32)[None, :]

    lined, halves = [], []

    def take_in(moves, group, *after):
        moves, at = hold(moves, *after), 0
        for i in group:
            n = pieces[i].shape[0]
            came = [m[at : at + n] for m in moves]
            lined.append(in_order(pieces[i], came, place, line))
            halves.append(shard_gather(lined[-1]))
            at += n

    def set_out(group, *after):
        together = hold([pieces[i] for i in group], *after)
        piece = jnp.concatenate(together, axis=0) if len(group) > 1 else together[0]
        return piece, line_moves(piece, line)

    _, moves = set_out([0], lined_qo)
    take_in(moves, [0], tip(kv_half))
    piece, moves = set_out([1], lined[0])
    (kv_own,) = hold([kv_own], piece)
    attn_kv = (core_place, kv_own, kv_other)
    kv_adapters = (key_in, value_in, key_out, value_out)
    normed, rank_k, rank_v, key_value = key_value_side(
        adapter_of, *attn_kv, 0, tokens, gain_one, kv_bias, kv_adapters, cosine, sine
    )
    hops = [key_value, hop_up(key_value, 1, line)]
    below = hops_down(key_value, line)
    mate = (swap_cores(key_value),) if mates else ()
    hops.append(hop_up(hops[1], 2, line))
    for t in range(3, line):
        hops.append(hop_up(hops[-1], t, line))
    (qo_half,) = hold([qo_half], tip(hops[2]))
    attn = (core_place, wide(qo_half), wide(swap_cores(qo_half)))
    rank_q, queries = query_side(
        adapter_of, *attn, normed, q_bias, (query_in, query_out), cosine, sine
    )
    side = prompt_blocks(hops, below, place, line)
    other_side = swap_cores(side)
    take_in(moves, [1], tip(side), *down_in, *gate_out, *up_out)
    piece, moves = set_out([2], lined[1])
    (queries,) = hold([queries], piece)
    context, mixed, logs = attend(flags, queries, key_value, side, other_side, mate, kv_heads)
    take_in(moves, [2], context)
    piece, moves = set_out([3], lined[2])
    (context,) = hold([context], piece)
    mid, normed2, grad_out, rank_o, rank_g, rank_u, rank_d = middle_side(
        adapter_of, live, *attn, o_at, context, tokens, cotangent, output_in, output_out, gain_two,
        gate_in, up_in, down_out,
    )

    sums, own_terms, other_terms, others = None, [], [], []
    before = normed2
    for i in range(parts + 1):
        if 0 < i < 3:
            take_in(moves, [i + 2], before)
            if i + 3 < parts:
                _, moves = set_out([i + 3], lined[i + 2])
        if i < parts:
            (halves[i],) = hold([halves[i]], before, lined[-1])
            others.append(swap_cores(halves[i]))
        use = []
        if i < parts:
            use.append((wide_feed(halves[i]), False, (down_in[i], gate_out[i], up_out[i])))
        if i:
            j = i - 1
            use.append((wide_feed(others[j]), True, (down_in[j], gate_out[j], up_out[j])))
        done = feed_part(core_place, use, normed2, grad_out, (rank_d, rank_g, rank_u), sums)
        sums, terms = done[:5], done[5:]
        if i < parts:
            own_terms.append(terms[0])
        if i:
            other_terms.append(terms[-1])
        before = sums[2]
    early_keep = jnp.concatenate(own_terms, axis=1)
    early_came = swap_cores(jnp.concatenate(other_terms, axis=1))
    layer_out, d_mid, d_context, terms = return_side(
        adapter_of, live, *attn, o_at, sums, mid, normed2, grad_out, context, rank_o,
        output_in, output_out, gain_two, gate_in, up_in, down_out,
    )

    first_half = slots // 2

    def slots_back(start, count, d_context, d_query=None):
        return attend_back(
            flags, queries, key_value, side, other_side, mate, d_context, mixed, logs, cosine, sine,
            kv_heads, start, count, d_query,
        )

    (early_came,) = hold([early_came], d_context)
    early = split_rows(add_up([early_keep, early_came]), shards)
    early_outs = wsh_outs(early, shard_place)
    late_keep, late_give = terms[0], terms[1]
    (d_context, late_give) = hold([d_context, late_give], *early_outs)
    early_moves = wsh_send(early_outs)
    late_came = swap_cores(late_give)
    back = [slots_back(0, first_half, d_context)]
    sides = [add_up([back[0][2], swap_cores(back[0][3])])]
    late_came, *early_moves = hold([late_came, *early_moves], back[0][1])
    late = split_rows(add_up([late_keep, late_came]), shards)
    late_outs = wsh_outs(late, shard_place)
    early = wsh_sum(early, shard_place, early_moves)
    early_outs = line_outs(early, place, line)
    (d_context,) = hold([d_context], sides[0], *late_outs, *early_outs)
    folded = [fold_blocks(sides[0], line)]
    late_moves = wsh_send(late_outs)
    early_moves = line_send(early_outs, line)
    back.append(slots_back(first_half, slots - first_half, d_context, back[0][0]))
    swapped = swap_cores(back[1][3])
    folded[0] = hold(folded[0], back[1][1]) if folded[0] else []
    sides.append(add_up([back[1][2], swapped]))
    total = add_up([sides[0]] + folded[0])
    (d_query,) = hold([back[1][0]], sides[1], total)
    folded.append(fold_blocks(sides[1], line))
    came = [return_blocks(sides[0], total, place, line)]
    d_normed_q, query_terms = query_back_side(
        adapter_of, *attn, d_query, normed, rank_q, query_in, query_out
    )
    folded[1] = hold(folded[1], query_terms) if folded[1] else []
    total = add_up([sides[1]] + folded[1])
    came.append(return_blocks(sides[1], total, place, line))
    late = wsh_sum(late, shard_place, hold(late_moves, query_terms, tip(total)))
    late_moves = line_send(line_outs(late, place, line), line)
    early_terms = line_sum(early, place, hold(early_moves, query_terms, tip(total)))
    came[0] = hold(came[0], query_terms)
    d_kv = jnp.concatenate(
        [b[1] + owned_blocks(p, c, place, line) for b, p, c in zip(back, sides, came)], axis=0
    )
    if mates:
        d_kv = d_kv + swap_cores(jnp.concatenate([b[4] for b in back], axis=0)).astype(f32)
    (early_terms,) = hold([early_terms], tip(d_kv))
    early_moves = line_moves(early_terms, line)
    (d_kv,) = hold([d_kv], early_terms)
    input_grad, kv_terms = output_side(
        adapter_of, live, *attn_kv, 0, d_kv, d_normed_q, d_mid, normed, rank_k, rank_v, tokens, gain_one,
        cosine, sine, kv_adapters,
    )

    width_rows = width // (2 * line)
    early_lined = in_order(early_terms, hold(early_moves, kv_terms), place, line)
    early_half = shard_gather(early_lined)
    late_terms = line_sum(late, place, hold(late_moves, kv_terms))
    last_keep = jnp.concatenate([query_terms[0], kv_terms[0]], axis=1)
    last_came = swap_cores(jnp.concatenate([query_terms[1], kv_terms[1]], axis=1))
    last = split_rows(add_up([last_keep, last_came]), shards)
    moves = wsh_send(wsh_outs(last, shard_place))
    last = wsh_sum(last, shard_place, moves)
    moves = line_send(line_outs(last, place, line), line)
    last_terms = line_sum(last, place, moves)
    last_terms = jnp.concatenate([late_terms, last_terms], axis=0)
    last_lined = in_order(last_terms, line_moves(last_terms, line), place, line)
    (early_half,) = hold([early_half], tip(last_lined))
    early_other = swap_cores(early_half)
    segments = [(3 * at + i * n, n, i, at) for at, n in spans for i in range(3)]
    g_gate_out, g_up_out, g_down_in = finish(
        core_place, early_half, early_other, (shard_hidden,) * 3, segments
    )
    last_own = gather_wsh(last_lined, shard_place, (tip(g_gate_out),))
    last_other = swap_cores(last_own)
    kv_rows = kv_width // (2 * line)
    segments = late_segments(late_terms.shape[0], last_terms.shape[0], 0, (width_rows,) * 5, 0)
    segments += late_segments(
        last_terms.shape[0] - late_terms.shape[0], last_terms.shape[0], late_terms.shape[0],
        (width_rows,) * 4 + (kv_rows,) * 2, 5,
    )
    (
        g_output_in, g_output_out, g_gate_in, g_up_in, g_down_out,
        g_query_in, g_query_out, g_key_in, g_value_in, g_key_out, g_value_out,
    ) = finish(
        core_place, last_own, last_other, (width_rows,) * 9 + (kv_rows,) * 2, segments
    )
    return (
        layer_out,
        input_grad,
        g_query_in,
        g_query_out,
        g_key_in,
        g_key_out,
        g_value_in,
        g_value_out,
        g_output_in,
        g_output_out,
        g_gate_in,
        g_gate_out,
        g_up_in,
        g_up_out,
        g_down_in,
        g_down_out,
    )


def solution(mesh):
    weight = P("wsh", "ctx")
    rows = P("wsh", "ctx", None)
    return jax.shard_map(
        local,
        mesh=mesh,
        in_specs=(rows, rows) + (P(),) * 4 + (weight,) * 7 + (P(),) * 17,
        out_specs=(rows, rows) + (P(),) * 14,
        check_vma=False,
    )
```

```python
import functools
import math

import jax
import jax.numpy as jnp
from jax import lax
from jax.experimental import pallas as pl
from jax.experimental.pallas import tpu as pltpu
from jax.sharding import PartitionSpec as P

HEAD_DIM = 128
PROMPT = 1024
CONTS = 4
CONT = 256
RANK = 16

norm_eps = 1e-06
adapter_scale = 0.5
rope_base = 1000000.0
masked_score = -1e30
score_scale = HEAD_DIM ** (-0.5)
score_to_log2 = score_scale * math.log2(math.e)

f32 = jnp.float32
bf16 = jnp.bfloat16
VMEM_LIMIT = 60 * 2**20


def nt(left, right):
    return lax.dot_general(left, right, (((1,), (1,)), ((), ())), preferred_element_type=f32)


def nn(left, right):
    return lax.dot_general(left, right, (((1,), (0,)), ((), ())), preferred_element_type=f32)


def tn(left, right):
    return lax.dot_general(left, right, (((0,), (0,)), ((), ())), preferred_element_type=f32)


def along_line(array, pairs):
    return lax.ppermute(array, "ctx", [(2 * a + c, 2 * b + c) for a, b in pairs for c in (0, 1)])


def swap_cores(array):
    size = lax.axis_size("ctx")
    return lax.ppermute(array, "ctx", [(i, i ^ 1) for i in range(size)])


def hold_kernel(*refs):
    pass


def hold(arrays, *after):
    anywhere = pl.BlockSpec(memory_space=pl.ANY)
    count = len(arrays)
    held = pl.pallas_call(
        hold_kernel,
        in_specs=[anywhere] * (count + len(after)),
        out_specs=[anywhere] * count,
        out_shape=[jax.ShapeDtypeStruct(a.shape, a.dtype) for a in arrays],
        input_output_aliases={i: i for i in range(count)},
        name="hold",
    )(*arrays, *after)
    return list(held)


def line_moves(piece, line):
    return [
        along_line(piece, [(i, (i + by) % line) for i in range(line)]) for by in range(1, line)
    ]


def in_order(piece, came, place, line):
    out = jnp.zeros((line,) + piece.shape, piece.dtype)
    out = lax.dynamic_update_index_in_dim(out, piece, place, 0)
    for by in range(1, line):
        out = lax.dynamic_update_index_in_dim(out, came[by - 1], (place - by) % line, 0)
    return out


def shard_gather(lined):
    return lax.all_gather(lined, "wsh", axis=0, tiled=False)


def add_up(arrays):
    return functools.reduce(jnp.add, [a.astype(f32) for a in arrays]).astype(bf16)


def line_outs(mine, place, line):
    return [
        lax.dynamic_index_in_dim(mine, (place + by) % line, 0, False) for by in range(1, line)
    ]


def line_send(outs, line):
    return [
        along_line(out, [(i, (i + by + 1) % line) for i in range(line)]) for by, out in enumerate(outs)
    ]


def line_sum(mine, place, came):
    return add_up([lax.dynamic_index_in_dim(mine, place, 0, False)] + came)


def across(array, by):
    size = lax.axis_size("wsh")
    return lax.ppermute(array, "wsh", [(i, i ^ by) for i in range(size)])


def wsh_outs(parts, shard):
    return [
        lax.dynamic_index_in_dim(parts, shard ^ by, 1, False) for by in range(1, parts.shape[1])
    ]


def wsh_send(outs):
    return [across(out, by + 1) for by, out in enumerate(outs)]


def wsh_sum(parts, shard, came):
    return add_up([lax.dynamic_index_in_dim(parts, shard, 1, False)] + came)


def tip(array):
    ends = (1,) * (array.ndim - 2) + (min(16, array.shape[-2]), min(128, array.shape[-1]))
    return lax.slice(array, (0,) * array.ndim, ends)


def gather_wsh(piece, shard, after=()):
    shards = lax.axis_size("wsh")
    came = [across(piece, by) for by in range(1, shards)]
    came = hold(came, *after) if after else came
    out = jnp.zeros((shards,) + piece.shape, piece.dtype)
    out = lax.dynamic_update_index_in_dim(out, piece, shard, 0)
    for by in range(1, shards):
        out = lax.dynamic_update_index_in_dim(out, came[by - 1], shard ^ by, 0)
    return out


def both_cores(half, other, core):
    return jnp.stack([jnp.where(core == 0, half, other), jnp.where(core == 0, other, half)])


def params(**more):
    return pltpu.CompilerParams(
        dimension_semantics=("arbitrary",), vmem_limit_bytes=VMEM_LIMIT, **more
    )


def whole(array):
    return pl.BlockSpec(array.shape, lambda s, *pre: (0,) * array.ndim)


def by_slot(array):
    return pl.BlockSpec((1,) + array.shape[1:], lambda s, *pre: (s,) + (0,) * (array.ndim - 1))


def second_by_slot(array):
    return pl.BlockSpec(
        (array.shape[0], 1) + array.shape[2:], lambda s, *pre: (0, s) + (0,) * (array.ndim - 2)
    )


def half_copies(core, own, other, parts, sems):
    copies = []
    shards, _, _, cols = own.shape
    for side, half in ((core, own), (1 - core, other)):
        for w in range(shards):
            for at, count, buffer in parts:
                copies.append(
                    pltpu.make_async_copy(
                        half.at[w, :, pl.ds(at, count), :],
                        buffer.at[:, side, :, pl.ds(w * cols, cols)],
                        sems.at[len(copies)],
                    )
                )
    return copies


def fetch_once(copies):
    @pl.when(pl.program_id(0) == 0)
    def _():
        for c in copies:
            c.start()
        for c in copies:
            c.wait()


def buffers(own, rows, width):
    line, shards = own.shape[1], own.shape[0]
    held = [pltpu.VMEM((line, 2, n, width), bf16) for n in rows]
    return held + [pltpu.SemaphoreType.DMA((2 * shards * len(rows),))]


def as_matrix(buffer):
    return buffer[...].reshape(-1, buffer.shape[-1])


anywhere = pl.BlockSpec(memory_space=pl.ANY)


def cost(flops, bytes_accessed, exps=0):
    return pl.CostEstimate(flops=int(flops), bytes_accessed=int(bytes_accessed), transcendentals=int(exps))


def slot_lanes(adapter, block, ranks):
    lane = lax.broadcasted_iota(jnp.int32, (block, ranks), 1)
    return lane // RANK == adapter[pl.program_id(0)]


def picked(mask, values):
    return jnp.where(mask, values, 0.0).astype(bf16)


def struct(shape, dtype):
    return jax.ShapeDtypeStruct(shape, dtype)


def turn(u, cos, sin):
    return u * cos + pltpu.roll(u, HEAD_DIM // 2, 1) * sin


def turn_back(u, cos, sin):
    return u * cos - pltpu.roll(u, HEAD_DIM // 2, 1) * sin


def key_value_kernel(
    first, adapter, core, own, other, tok, gain, bias, in_k, in_v, out_k, out_v, cosine, sine,
    normed_ref, rank_k_ref, rank_v_ref, kv_ref, key_w, value_w, sems,
):
    rows = key_w.shape[2]
    parts = ((first, rows, key_w), (first + rows, rows, value_w))
    fetch_once(half_copies(core[0], own, other, parts, sems))
    hidden = tok[0].astype(f32)
    inverse = lax.rsqrt(jnp.mean(hidden * hidden, axis=-1, keepdims=True) + norm_eps)
    normed = (hidden * inverse * gain[...]).astype(bf16)
    normed_ref[0] = normed
    mask = slot_lanes(adapter, normed.shape[0], in_k.shape[0])
    kv_width = kv_ref.shape[-1] // 2
    rank_k = picked(mask, nt(normed, in_k[...]))
    rank_v = picked(mask, nt(normed, in_v[...]))
    rank_k_ref[0], rank_v_ref[0] = rank_k, rank_v
    lin_k = nt(normed, as_matrix(key_w)) + bias[:, :kv_width]
    lin_v = nt(normed, as_matrix(value_w)) + bias[:, kv_width:]
    key = lin_k + adapter_scale * nn(rank_k, out_k[...])
    value = lin_v + adapter_scale * nn(rank_v, out_v[...])
    cos, sin = cosine[...], sine[...]
    for h in range(kv_width // HEAD_DIM):
        part = slice(h * HEAD_DIM, (h + 1) * HEAD_DIM)
        kv_ref[0, :, part] = turn(key[:, part], cos, sin).astype(bf16)
    kv_ref[0, :, kv_width:] = value.astype(bf16)


def key_value_side(adapter_of, core, own, other, first, tokens, gain, bias, adapters, cosine, sine):
    slots, block, width = tokens.shape
    kv_rows = bias.shape[1] // 4 // own.shape[1]
    shared = (gain, bias, *adapters, cosine, sine)
    ranks = struct((slots, block, adapters[0].shape[0]), bf16)
    outs = (struct(tokens.shape, bf16), ranks, ranks, struct((slots, block, bias.shape[1]), bf16))
    return pl.pallas_call(
        functools.partial(key_value_kernel, first),
        grid_spec=pltpu.PrefetchScalarGridSpec(
            num_scalar_prefetch=2,
            grid=(slots,),
            in_specs=[anywhere, anywhere, by_slot(tokens)] + [whole(a) for a in shared],
            out_specs=[by_slot(o) for o in outs],
            scratch_shapes=buffers(own, (kv_rows, kv_rows), width),
        ),
        out_shape=outs,
        compiler_params=params(),
        cost_estimate=cost(3 * slots * block * width * bias.shape[1], 12e6),
        name="key_value_side",
    )(adapter_of, core, own, other, tokens, *shared)


def query_kernel(
    adapter, core, own, other, normed, bias, in_q, out_q, cosine, sine, rank_ref, query_ref, weight, sems
):
    fetch_once(half_copies(core[0], own, other, ((0, weight.shape[2], weight),), sems))
    x = normed[0]
    mask = slot_lanes(adapter, x.shape[0], in_q.shape[0])
    rank = picked(mask, nt(x, in_q[...]))
    rank_ref[0] = rank
    query = nt(x, as_matrix(weight)) + bias[...] + adapter_scale * nn(rank, out_q[...])
    cos, sin = cosine[...], sine[...]
    for h in range(query.shape[1] // HEAD_DIM):
        part = slice(h * HEAD_DIM, (h + 1) * HEAD_DIM)
        query_ref[0, :, part] = turn(query[:, part], cos, sin).astype(bf16)


def query_side(adapter_of, core, own, other, normed, bias, adapters, cosine, sine):
    slots, block, width = normed.shape
    shared = (bias, *adapters, cosine, sine)
    outs = (struct((slots, block, adapters[0].shape[0]), bf16), struct(normed.shape, bf16))
    return pl.pallas_call(
        query_kernel,
        grid_spec=pltpu.PrefetchScalarGridSpec(
            num_scalar_prefetch=2,
            grid=(slots,),
            in_specs=[anywhere, anywhere, by_slot(normed)] + [whole(a) for a in shared],
            out_specs=[by_slot(o) for o in outs],
            scratch_shapes=buffers(own, (width // 2 // own.shape[1],), width),
        ),
        out_shape=outs,
        compiler_params=params(),
        cost_estimate=cost(2.5 * slots * block * width * width, 12e6),
        name="query_side",
    )(adapter_of, core, own, other, normed, *shared)


def attend_kernel(kv_heads, group, mates, flags, *refs):
    query, own, even, odd = refs[:4]
    mate = refs[4] if mates else None
    context_ref, mixed_ref, log_ref = refs[4 + mates :]
    block = query.shape[1]
    half = even.shape[0]
    kv_width = kv_heads * HEAD_DIM
    rows = lax.broadcasted_iota(jnp.int32, (block, block), 0)
    cols = lax.broadcasted_iota(jnp.int32, (block, block), 1)
    causal = rows <= cols
    bias = [jnp.where(flags[i] != 0, 0.0, masked_score) for i in range(2 * half + mates)]
    for kv in range(kv_heads):
        k_part = slice(kv * HEAD_DIM, (kv + 1) * HEAD_DIM)
        v_part = slice(kv_width + kv * HEAD_DIM, kv_width + (kv + 1) * HEAD_DIM)
        sources = [own[0]] + [even[i, 0] for i in range(half)] + [odd[i, 0] for i in range(half)]
        sources += [mate[0]] if mates else []
        keys = [s[:, k_part] for s in sources]
        values_t = [s[:, v_part].T for s in sources]
        for g in range(group):
            h = kv * group + g
            part = slice(h * HEAD_DIM, (h + 1) * HEAD_DIM)
            q = query[0, :, part]
            scores = [nt(k, q) for k in keys]
            scores[0] = jnp.where(causal, scores[0], masked_score)
            scores = scores[:1] + [s + b for s, b in zip(scores[1:], bias)]
            top = functools.reduce(jnp.maximum, [jnp.max(s, axis=0, keepdims=True) for s in scores])
            shift = top * score_to_log2
            total, mixed = 0.0, 0.0
            for s, v in zip(scores, values_t):
                p = jnp.exp2(s * score_to_log2 - shift)
                total = total + jnp.sum(p, axis=0, keepdims=True)
                mixed = mixed + nn(v, p.astype(bf16))
            mixed = mixed / total
            mixed_ref[0, h] = mixed
            log_ref[0, h : h + 1, :] = shift + jnp.log2(total)
            context_ref[0, :, part] = mixed.T.astype(bf16)


def attend(flags, query, own, even, odd, mate, kv_heads):
    slots, block, width = query.shape
    heads = width // HEAD_DIM
    mates = len(mate)
    operands = (query, own, even, odd, *mate)
    specs = [by_slot(query), by_slot(own), second_by_slot(even), second_by_slot(odd)]
    specs += [by_slot(m) for m in mate]
    outs = (
        struct((slots, block, width), bf16),
        struct((slots, heads, HEAD_DIM, block), f32),
        struct((slots, heads, block), f32),
    )
    return pl.pallas_call(
        functools.partial(attend_kernel, kv_heads, heads // kv_heads, mates),
        grid_spec=pltpu.PrefetchScalarGridSpec(
            num_scalar_prefetch=1, grid=(slots,), in_specs=specs, out_specs=[by_slot(o) for o in outs]
        ),
        out_shape=outs,
        compiler_params=params(),
        cost_estimate=cost(20e9, 20e6, slots * heads * block * (own.shape[1] * 5)),
        name="attend",
    )(flags, *operands)


def attend_back_kernel(kv_heads, group, mates, more, flags, *refs):
    refs = refs[more:]
    query, own, even, odd = refs[:4]
    mate = refs[4] if mates else None
    grad, mixed_ref, log_ref, cosine, sine = refs[4 + mates : 9 + mates]
    d_query, d_own, d_even, d_odd = refs[9 + mates : 13 + mates]
    d_mate = refs[13 + mates] if mates else None
    acc = refs[13 + 2 * mates]
    block = query.shape[1]
    half = even.shape[0]
    kv_width = kv_heads * HEAD_DIM
    rows = lax.broadcasted_iota(jnp.int32, (block, block), 0)
    cols = lax.broadcasted_iota(jnp.int32, (block, block), 1)
    causal = rows <= cols
    bias = [jnp.where(flags[i] != 0, 0.0, masked_score) for i in range(2 * half + mates)]
    cos, sin = cosine[...], sine[...]
    for kv in range(kv_heads):
        k_part = slice(kv * HEAD_DIM, (kv + 1) * HEAD_DIM)
        v_part = slice(kv_width + kv * HEAD_DIM, kv_width + (kv + 1) * HEAD_DIM)
        sources = [own[0]] + [even[i, 0] for i in range(half)] + [odd[i, 0] for i in range(half)]
        sources += [mate[0]] if mates else []
        keys = [s[:, k_part] for s in sources]
        keys_t = [k.T for k in keys]
        values = [s[:, v_part] for s in sources]
        for g in range(group):
            h = kv * group + g
            part = slice(h * HEAD_DIM, (h + 1) * HEAD_DIM)
            q = query[0, :, part]
            d_o = grad[0, :, part]
            delta = jnp.sum(d_o.astype(f32).T * mixed_ref[0, h], axis=0, keepdims=True)
            shift = log_ref[0, h : h + 1, :]
            d_q = 0.0
            for i in range(len(sources)):
                s = nt(keys[i], q)
                s = jnp.where(causal, s, masked_score) if i == 0 else s + bias[i - 1]
                p = jnp.exp2(s * score_to_log2 - shift)
                d_p = nt(values[i], d_o)
                d_s = (p * (d_p - delta)).astype(bf16)
                d_value = nn(p.astype(bf16), d_o)
                d_key = nn(d_s, q)
                if g == 0:
                    acc[i, :, v_part] = d_value
                    acc[i, :, k_part] = d_key
                else:
                    acc[i, :, v_part] += d_value
                    acc[i, :, k_part] += d_key
                d_q = d_q + nn(keys_t[i], d_s)
            u = d_q.T * score_scale
            d_query[0, :, part] = (u * cos - pltpu.roll(u, HEAD_DIM // 2, 1) * sin).astype(bf16)
    targets = [(d_own, 0)] + [(d_even, i) for i in range(half)] + [(d_odd, i) for i in range(half)]
    targets += [(d_mate, 0)] if mates else []
    for i, (target, j) in enumerate(targets):
        if target is d_own or target is d_mate:
            target[0, :, :kv_width] = (acc[i, :, :kv_width] * score_scale).astype(target.dtype)
            target[0, :, kv_width:] = acc[i, :, kv_width:].astype(target.dtype)
        else:
            target[j, 0, :, :kv_width] = (acc[i, :, :kv_width] * score_scale).astype(target.dtype)
            target[j, 0, :, kv_width:] = acc[i, :, kv_width:].astype(target.dtype)


def attend_back(flags, query, own, even, odd, mate, grad, mixed, logs, cosine, sine, kv_heads, start, slots, d_query=None):
    _, block, width = query.shape

    def by_slot(array):
        lead = array.ndim - 1
        return pl.BlockSpec((1,) + array.shape[1:], lambda s, *pre: (s + start,) + (0,) * lead)

    def second_by_slot(array):
        lead = array.ndim - 2
        shape = (array.shape[0], 1) + array.shape[2:]
        return pl.BlockSpec(shape, lambda s, *pre: (0, s + start) + (0,) * lead)

    def out_by_slot(array):
        return pl.BlockSpec((1,) + array.shape[1:], lambda s, *pre: (s,) + (0,) * (array.ndim - 1))

    def out_second(array):
        shape = (array.shape[0], 1) + array.shape[2:]
        return pl.BlockSpec(shape, lambda s, *pre: (0, s) + (0,) * (array.ndim - 2))

    heads = width // HEAD_DIM
    mates = len(mate)
    earlier = () if d_query is None else (d_query,)
    operands = (*earlier, query, own, even, odd, *mate, grad, mixed, logs, cosine, sine)
    specs = [anywhere] * len(earlier) + [by_slot(query), by_slot(own), second_by_slot(even), second_by_slot(odd)]
    specs += [by_slot(m) for m in mate]
    specs += [by_slot(grad), by_slot(mixed), by_slot(logs), whole(cosine), whole(sine)]
    outs = (
        struct(query.shape, bf16),
        struct((slots,) + own.shape[1:], f32),
        struct((even.shape[0], slots) + even.shape[2:], bf16),
        struct((odd.shape[0], slots) + odd.shape[2:], bf16),
        *(struct((slots,) + m.shape[1:], bf16) for m in mate),
    )
    out_specs = [by_slot(outs[0]), out_by_slot(outs[1]), out_second(even), out_second(odd)]
    out_specs += [out_by_slot(m) for m in mate]
    count = 1 + 2 * even.shape[0] + mates
    return pl.pallas_call(
        functools.partial(attend_back_kernel, kv_heads, heads // kv_heads, mates, len(earlier)),
        grid_spec=pltpu.PrefetchScalarGridSpec(
            num_scalar_prefetch=1,
            grid=(slots,),
            in_specs=specs,
            out_specs=out_specs,
            scratch_shapes=[pltpu.VMEM((count,) + own.shape[1:], f32)],
        ),
        out_shape=outs,
        input_output_aliases={1: 0} if earlier else {},
        compiler_params=params(),
        cost_estimate=cost(25e9, 20e6, slots * heads * block * (own.shape[1] * 5)),
        name="attend_back",
    )(flags, *operands)


def middle_kernel(
    first, adapter, live, core, own, other, context, tok, cot, in_o, out_o, gain, in_g, in_u, out_d,
    mid_ref, normed_ref, grad_ref, rank_o_ref, rank_g_ref, rank_u_ref, grad_rank_ref, weight, sems,
):
    fetch_once(half_copies(core[0], own, other, ((first, weight.shape[2], weight),), sems))
    s = pl.program_id(0)
    ctx = context[0]
    mask = slot_lanes(adapter, ctx.shape[0], in_o.shape[0])
    rank = picked(mask, nt(ctx, in_o[...]))
    rank_o_ref[0] = rank
    mid = tok[0].astype(f32) + nt(ctx, as_matrix(weight)) + adapter_scale * nn(rank, out_o[...])
    mid_ref[0] = mid
    inverse = lax.rsqrt(jnp.mean(mid * mid, axis=-1, keepdims=True) + norm_eps)
    normed = (mid * inverse * gain[...]).astype(bf16)
    normed_ref[0] = normed
    rank_g_ref[0] = picked(mask, nt(normed, in_g[...]))
    rank_u_ref[0] = picked(mask, nt(normed, in_u[...]))
    on = jnp.where(live[s] != 0, 1.0, 0.0)
    grad = (cot[0].astype(f32) * on).astype(bf16)
    grad_ref[0] = grad
    grad_rank_ref[0] = picked(mask, adapter_scale * nt(grad, out_d[...]))


def middle_side(adapter_of, live, core, own, other, first, context, tokens, cotangent, in_o, out_o, gain,
                in_g, in_u, out_d):
    slots, block, width = tokens.shape
    shared = (in_o, out_o, gain, in_g, in_u, out_d)
    rank = struct((slots, block, in_o.shape[0]), bf16)
    wide = struct(tokens.shape, bf16)
    outs = (struct(tokens.shape, f32), wide, wide, rank, rank, rank, rank)
    return pl.pallas_call(
        functools.partial(middle_kernel, first),
        grid_spec=pltpu.PrefetchScalarGridSpec(
            num_scalar_prefetch=3,
            grid=(slots,),
            in_specs=[anywhere, anywhere]
            + [by_slot(a) for a in (context, tokens, cotangent)]
            + [whole(a) for a in shared],
            out_specs=[by_slot(o) for o in outs],
            scratch_shapes=buffers(own, (width // 2 // own.shape[1],), width),
        ),
        out_shape=outs,
        compiler_params=params(),
        cost_estimate=cost(3 * slots * block * width * width, 28e6),
        name="middle_side",
    )(adapter_of, live, core, own, other, context, tokens, cotangent, *shared)


def feed_copies(half, gate, up, down, sems, base):
    copies = []

    def add(source, target):
        copies.append(pltpu.make_async_copy(source, target, sems.at[base + len(copies)]))

    shards, line, rows, cols = half.shape
    rows //= 3
    for w in range(shards):
        span = pl.ds(w * cols, cols)
        add(half.at[w, :, pl.ds(0, rows), :], gate.at[:, :, span])
        add(half.at[w, :, pl.ds(rows, rows), :], up.at[:, :, span])
    last = pl.ds(2 * rows, rows)
    if shards == 1:
        add(half.at[0, :, last, :], down)
    else:
        for w in range(shards):
            for z in range(line):
                add(half.at[w, z, last, :], down.at[w, :, pl.ds(z * cols, cols)])
    return copies


def feed_kernel(first, count, span, core, *refs):
    halves, refs = refs[:count], refs[count:]
    x_ref, g_ref, rank_d, rank_g, rank_u = refs[:5]
    adapters, refs = refs[5 : 5 + 3 * count], refs[5 + 3 * count :]
    if first:
        sums_in = None
    else:
        sums_in, refs = refs[:5], refs[5:]
    sums_out, terms, refs = refs[:5], refs[5 : 5 + count], refs[5 + count :]
    weights, accs, sems = refs[: 3 * count], refs[3 * count : 4 * count], refs[4 * count]
    s = pl.program_id(0)
    copies, base = [], 0
    for i in range(count):
        copies.append(feed_copies(halves[i], *weights[3 * i : 3 * i + 3], sems, base))
        base += len(copies[-1])

    @pl.when(s == 0)
    def _():
        for group in copies:
            for c in group:
                c.start()
        for acc in accs:
            acc[...] = jnp.zeros_like(acc)

    x, g = x_ref[0], g_ref[0]
    r_d, r_g, r_u = rank_d[0], rank_g[0], rank_u[0]
    sums = [0.0] * 5 if first else [r[0] for r in sums_in]
    for i in range(count):

        @pl.when(s == 0)
        def _(i=i):
            for c in copies[i]:
                c.wait()

        gate_m, up_m, down_m = (as_matrix(b) for b in weights[3 * i : 3 * i + 3])
        in_d, out_g, out_u = (a[0] for a in adapters[3 * i : 3 * i + 3])
        acc = accs[i]
        hidden = gate_m.shape[0]
        for at in range(0, hidden, span):
            part = slice(at, min(at + span, hidden))
            o_g, o_u, i_d = out_g[part], out_u[part], in_d[part]
            w_g, w_u, w_d = gate_m[part], up_m[part], down_m[part]
            gate = nt(x, w_g) + adapter_scale * nt(r_g, o_g)
            up = nt(x, w_u) + adapter_scale * nt(r_u, o_u)
            d_act = nt(g, w_d) + nt(r_d, i_d)
            sig = 1.0 / (1.0 + jnp.exp(-gate))
            lit = gate * sig
            act = (lit * up).astype(bf16)
            d_gate = (d_act * up * sig * (1.0 + gate * (1.0 - sig))).astype(bf16)
            d_up = (d_act * lit).astype(bf16)
            sums[0] = sums[0] + nn(act, w_d)
            sums[1] = sums[1] + nn(d_gate, w_g) + nn(d_up, w_u)
            sums[2] = sums[2] + nn(act, i_d)
            sums[3] = sums[3] + nn(d_gate, o_g)
            sums[4] = sums[4] + nn(d_up, o_u)
            acc[0, :, part] += tn(r_g, d_gate)
            acc[1, :, part] += tn(r_u, d_up)
            acc[2, :, part] += tn(r_d, act)
    for ref, value in zip(sums_out, sums):
        ref[0] = value

    @pl.when(s == pl.num_programs(0) - 1)
    def _():
        for i in range(count):
            line, rows, _ = weights[3 * i].shape
            for j, scale in enumerate((adapter_scale, adapter_scale, 1.0)):
                turned = (accs[i][j] * scale).T.astype(bf16)
                for z in range(line):
                    terms[i][z, j * rows : (j + 1) * rows, :] = turned[z * rows : (z + 1) * rows]


def feed_part(core, halves, normed, grad, ranks, sums):
    slots, block, width = normed.shape
    rank_width = ranks[0].shape[-1]
    count = len(halves)
    first = sums is None
    operands = [h[0] for h in halves] + [normed, grad, *ranks]
    specs = [anywhere] * count + [by_slot(a) for a in (normed, grad, *ranks)]
    for _, of_other, adapters in halves:
        for a in adapters:
            operands.append(a)
            side = (lambda s, c: (1 - c[0], 0, 0)) if of_other else (lambda s, c: (c[0], 0, 0))
            specs.append(pl.BlockSpec((1,) + a.shape[1:], side))
    aliases = {}
    if not first:
        aliases = {1 + len(operands) + i: i for i in range(len(sums))}
        operands += list(sums)
        specs += [by_slot(a) for a in sums]
    rank_sum = struct((slots, block, rank_width), f32)
    wide_sum = struct((slots, block, width), f32)
    outs = [wide_sum, wide_sum, rank_sum, rank_sum, rank_sum]
    out_specs = [by_slot(o) for o in outs]
    scratch, hidden, copies = [], 0, 0
    for half, _, _ in halves:
        shards, line, rows = half.shape[:3]
        terms = struct((line, rows, rank_width), bf16)
        outs.append(terms)
        out_specs.append(whole(terms))
        scratch += [pltpu.VMEM((line, rows // 3, width), bf16)] * 3
        hidden += line * rows // 3
        copies += 2 * shards + (1 if shards == 1 else shards * line)
    for half, _, _ in halves:
        scratch.append(pltpu.VMEM((3, rank_width, half.shape[1] * half.shape[2] // 3), f32))
    return pl.pallas_call(
        functools.partial(feed_kernel, first, count, 512),
        grid_spec=pltpu.PrefetchScalarGridSpec(
            num_scalar_prefetch=1,
            grid=(slots,),
            in_specs=specs,
            out_specs=out_specs,
            scratch_shapes=scratch + [pltpu.SemaphoreType.DMA((copies,))],
        ),
        out_shape=outs,
        input_output_aliases=aliases,
        compiler_params=params(),
        cost_estimate=cost(20 * slots * block * hidden * width, 60e6, slots * block * hidden),
        name="feed_part",
    )(core, *operands)


def rms_back(hidden, gain, grad_normed):
    scaled = grad_normed * gain
    inverse = lax.rsqrt(jnp.mean(hidden * hidden, axis=-1, keepdims=True) + norm_eps)
    return inverse * scaled - hidden * (inverse * inverse * inverse) * jnp.mean(
        scaled * hidden, axis=-1, keepdims=True
    )


def keep_terms(acc, out, core, terms):
    s = pl.program_id(0)

    @pl.when(s == 0)
    def _():
        at = 0
        for t in terms:
            acc[:, at : at + t.shape[1]] = t
            at += t.shape[1]

    @pl.when(s != 0)
    def _():
        at = 0
        for t in terms:
            acc[:, at : at + t.shape[1]] += t
            at += t.shape[1]

    @pl.when(s == pl.num_programs(0) - 1)
    def _():
        line = out.shape[1]
        at, row = 0, 0
        for t in terms:
            n = t.shape[1]
            cut = n // (2 * line)
            turned = acc[:, at : at + n].T.astype(bf16)
            for z in range(line):
                for side in (0, 1):
                    block = turned[(2 * z + side) * cut : (2 * z + side + 1) * cut]
                    out[jnp.where(core == side, 0, 1), z, row : row + cut, :] = block
            at += n
            row += cut


def turned_terms(line, columns, ranks):
    return struct((2, line, columns // (2 * line), ranks), bf16)


def return_kernel(
    first, adapter, live, core, own, other, y, dx, sum_d, sum_g, sum_u, mid_in, normed, grad, context,
    rank_o, in_o, out_o, gain, in_g, in_u, out_d, layer_ref, d_mid_ref, d_ctx_ref, terms_ref, acc,
    weight, sems,
):
    fetch_once(half_copies(core[0], own, other, ((first, weight.shape[2], weight),), sems))
    s = pl.program_id(0)
    on = jnp.where(live[s] != 0, 1.0, 0.0)
    mid = mid_in[0]
    g = grad[0]
    mask = slot_lanes(adapter, g.shape[0], in_o.shape[0])
    rank_down = picked(mask, sum_d[0])
    result = mid + y[0] + adapter_scale * nn(rank_down, out_d[...])
    layer_ref[0] = (result * on).astype(bf16)
    back_g = picked(mask, adapter_scale * sum_g[0])
    back_u = picked(mask, adapter_scale * sum_u[0])
    d_normed = dx[0] + nn(back_g, in_g[...]) + nn(back_u, in_u[...])
    d_mid = g.astype(f32) + rms_back(mid, gain[...], d_normed)
    d_mid_ref[0] = d_mid
    branch = d_mid.astype(bf16)
    back_o = picked(mask, adapter_scale * nt(branch, out_o[...]))
    d_ctx_ref[0] = (nn(branch, as_matrix(weight)) + nn(back_o, in_o[...])).astype(bf16)
    x = normed[0]
    keep_terms(
        acc,
        terms_ref,
        core[0],
        (
            tn(back_o, context[0]),
            adapter_scale * tn(rank_o[0], branch),
            tn(back_g, x),
            tn(back_u, x),
            adapter_scale * tn(rank_down, g),
        ),
    )


def return_side(adapter_of, live, core, own, other, first, sums, mid, normed, grad, context, rank_o, in_o,
                out_o, gain, in_g, in_u, out_d):
    slots, block, width = mid.shape
    rows = (*sums, mid, normed, grad, context, rank_o)
    shared = (in_o, out_o, gain, in_g, in_u, out_d)
    ranks = in_o.shape[0]
    outs = (
        struct(mid.shape, bf16),
        struct(mid.shape, f32),
        struct(mid.shape, bf16),
        turned_terms(own.shape[1], 5 * width, ranks),
    )
    return pl.pallas_call(
        functools.partial(return_kernel, first),
        grid_spec=pltpu.PrefetchScalarGridSpec(
            num_scalar_prefetch=3,
            grid=(slots,),
            in_specs=[anywhere, anywhere] + [by_slot(r) for r in rows] + [whole(a) for a in shared],
            out_specs=[by_slot(o) for o in outs[:3]] + [whole(outs[3])],
            scratch_shapes=[pltpu.VMEM((ranks, 5 * width), f32)]
            + buffers(own, (width // 2 // own.shape[1],), width),
        ),
        out_shape=outs,
        compiler_params=params(),
        cost_estimate=cost(4 * slots * block * width * width, 50e6),
        name="return_side",
    )(adapter_of, live, core, own, other, *rows, *shared)


def query_back_kernel(
    adapter, core, own, other, d_query, normed, rank_q, in_q, out_q, d_normed_ref, terms_ref, acc,
    weight, sems,
):
    fetch_once(half_copies(core[0], own, other, ((0, weight.shape[2], weight),), sems))
    g, x = d_query[0], normed[0]
    mask = slot_lanes(adapter, g.shape[0], in_q.shape[0])
    rank_back = picked(mask, adapter_scale * nt(g, out_q[...]))
    d_normed_ref[0] = nn(g, as_matrix(weight)) + nn(rank_back, in_q[...])
    keep_terms(acc, terms_ref, core[0], (tn(rank_back, x), adapter_scale * tn(rank_q[0], g)))


def query_back_side(adapter_of, core, own, other, d_query, normed, rank_q, in_q, out_q):
    slots, block, width = normed.shape
    ranks = in_q.shape[0]
    rows = (d_query, normed, rank_q)
    shared = (in_q, out_q)
    outs = (struct(normed.shape, f32), turned_terms(own.shape[1], 2 * width, ranks))
    return pl.pallas_call(
        query_back_kernel,
        grid_spec=pltpu.PrefetchScalarGridSpec(
            num_scalar_prefetch=2,
            grid=(slots,),
            in_specs=[anywhere, anywhere] + [by_slot(r) for r in rows] + [whole(a) for a in shared],
            out_specs=[by_slot(outs[0]), whole(outs[1])],
            scratch_shapes=[pltpu.VMEM((ranks, 2 * width), f32)]
            + buffers(own, (width // 2 // own.shape[1],), width),
        ),
        out_shape=outs,
        compiler_params=params(),
        cost_estimate=cost(3 * slots * block * width * width, 22e6),
        name="query_back_side",
    )(adapter_of, core, own, other, *rows, *shared)


def output_kernel(
    first, adapter, live, core, own, other, d_kv, d_normed_q, d_mid, normed, rank_k, rank_v, tok, gain,
    cosine, sine, in_k, in_v, out_k, out_v, grad_ref, terms_ref, acc, key_w, value_w, sems,
):
    count = key_w.shape[2]
    parts = ((first, count, key_w), (first + count, count, value_w))
    fetch_once(half_copies(core[0], own, other, parts, sems))
    s = pl.program_id(0)
    on = jnp.where(live[s] != 0, 1.0, 0.0)
    kv_width = d_kv.shape[-1] // 2
    cos, sin = cosine[...], sine[...]
    back = d_kv[0]
    x = normed[0]
    mask = slot_lanes(adapter, x.shape[0], in_k.shape[0])
    keys = []
    for h in range(kv_width // HEAD_DIM):
        keys.append(turn_back(back[:, h * HEAD_DIM : (h + 1) * HEAD_DIM], cos, sin).astype(bf16))
    g_k, g_v = jnp.concatenate(keys, axis=1), back[:, kv_width:].astype(bf16)
    back_k = picked(mask, adapter_scale * nt(g_k, out_k[...]))
    back_v = picked(mask, adapter_scale * nt(g_v, out_v[...]))
    d_normed = d_normed_q[0] + nn(g_k, as_matrix(key_w)) + nn(g_v, as_matrix(value_w))
    d_normed = d_normed + nn(back_k, in_k[...]) + nn(back_v, in_v[...])
    hidden = tok[0].astype(f32)
    d_hidden = d_mid[0] + rms_back(hidden, gain[...], d_normed)
    grad_ref[0] = (d_hidden * on).astype(bf16)
    keep_terms(
        acc,
        terms_ref,
        core[0],
        (
            tn(back_k, x),
            tn(back_v, x),
            adapter_scale * tn(rank_k[0], g_k),
            adapter_scale * tn(rank_v[0], g_v),
        ),
    )


def output_side(adapter_of, live, core, own, other, first, d_kv, d_normed_q, d_mid, normed, rank_k, rank_v,
                tokens, gain, cosine, sine, adapters):
    slots, block, width = tokens.shape
    ranks = adapters[0].shape[0]
    kv_columns = d_kv.shape[-1]
    columns = 2 * width + kv_columns
    kv_rows = kv_columns // 4 // own.shape[1]
    rows = (d_kv, d_normed_q, d_mid, normed, rank_k, rank_v, tokens)
    shared = (gain, cosine, sine, *adapters)
    outs = (struct(tokens.shape, bf16), turned_terms(own.shape[1], columns, ranks))
    return pl.pallas_call(
        functools.partial(output_kernel, first),
        grid_spec=pltpu.PrefetchScalarGridSpec(
            num_scalar_prefetch=3,
            grid=(slots,),
            in_specs=[anywhere, anywhere] + [by_slot(r) for r in rows] + [whole(a) for a in shared],
            out_specs=[by_slot(outs[0]), whole(outs[1])],
            scratch_shapes=[pltpu.VMEM((ranks, columns), f32)]
            + buffers(own, (kv_rows, kv_rows), width),
        ),
        out_shape=outs,
        compiler_params=params(),
        cost_estimate=cost(3 * slots * block * width * kv_columns, 30e6),
        name="output_side",
    )(adapter_of, live, core, own, other, *rows, *shared)


def hop_up(array, t, line):
    half = line // 2
    return along_line(array, [(z, z - 1) for z in range(1, line) if half <= z + t - 1 < line])


def hops_down(mine, line):
    half = line // 2
    moved = [mine]
    for t in range(1, half):
        pairs = [(z, z + 1) for z in range(line - 1) if half <= z - t + 1]
        moved.append(along_line(moved[-1], pairs))
    return moved


def prompt_blocks(from_above, from_below, place, line):
    half = line // 2
    mine = from_above[0]
    blocks = []
    for b in range(half, line):
        out = mine
        for z in range(line):
            if z < b:
                out = jnp.where(place == z, from_above[b - z], out)
            elif z > b:
                out = jnp.where(place == z, from_below[z - b], out)
        blocks.append(out)
    return jnp.stack(blocks)


def take(blocks, at):
    return lax.dynamic_index_in_dim(blocks, jnp.clip(at, 0, blocks.shape[0] - 1), 0, False)


def fold_blocks(parts, line):
    half = line // 2
    return [along_line(parts, [(z, half - 1)]) for z in range(half - 1)]


def return_blocks(parts, total, place, line):
    half = line // 2
    came = []
    for b in range(half, line):
        came.append(along_line(total[b - half], [(half - 1, b)]))
    for by in range(1, half):
        pairs = [(z, z - by) for z in range(half + by, line)]
        came.append(along_line(take(parts, place - by - half), pairs))
    return came


def owned_blocks(parts, came, place, line):
    half = line // 2
    total = functools.reduce(jnp.add, [c.astype(f32) for c in came])
    total = total + take(parts, place - half).astype(f32)
    return jnp.where(place >= half, total, 0.0)


def finish_kernel(places, segments, core, own, other, *refs):
    count = len(places)
    outs, buffers, sems = refs[:count], refs[count : 2 * count], refs[2 * count]
    shards, line, rows, _ = own.shape
    copies = []
    for side, half in ((core[0], own), (1 - core[0], other)):
        for at, n, to, offset in segments:
            while n:
                w, row = at // rows, at % rows
                take = min(n, rows - row)
                for z in range(line):
                    start = pl.multiple_of((2 * z + side) * places[to] + offset, 16)
                    copies.append(
                        pltpu.make_async_copy(
                            half.at[w, z, pl.ds(row, take), :],
                            buffers[to].at[pl.ds(start, take), :],
                            sems.at[len(copies)],
                        )
                    )
                at, n, offset = at + take, n - take, offset + take
    for c in copies:
        c.start()
    for c in copies:
        c.wait()
    for out, buffer in zip(outs, buffers):
        total = buffer.shape[0]
        step = next(d for d in (1280, 768, 256) if total % d == 0)
        for at in range(0, total, step):
            block = buffer[at : at + step, :].astype(f32).T
            out[:, :, at : at + step] = block.reshape(out.shape[:2] + (step,))


def finish(core, own, other, places, segments):
    shards, line, rows, ranks = own.shape
    outs = [struct((ranks // RANK, RANK, 2 * line * p), f32) for p in places]
    pieces = 0
    for at, n, _, _ in segments:
        pieces += (at + n - 1) // rows - at // rows + 1
    return pl.pallas_call(
        functools.partial(finish_kernel, places, segments),
        grid_spec=pltpu.PrefetchScalarGridSpec(
            num_scalar_prefetch=1,
            grid=(1,),
            in_specs=[anywhere, anywhere],
            out_specs=[whole(o) for o in outs],
            scratch_shapes=[pltpu.VMEM((2 * line * p, ranks), bf16) for p in places]
            + [pltpu.SemaphoreType.DMA((2 * line * pieces,))],
        ),
        out_shape=outs,
        compiler_params=params(),
        name="finish",
    )(core, own, other)


def split_rows(mine, shards):
    n = mine.shape[1]
    padded = jnp.pad(mine, ((0, 0), (0, -n % (16 * shards)), (0, 0)))
    return padded.reshape(mine.shape[0], shards, -1, mine.shape[2])


def late_segments(rows, pitch, shift, counts, first):
    segments, at = [], 0
    for i, n in enumerate(counts):
        done = 0
        while done < n:
            w, row = (at + done) // rows, (at + done) % rows
            take = min(n - done, rows - row)
            segments.append((w * pitch + shift + row, take, first + i, done))
            done += take
        at += n
    return segments


def pack_kernel(spans, core, gate, up, down, given, *outs):
    kept = down[core[0]]
    came = given[...]
    first = jnp.where(core[0] == 0, kept, came)
    second = jnp.where(core[0] == 0, came, kept)
    turned = (gate[...].T, up[...].T, jnp.concatenate([first, second], axis=1))
    for out, (at, n) in zip(outs, spans):
        for i, t in enumerate(turned):
            out[i * n : (i + 1) * n, :] = t[at : at + n]


def pack_weights(spans, core, gate, up, down, given):
    outs = [struct((3 * n, gate.shape[0]), bf16) for _, n in spans]
    return pl.pallas_call(
        functools.partial(pack_kernel, spans),
        grid_spec=pltpu.PrefetchScalarGridSpec(
            num_scalar_prefetch=1,
            grid=(1,),
            in_specs=[whole(a) for a in (gate, up, down, given)],
            out_specs=[whole(o) for o in outs],
        ),
        out_shape=outs,
        compiler_params=params(),
        cost_estimate=cost(0, 12e6),
        name="pack_weights",
    )(core, gate, up, down, given)


def order_kernel(spans, line, wide, *outs):
    scratch = outs[-1]
    hidden = wide.shape[1]
    step = next(d for d in (1280, 256) if hidden % d == 0)
    for at in range(0, hidden, step):
        scratch[at : at + step, :] = wide[:, at : at + step].T
    shard = hidden // (2 * line)
    for out, (at, n) in zip(outs, spans):
        for z in range(line):
            for side in (0, 1):
                start = (2 * z + side) * shard + at
                out[side, z * n : (z + 1) * n, :] = scratch[start : start + n, :]


def order_adapters(spans, line, wide):
    ranks, hidden = wide.shape
    outs = [struct((2, line * n, ranks), bf16) for _, n in spans]
    return pl.pallas_call(
        functools.partial(order_kernel, spans, line),
        out_shape=outs,
        scratch_shapes=[pltpu.VMEM((hidden, ranks), bf16)],
        compiler_params=pltpu.CompilerParams(vmem_limit_bytes=VMEM_LIMIT),
        cost_estimate=cost(0, 5e6),
        name="order_adapters",
    )(wide)


def local(
    tokens,
    cotangent,
    group_slot,
    group_adapter,
    attn_gain,
    mlp_gain,
    w_query,
    w_key,
    w_value,
    w_output,
    w_gate,
    w_up,
    w_down,
    query_bias,
    key_bias,
    value_bias,
    adapt_query_in,
    adapt_query_out,
    adapt_key_in,
    adapt_key_out,
    adapt_value_in,
    adapt_value_out,
    adapt_output_in,
    adapt_output_out,
    adapt_gate_in,
    adapt_gate_out,
    adapt_up_in,
    adapt_up_out,
    adapt_down_in,
    adapt_down_out,
):
    slots, block, width = tokens.shape
    ctx_size, shards = lax.axis_size("ctx"), lax.axis_size("wsh")
    line = ctx_size // 2
    ctx_place, shard_place = lax.axis_index("ctx"), lax.axis_index("wsh")
    place, core = ctx_place // 2, ctx_place % 2
    kv_width = key_bias.shape[0]
    kv_heads = kv_width // HEAD_DIM
    hidden = adapt_gate_out.shape[-1]
    if line != shards or (CONTS * CONT) != line * block or CONT // block > 2:
        raise ValueError("unsupported mesh")
    mates = CONT // block - 1

    slot_ids = shard_place * slots + jnp.arange(slots, dtype=jnp.int32)
    matches = group_slot[None, :] == slot_ids[:, None]
    live = jnp.any(matches, axis=1).astype(jnp.int32)
    adapter_of = jnp.sum(jnp.where(matches, group_adapter[None, :], 0), axis=1).astype(jnp.int32)
    index = ctx_place * block + jnp.arange(block, dtype=jnp.int32)
    position = jnp.where(index >= CONTS * CONT, index - CONTS * CONT, PROMPT + index % CONT)
    frequency = rope_base ** (-(jnp.arange(HEAD_DIM // 2, dtype=f32) * 2.0) / HEAD_DIM)
    angles = position.astype(f32)[:, None] * frequency[None, :]
    cosine = jnp.concatenate([jnp.cos(angles), jnp.cos(angles)], axis=-1)
    sine = jnp.concatenate([-jnp.sin(angles), jnp.sin(angles)], axis=-1)

    is_cont = ctx_place < line
    of_side = [2 * (line // 2 + i) + core for i in range(line // 2)]
    of_other = [2 * (line // 2 + i) + 1 - core for i in range(line // 2)]
    flags = [(is_cont | (b < ctx_place)) for b in of_side + of_other]
    flags += [is_cont & (core == 1)] if mates else []
    flags = jnp.stack(flags).astype(jnp.int32)

    def wide(half):
        if half.shape[-1] % 128 == 0:
            return half
        return jnp.transpose(half, (1, 2, 0, 3)).reshape(1, line, half.shape[2], width)

    def wide_feed(half):
        if half.shape[-1] % 128 == 0:
            return half
        split = half.shape[2] // 3 * 2
        out_in = jnp.transpose(half[:, :, :split], (1, 2, 0, 3)).reshape(1, line, split, width)
        in_out = jnp.transpose(half[:, :, split:], (0, 2, 1, 3)).reshape(1, line, split // 2, width)
        return jnp.concatenate([out_in, in_out], axis=2)

    q_rows = w_query.shape[1]
    o_at = q_rows
    kv_piece = jnp.concatenate([w_key.T, w_value.T], axis=0)
    qo_piece = jnp.concatenate([w_query.T, w_output.T], axis=0)
    kv_moves = line_moves(kv_piece, line)
    qo_moves = line_moves(qo_piece, line)

    shard_hidden = w_gate.shape[1]
    unit = shard_hidden // 35
    part_rows = [8 * unit, 8 * unit, 9 * unit, 6 * unit, 4 * unit]
    part_at = [sum(part_rows[:i]) for i in range(len(part_rows))]
    parts = len(part_rows)
    spans = list(zip(part_at, part_rows))
    core_place = core.astype(jnp.int32)[None]
    down_halves = w_down.reshape(2, shard_hidden, w_down.shape[1])
    given = swap_cores(lax.dynamic_index_in_dim(down_halves, 1 - core, 0, False))
    pieces = pack_weights(spans, core_place, w_gate, w_up, down_halves, given)
    pieces = list(pieces)

    lined_kv = in_order(kv_piece, kv_moves, place, line)
    down_in, gate_out, up_out = (
        order_adapters(spans, line, a.reshape(-1, a.shape[-1]))
        for a in (adapt_down_in, adapt_gate_out, adapt_up_out)
    )
    kv_half = gather_wsh(lined_kv, shard_place)
    kv_own, kv_other = wide(kv_half), wide(swap_cores(kv_half))
    lined_qo = in_order(qo_piece, hold(qo_moves, pieces[0]), place, line)
    qo_half = shard_gather(lined_qo)

    def flat(adapters):
        return adapters.reshape(-1, adapters.shape[-1])

    query_in, key_in, value_in, output_in, gate_in, up_in = (
        flat(a)
        for a in (adapt_query_in, adapt_key_in, adapt_value_in, adapt_output_in, adapt_gate_in, adapt_up_in)
    )
    query_out, key_out, value_out, output_out, down_out = (
        flat(a)
        for a in (adapt_query_out, adapt_key_out, adapt_value_out, adapt_output_out, adapt_down_out)
    )

    gain_one = attn_gain.astype(f32)[None, :]
    gain_two = mlp_gain.astype(f32)[None, :]
    q_bias = query_bias.astype(f32)[None, :]
    kv_bias = jnp.concatenate([key_bias, value_bias]).astype(f32)[None, :]

    lined, halves = [], []

    def take_in(moves, group, *after):
        moves, at = hold(moves, *after), 0
        for i in group:
            n = pieces[i].shape[0]
            came = [m[at : at + n] for m in moves]
            lined.append(in_order(pieces[i], came, place, line))
            halves.append(shard_gather(lined[-1]))
            at += n

    def set_out(group, *after):
        together = hold([pieces[i] for i in group], *after)
        piece = jnp.concatenate(together, axis=0) if len(group) > 1 else together[0]
        return piece, line_moves(piece, line)

    _, moves = set_out([0], lined_qo)
    take_in(moves, [0], tip(kv_half))
    piece, moves = set_out([1], lined[0])
    (kv_own,) = hold([kv_own], piece)
    attn_kv = (core_place, kv_own, kv_other)
    kv_adapters = (key_in, value_in, key_out, value_out)
    normed, rank_k, rank_v, key_value = key_value_side(
        adapter_of, *attn_kv, 0, tokens, gain_one, kv_bias, kv_adapters, cosine, sine
    )
    hops = [key_value, hop_up(key_value, 1, line)]
    below = hops_down(key_value, line)
    mate = (swap_cores(key_value),) if mates else ()
    hops.append(hop_up(hops[1], 2, line))
    for t in range(3, line):
        hops.append(hop_up(hops[-1], t, line))
    (qo_half,) = hold([qo_half], tip(hops[2]))
    attn = (core_place, wide(qo_half), wide(swap_cores(qo_half)))
    rank_q, queries = query_side(
        adapter_of, *attn, normed, q_bias, (query_in, query_out), cosine, sine
    )
    side = prompt_blocks(hops, below, place, line)
    other_side = swap_cores(side)
    take_in(moves, [1], tip(side), *down_in, *gate_out, *up_out)
    piece, moves = set_out([2], lined[1])
    (queries,) = hold([queries], piece)
    context, mixed, logs = attend(flags, queries, key_value, side, other_side, mate, kv_heads)
    take_in(moves, [2], context)
    piece, moves = set_out([3], lined[2])
    (context,) = hold([context], piece)
    mid, normed2, grad_out, rank_o, rank_g, rank_u, rank_d = middle_side(
        adapter_of, live, *attn, o_at, context, tokens, cotangent, output_in, output_out, gain_two,
        gate_in, up_in, down_out,
    )

    sums, own_terms, other_terms, others = None, [], [], []
    before = normed2
    for i in range(parts + 1):
        if 0 < i < 3:
            take_in(moves, [i + 2], before)
            if i + 3 < parts:
                _, moves = set_out([i + 3], lined[i + 2])
        if i < parts:
            (halves[i],) = hold([halves[i]], before, lined[-1])
            others.append(swap_cores(halves[i]))
        use = []
        if i < parts:
            use.append((wide_feed(halves[i]), False, (down_in[i], gate_out[i], up_out[i])))
        if i:
            j = i - 1
            use.append((wide_feed(others[j]), True, (down_in[j], gate_out[j], up_out[j])))
        done = feed_part(core_place, use, normed2, grad_out, (rank_d, rank_g, rank_u), sums)
        sums, terms = done[:5], done[5:]
        if i < parts:
            own_terms.append(terms[0])
        if i:
            other_terms.append(terms[-1])
        before = sums[2]
    early_keep = jnp.concatenate(own_terms, axis=1)
    early_came = swap_cores(jnp.concatenate(other_terms, axis=1))
    layer_out, d_mid, d_context, terms = return_side(
        adapter_of, live, *attn, o_at, sums, mid, normed2, grad_out, context, rank_o,
        output_in, output_out, gain_two, gate_in, up_in, down_out,
    )

    first_half = slots // 2

    def slots_back(start, count, d_context, d_query=None):
        return attend_back(
            flags, queries, key_value, side, other_side, mate, d_context, mixed, logs, cosine, sine,
            kv_heads, start, count, d_query,
        )

    (early_came,) = hold([early_came], d_context)
    early = split_rows(add_up([early_keep, early_came]), shards)
    early_outs = wsh_outs(early, shard_place)
    late_keep, late_give = terms[0], terms[1]
    (d_context, late_give) = hold([d_context, late_give], *early_outs)
    early_moves = wsh_send(early_outs)
    late_came = swap_cores(late_give)
    back = [slots_back(0, first_half, d_context)]
    sides = [add_up([back[0][2], swap_cores(back[0][3])])]
    late_came, *early_moves = hold([late_came, *early_moves], back[0][1])
    late = split_rows(add_up([late_keep, late_came]), shards)
    late_outs = wsh_outs(late, shard_place)
    early = wsh_sum(early, shard_place, early_moves)
    early_outs = line_outs(early, place, line)
    (d_context,) = hold([d_context], sides[0], *late_outs, *early_outs)
    folded = [fold_blocks(sides[0], line)]
    late_moves = wsh_send(late_outs)
    early_moves = line_send(early_outs, line)
    back.append(slots_back(first_half, slots - first_half, d_context, back[0][0]))
    swapped = swap_cores(back[1][3])
    folded[0] = hold(folded[0], back[1][1]) if folded[0] else []
    sides.append(add_up([back[1][2], swapped]))
    total = add_up([sides[0]] + folded[0])
    (d_query,) = hold([back[1][0]], sides[1], total)
    folded.append(fold_blocks(sides[1], line))
    came = [return_blocks(sides[0], total, place, line)]
    d_normed_q, query_terms = query_back_side(
        adapter_of, *attn, d_query, normed, rank_q, query_in, query_out
    )
    folded[1] = hold(folded[1], query_terms) if folded[1] else []
    total = add_up([sides[1]] + folded[1])
    came.append(return_blocks(sides[1], total, place, line))
    late = wsh_sum(late, shard_place, hold(late_moves, query_terms, tip(total)))
    late_moves = line_send(line_outs(late, place, line), line)
    early_terms = line_sum(early, place, hold(early_moves, query_terms, tip(total)))
    came[0] = hold(came[0], query_terms)
    d_kv = jnp.concatenate(
        [b[1] + owned_blocks(p, c, place, line) for b, p, c in zip(back, sides, came)], axis=0
    )
    if mates:
        d_kv = d_kv + swap_cores(jnp.concatenate([b[4] for b in back], axis=0)).astype(f32)
    (early_terms,) = hold([early_terms], tip(d_kv))
    early_moves = line_moves(early_terms, line)
    (d_kv,) = hold([d_kv], early_terms)
    input_grad, kv_terms = output_side(
        adapter_of, live, *attn_kv, 0, d_kv, d_normed_q, d_mid, normed, rank_k, rank_v, tokens, gain_one,
        cosine, sine, kv_adapters,
    )

    width_rows = width // (2 * line)
    early_lined = in_order(early_terms, hold(early_moves, kv_terms), place, line)
    early_half = shard_gather(early_lined)
    late_terms = line_sum(late, place, hold(late_moves, kv_terms))
    last_keep = jnp.concatenate([query_terms[0], kv_terms[0]], axis=1)
    last_came = swap_cores(jnp.concatenate([query_terms[1], kv_terms[1]], axis=1))
    last = split_rows(add_up([last_keep, last_came]), shards)
    moves = wsh_send(wsh_outs(last, shard_place))
    last = wsh_sum(last, shard_place, moves)
    moves = line_send(line_outs(last, place, line), line)
    last_terms = line_sum(last, place, moves)
    last_terms = jnp.concatenate([late_terms, last_terms], axis=0)
    last_lined = in_order(last_terms, line_moves(last_terms, line), place, line)
    (early_half,) = hold([early_half], tip(last_lined))
    early_other = swap_cores(early_half)
    segments = [(3 * at + i * n, n, i, at) for at, n in spans for i in range(3)]
    g_gate_out, g_up_out, g_down_in = finish(
        core_place, early_half, early_other, (shard_hidden,) * 3, segments
    )
    last_own = gather_wsh(last_lined, shard_place, (tip(g_gate_out),))
    last_other = swap_cores(last_own)
    kv_rows = kv_width // (2 * line)
    segments = late_segments(late_terms.shape[0], last_terms.shape[0], 0, (width_rows,) * 5, 0)
    segments += late_segments(
        last_terms.shape[0] - late_terms.shape[0], last_terms.shape[0], late_terms.shape[0],
        (width_rows,) * 4 + (kv_rows,) * 2, 5,
    )
    (
        g_output_in, g_output_out, g_gate_in, g_up_in, g_down_out,
        g_query_in, g_query_out, g_key_in, g_value_in, g_key_out, g_value_out,
    ) = finish(
        core_place, last_own, last_other, (width_rows,) * 9 + (kv_rows,) * 2, segments
    )
    return (
        layer_out,
        input_grad,
        g_query_in,
        g_query_out,
        g_key_in,
        g_key_out,
        g_value_in,
        g_value_out,
        g_output_in,
        g_output_out,
        g_gate_in,
        g_gate_out,
        g_up_in,
        g_up_out,
        g_down_in,
        g_down_out,
    )


def solution(mesh):
    weight = P("wsh", "ctx")
    rows = P("wsh", "ctx", None)
    return jax.shard_map(
        local,
        mesh=mesh,
        in_specs=(rows, rows) + (P(),) * 4 + (weight,) * 7 + (P(),) * 17,
        out_specs=(rows, rows) + (P(),) * 14,
        check_vma=False,
    )
```
